32 devices in a mesh: groups: 2 (over y), adapter: 4 (over z), tensor: 4 (over x, core).
Axes of the slice: x: 2, y: 2, z: 4, core: 2. Of those that a mesh axis runs over, the one named last changes fastest.
Arguments:
- tokens: bfloat16 [128, 8192], P(('groups', 'adapter'), 'tensor'), parts along dimension 0, may hold values from -6 to 6
- base_up_weight: bfloat16 [8192, 28672], P('tensor', 'adapter'), may hold values from -0.0625 to 0.0625
- adapter_shrink_weight: bfloat16 [4, 8192, 64], P('adapter', 'tensor'), may hold values from -0.0625 to 0.0625
- adapter_expand_weight: bfloat16 [4, 64, 28672], P('adapter', 'tensor'), may hold values from -0.75 to 0.75
- row_adapter_index: int32 [128, 1], P('groups'), parts along dimension 0, may hold values from 0 to 3; in each aligned block of 64 rows (0 to 63, 64 to 127, ...) at most 32 rows name the same one
- adapter_slot_index: int32 [4], replicated, may hold values from 0 to 3, each once
Outputs:
- mixed: bfloat16 [128, 28672], P(('groups', 'tensor'), 'adapter'), parts along dimension 0
The draws below stay inside these ranges and needn't reach their ends.
There are 2 independent parts, one for each index of `groups`. The reference program is written for one: setup_inputs(seed, part) draws one part's arguments, and reference() takes and returns one part's arrays. A program takes and returns all parts, laid end to end along the dimension named above; an argument that names none is the same for every part. Nothing has to cross between parts.
Inputs may be any that keep to these rules, and one draw needn't show every extreme that they name: `row_adapter_index`: every adapter is named by at least one row and by at most 32 rows; some adapter by exactly 32. A permutation: adapter a's matrices are adapter_shrink_weight[adapter_slot_index[a]] and adapter_expand_weight[adapter_slot_index[a]].
All inputs are finite; a program needn't handle non-finite values.
Results may differ from the reference program's by a relative error of at most 0.0031.
Values may be sent and summed in bfloat16 or wider, within the bound.
No kernel may reach another device: no remote copies, remote signals or barrier semaphores. Data moves between devices by JAX's collectives and lax.ppermute only.
A program may use at most 128 MiB of HBM per device.

```python
import math
import jax
import jax.numpy as jnp
import numpy as np
from jax import lax

MODEL_WIDTH = 8192
HIDDEN_UNITS = 28672
ADAPTER_RANK = 64
ROWS = 64
ADAPTER_COUNT = 4
CAP = 32


def steps_of(rng, extent, shards, least, top_value):
    def one(axis_at, blocks):
        draws = jax.random.uniform(jax.random.fold_in(jax.random.fold_in(rng, 6), axis_at), (blocks,), jnp.float32, least / len(shards), top_value / len(shards))
        return jnp.repeat(jnp.exp(draws), extent[axis_at] // blocks).reshape((-1,) + (1,) * (len(extent) - axis_at - 1))

    loudness = one(*shards[0])
    for cut in shards[1:]:
        loudness = loudness * one(*cut)
    return loudness


def deal_out(stream_key, own, number, rows, number_of, top, limit, lean):
    order = jax.random.permutation(stream_key, number_of)
    heavy_load, common = portions_of(number_of, rows * top, limit, lean, True), portions_of(number_of, rows * top, limit, lean, False)
    places = jnp.arange(number_of)

    def named(tallies, offset_by):
        used = int((tallies > 0).sum())
        fixed = max(1, used // 4)
        shifted = fixed + (places - fixed + offset_by * (used - fixed)) % max(1, number_of - fixed)
        return jnp.zeros((number_of,), jnp.int32).at[order[jnp.where(places < fixed, places, shifted)]].set(jnp.asarray(tallies, jnp.int32))

    tallies = jnp.where(number % 4 == 0, named(heavy_load, number // 4), named(common, number - number // 4 - 1))
    mixed = jax.random.permutation(jax.random.fold_in(own, 3), number_of)
    giver, sink = mixed[0:number_of // 2 * 2:2], mixed[1:number_of // 2 * 2:2]
    margin = jnp.minimum(tallies[giver] - 1, limit - tallies[sink]) // 2
    margin = jnp.where((giver == order[0]) | (sink == order[0]) | (tallies[sink] == 0), 0, jnp.maximum(margin, 0))
    shifted = jax.random.randint(jax.random.fold_in(own, 4), (number_of // 2,), 0, 1 << 20) % (margin + 1)
    tallies = tallies.at[giver].add(-shifted).at[sink].add(shifted)
    labels = jnp.searchsorted(jnp.cumsum(tallies), jnp.arange(rows * top), side="right").astype(jnp.int32)
    listing = labels.reshape(top, rows).T
    listing = listing[jax.random.permutation(jax.random.fold_in(own, 1), rows)]
    offset_by = jax.random.randint(jax.random.fold_in(own, 2), (rows, 1), 0, top)
    return jnp.take_along_axis(listing, (jnp.arange(top)[None, :] + offset_by) % top, axis=1)


def portions_of(amount, total, bound, lean, full):
    portions = [(1 << 20) // math.isqrt(rank ** lean) + 1 for rank in range(1, amount + 1)]
    largest = bound if full else min(bound, max(-(-total // amount), total * portions[0] // sum(portions)))
    least = 1 if total - largest >= amount - 1 else 0
    counts, spare = [largest] + [least] * (amount - 1), total - largest - least * (amount - 1)
    while spare > 0:
        movable = [i for i in range(1, amount) if counts[i] < largest] or [i for i in range(1, amount) if counts[i] < bound]
        mass, left = sum([portions[i] for i in movable]), spare
        for i in movable:
            more = min(bound - counts[i], max(1, left * portions[i] // mass), spare)
            counts[i] = counts[i] + more
            spare = spare - more
    return np.array(counts)


def gaussian(key, dims, deviation, most, shards=(), kind=jnp.bfloat16):
    entries = deviation * jax.random.normal(key, dims, jnp.float32)
    if shards:
        entries = entries * steps_of(key, dims, shards, -0.22, 0.18)
    return jnp.clip(entries, -most, most).astype(kind)


def setup_inputs(seed: int = 0, part: int = 0) -> dict:
    keys = jax.random.split(jax.random.key(seed), 7)
    own_keys = jax.random.split(jax.random.fold_in(keys[6], part), 7)
    tokens = gaussian(own_keys[0], (ROWS, MODEL_WIDTH), 1.0, 6.0, ((0, 4), (1, 4)))
    base_up_weight = gaussian(keys[1], (MODEL_WIDTH, HIDDEN_UNITS), MODEL_WIDTH ** -0.5, 0.0625, ((0, 4), (1, 4)))
    adapter_shrink_weight = gaussian(keys[2], (ADAPTER_COUNT, MODEL_WIDTH, ADAPTER_RANK), MODEL_WIDTH ** -0.5, 0.0625, ((0, 4), (1, 4)))
    adapter_expand_weight = gaussian(keys[3], (ADAPTER_COUNT, ADAPTER_RANK, HIDDEN_UNITS), ADAPTER_RANK ** -0.5, 0.75, ((0, 4), (1, 4)))
    row_adapter_index_keys = jax.random.split(jax.random.fold_in(own_keys[4], 1), ROWS // ROWS)
    row_adapter_index_turns = jax.random.permutation(jax.random.fold_in(own_keys[4], 3), ROWS // ROWS)
    row_adapter_index = jax.vmap(lambda own, number: deal_out(jax.random.fold_in(own_keys[4], 2), own, number, ROWS, ADAPTER_COUNT, 1, CAP, 2))(row_adapter_index_keys, row_adapter_index_turns).reshape((ROWS, 1))
    adapter_slot_index = jax.random.permutation(keys[5], ADAPTER_COUNT).astype(jnp.int32)
    return dict(tokens=tokens, base_up_weight=base_up_weight, adapter_shrink_weight=adapter_shrink_weight, adapter_expand_weight=adapter_expand_weight, row_adapter_index=row_adapter_index, adapter_slot_index=adapter_slot_index)


adapter_scale = 0.5


def reference(tokens, base_up_weight, adapter_shrink_weight, adapter_expand_weight, row_adapter_index, adapter_slot_index):
    slot_of_row = jnp.take(adapter_slot_index, row_adapter_index[:, 0], axis=0).astype(jnp.int32)
    base_part = jnp.dot(tokens, base_up_weight, preferred_element_type=jnp.float32)
    block_rows = math.gcd(ROWS, 16)
    block_count = ROWS // block_rows

    def one_block(index):
        begin = (index * block_rows).astype(jnp.int32)
        token_block = lax.dynamic_slice_in_dim(tokens, begin, block_rows, 0).astype(jnp.float32)
        adapter_slot_block = lax.dynamic_slice_in_dim(slot_of_row, begin, block_rows, 0)
        shrink_weight_block = jnp.take(adapter_shrink_weight, adapter_slot_block, axis=0).astype(jnp.float32)
        shrunk_rows = jnp.einsum("rd,rdk->rk", token_block, shrink_weight_block, precision=lax.Precision.HIGHEST)
        shrunk_rows = (adapter_scale * shrunk_rows).astype(jnp.bfloat16)
        expand_weight_block = jnp.take(adapter_expand_weight, adapter_slot_block, axis=0).astype(jnp.float32)
        return jnp.einsum("rk,rkf->rf", shrunk_rows.astype(jnp.float32), expand_weight_block, precision=lax.Precision.HIGHEST)

    delta = lax.map(one_block, jnp.arange(block_count, dtype=jnp.int32)).reshape(ROWS, HIDDEN_UNITS)
    return (base_part + delta).astype(jnp.bfloat16)
```

```python
import functools

import jax
import jax.numpy as jnp
from jax import lax
from jax.experimental import pallas as pl
from jax.experimental.pallas import tpu as pltpu
from jax.sharding import PartitionSpec as P

adapter_scale = 0.5
lane = 128
f32 = jnp.float32
bf16 = jnp.bfloat16


def general(
    tokens,
    base_up_weight,
    adapter_shrink_weight,
    adapter_expand_weight,
    row_adapter_index,
    adapter_slot_index,
):
    owner_count = lax.axis_size("adapter")
    owner_index = lax.axis_index("adapter")
    tensor_index = lax.axis_index("tensor")
    rank_block = adapter_expand_weight.shape[1]
    columns = base_up_weight.shape[1]
    slot = jnp.take(adapter_slot_index, row_adapter_index[:, 0], axis=0)
    rows = lax.all_gather(tokens, "adapter", axis=0, tiled=True)
    expand = adapter_expand_weight[0].reshape(rank_block, owner_count, columns)
    expand = lax.all_to_all(expand, "adapter", split_axis=1, concat_axis=1, tiled=True)
    shrunk = jnp.dot(rows, adapter_shrink_weight[0], preferred_element_type=f32)
    shrunk = jnp.where((slot == owner_index)[:, None], shrunk, 0.0)
    shrunk = lax.psum(shrunk, ("adapter", "tensor"))
    shrunk = (adapter_scale * shrunk).astype(bf16)
    shrunk = lax.dynamic_slice_in_dim(shrunk, tensor_index * rank_block, rank_block, 1)
    chosen = slot[:, None] == jnp.arange(owner_count, dtype=jnp.int32)[None, :]
    spread = jnp.where(chosen[:, None, :], shrunk[:, :, None], jnp.zeros((), bf16))
    total = jnp.dot(rows, base_up_weight, preferred_element_type=f32)
    total = total + jnp.dot(
        spread.reshape(-1, rank_block * owner_count),
        expand.reshape(rank_block * owner_count, columns),
        preferred_element_type=f32,
    )
    return lax.psum_scatter(total, "tensor", scatter_dimension=0, tiled=True).astype(bf16)


def gather_kernel(place, slots, index, *refs):
    owner_count = len(refs) - 1 - 1 - 4
    blocks = refs[:owner_count]
    shrink = refs[owner_count]
    rows_out = refs[owner_count + 1]
    parts_out = refs[owner_count + 2 :]
    a, t = place[0], place[1]
    height = blocks[0].shape[0]
    for j in range(owner_count):
        where = lax.rem(a + j, owner_count)
        rows_out[pl.ds(pl.multiple_of(where * height, height), height), :] = blocks[j][...]
    product = lax.dot_general(
        shrink[...], rows_out[...], (((1,), (1,)), ((), ())), preferred_element_type=f32
    )
    named = index[...]
    slot = jnp.zeros_like(named)
    for k in range(slots.shape[0]):
        slot = jnp.where(named == k, slots[k], slot)
    product = jnp.where(slot == a, product, 0.0)
    rank_block = parts_out[0].shape[0]
    for m in range(4):
        for block in range(4):
            @pl.when(lax.bitwise_xor(t, m) == block)
            def _():
                parts_out[m][...] = product[block * rank_block : (block + 1) * rank_block, :]


def base_kernel(place, rows, weight, total, ordered):
    t = place[1]
    height = rows.shape[0] // 4

    @pl.when(pl.program_id(0) == 0)
    def _():
        for i, flip in enumerate((0, 2, 1, 3)):
            start = pl.multiple_of(lax.bitwise_xor(t, flip) * height, height)
            ordered[i * height : (i + 1) * height, :] = rows[pl.ds(start, height), :]

    total[...] = jnp.dot(ordered[...], weight[...], preferred_element_type=f32)


def delta_kernel(place, base, own, *refs):
    owner_count = (len(refs) - 4 + 1) // 2
    others = refs[: owner_count - 1]
    shrunk = refs[owner_count - 1 : 2 * owner_count - 1]
    keep, send, flat, ordered = refs[2 * owner_count - 1 :]
    t = place[1]
    row_count = base.shape[0]
    height = row_count // 4

    @pl.when(pl.program_id(0) == 0)
    def _():
        stacked = jnp.concatenate([part[...].astype(f32) for part in shrunk], axis=0)
        flat[...] = stacked.T
        for i, flip in enumerate((0, 2, 1, 3)):
            start = pl.multiple_of(lax.bitwise_xor(t, flip) * height, height)
            ordered[i * height : (i + 1) * height, :] = flat[pl.ds(start, height), :].astype(bf16)

    expand = jnp.concatenate([own[0]] + [part[...] for part in others], axis=0)
    total = base[...] + jnp.dot(ordered[...], expand, preferred_element_type=f32)
    keep[...] = total[: row_count // 2]
    send[...] = total[row_count // 2 :]


def column_block(width):
    for size in (512, 256, 128):
        if width % size == 0:
            return size


def base_half(place, rows, weight, half_width, flip):
    row_count, depth = rows.shape
    block = column_block(half_width)
    steps = half_width // block

    def weight_map(i, place):
        return (0, lax.bitwise_xor(place[2], flip) * steps + i)

    return pl.pallas_call(
        base_kernel,
        grid_spec=pltpu.PrefetchScalarGridSpec(
            num_scalar_prefetch=1,
            grid=(steps,),
            in_specs=[
                pl.BlockSpec((row_count, depth), lambda i, place: (0, 0)),
                pl.BlockSpec((depth, block), weight_map),
            ],
            out_specs=pl.BlockSpec((row_count, block), lambda i, place: (0, i)),
            scratch_shapes=[pltpu.VMEM((row_count, depth), bf16)],
        ),
        out_shape=jax.ShapeDtypeStruct((row_count, half_width), f32),
        cost_estimate=pl.CostEstimate(
            flops=2 * row_count * depth * half_width,
            bytes_accessed=2 * depth * half_width,
            transcendentals=0,
        ),
        compiler_params=pltpu.CompilerParams(vmem_limit_bytes=24 << 20),
        name="base_half",
    )(place, rows, weight)


def delta_half(place, base, own, others, shrunk, flip):
    row_count, half_width = base.shape
    rank_block = own.shape[1]
    owner_count = len(shrunk)
    block = column_block(half_width)
    steps = half_width // block

    def own_map(i, place):
        return (0, 0, (2 * place[0] + lax.bitwise_xor(place[2], flip)) * steps + i)

    return pl.pallas_call(
        delta_kernel,
        grid_spec=pltpu.PrefetchScalarGridSpec(
            num_scalar_prefetch=1,
            grid=(steps,),
            in_specs=[
                pl.BlockSpec((row_count, block), lambda i, place: (0, i)),
                pl.BlockSpec((1, rank_block, block), own_map),
            ]
            + [pl.BlockSpec((rank_block, block), lambda i, place: (0, i))] * (owner_count - 1)
            + [pl.BlockSpec((rank_block, row_count), lambda i, place: (0, 0))] * owner_count,
            out_specs=[pl.BlockSpec((row_count // 2, block), lambda i, place: (0, i))] * 2,
            scratch_shapes=[
                pltpu.VMEM((row_count, rank_block * owner_count), f32),
                pltpu.VMEM((row_count, rank_block * owner_count), bf16),
            ],
        ),
        out_shape=[jax.ShapeDtypeStruct((row_count // 2, half_width), f32)] * 2,
        cost_estimate=pl.CostEstimate(
            flops=2 * row_count * rank_block * owner_count * half_width,
            bytes_accessed=12 * row_count * half_width,
            transcendentals=0,
        ),
        compiler_params=pltpu.CompilerParams(vmem_limit_bytes=24 << 20),
        name="delta_half",
    )(place, base, own, *others, *shrunk)


def paired(
    tokens,
    base_up_weight,
    adapter_shrink_weight,
    adapter_expand_weight,
    row_adapter_index,
    adapter_slot_index,
):
    owner_count = lax.axis_size("adapter")
    g = lax.axis_index("groups")
    a = lax.axis_index("adapter")
    t = lax.axis_index("tensor")
    place = jnp.stack([a, t, g]).astype(jnp.int32)
    height, depth = tokens.shape
    row_count = height * owner_count
    columns = base_up_weight.shape[1]
    half_width = columns // 2
    rank_block = adapter_expand_weight.shape[1]
    rank = adapter_shrink_weight.shape[2]

    def from_owner(x, j):
        return lax.ppermute(x, "adapter", [(s, (s - j) % owner_count) for s in range(owner_count)])

    def from_tensor(x, m):
        return lax.ppermute(x, "tensor", [(s, s ^ m) for s in range(4)])

    def from_group(x):
        return lax.ppermute(x, "groups", [(0, 1), (1, 0)])

    others = range(1, owner_count)
    blocks = [tokens] + [from_owner(tokens, j) for j in others]

    expand_near = []
    for j in others:
        to = lax.rem(a - j + owner_count, owner_count)
        piece = lax.dynamic_slice(
            adapter_expand_weight[0],
            (0, to * columns + g * half_width),
            (rank_block, half_width),
        )
        expand_near.append(from_owner(piece, j))
    expand_far = [from_group(x) for x in expand_near]

    full = pl.BlockSpec(memory_space=pltpu.VMEM)
    small = pl.BlockSpec(memory_space=pltpu.SMEM)
    gathered = pl.pallas_call(
        gather_kernel,
        in_specs=[small, small] + [full] * (owner_count + 2),
        out_specs=[full] * 5,
        out_shape=[jax.ShapeDtypeStruct((row_count, depth), bf16)]
        + [jax.ShapeDtypeStruct((rank_block, row_count), f32)] * 4,
        cost_estimate=pl.CostEstimate(
            flops=2 * row_count * depth * rank,
            bytes_accessed=4 * row_count * depth + 2 * depth * rank,
            transcendentals=0,
        ),
        name="gather_rows",
    )(
        place,
        adapter_slot_index,
        row_adapter_index.reshape(1, row_count),
        *blocks,
        adapter_shrink_weight[0].T,
    )
    rows, shrink_parts = gathered[0], gathered[1:]
    shrunk = shrink_parts[0]
    for m in (1, 2, 3):
        shrunk = shrunk + from_tensor(shrink_parts[m], m)
    shrunk = (adapter_scale * shrunk).astype(bf16)
    shrunk = [shrunk] + [from_owner(shrunk, j) for j in others]

    halves = []
    for flip, expand in ((0, expand_near), (1, expand_far)):
        base = base_half(place, rows, base_up_weight, half_width, flip)
        keep, send = delta_half(place, base, adapter_expand_weight, expand, shrunk, flip)
        both = keep + from_tensor(send, 1)
        middle = row_count // 4
        crossed = from_tensor(both[middle:].astype(bf16), 2)
        halves.append((both[:middle] + crossed.astype(f32)).astype(bf16))
    first = jnp.where(g == 0, halves[0], halves[1])
    second = jnp.where(g == 0, halves[1], halves[0])
    return jnp.concatenate([first, second], axis=1)


def on_device(tokens, base_up_weight, adapter_shrink_weight, adapter_expand_weight, *index):
    pairs = lax.axis_size("groups") == 2 and lax.axis_size("tensor") == 4
    few = lax.axis_size("adapter") <= 8
    even = base_up_weight.shape[1] % (2 * lane) == 0 and tokens.shape[0] % 16 == 0
    arrange = paired if pairs and few and even else general
    return arrange(
        tokens, base_up_weight, adapter_shrink_weight, adapter_expand_weight, *index
    )


def solution(mesh):
    placed = (
        P(("groups", "adapter"), "tensor"),
        P("tensor", "adapter"),
        P("adapter", "tensor", None),
        P("adapter", "tensor", None),
        P("groups", None),
        P(),
    )
    return jax.shard_map(
        on_device,
        mesh=mesh,
        in_specs=placed,
        out_specs=P(("groups", "tensor"), "adapter"),
        check_vma=False,
    )
```

```python
import functools

import jax
import jax.numpy as jnp
from jax import lax
from jax.experimental import pallas as pl
from jax.experimental.pallas import tpu as pltpu
from jax.sharding import PartitionSpec as P

adapter_scale = 0.5
lane = 128
f32 = jnp.float32
bf16 = jnp.bfloat16


def general(
    tokens,
    base_up_weight,
    adapter_shrink_weight,
    adapter_expand_weight,
    row_adapter_index,
    adapter_slot_index,
):
    owner_count = lax.axis_size("adapter")
    owner_index = lax.axis_index("adapter")
    tensor_index = lax.axis_index("tensor")
    rank_block = adapter_expand_weight.shape[1]
    columns = base_up_weight.shape[1]
    slot = jnp.take(adapter_slot_index, row_adapter_index[:, 0], axis=0)
    rows = lax.all_gather(tokens, "adapter", axis=0, tiled=True)
    expand = adapter_expand_weight[0].reshape(rank_block, owner_count, columns)
    expand = lax.all_to_all(expand, "adapter", split_axis=1, concat_axis=1, tiled=True)
    shrunk = jnp.dot(rows, adapter_shrink_weight[0], preferred_element_type=f32)
    shrunk = jnp.where((slot == owner_index)[:, None], shrunk, 0.0)
    shrunk = lax.psum(shrunk, ("adapter", "tensor"))
    shrunk = (adapter_scale * shrunk).astype(bf16)
    shrunk = lax.dynamic_slice_in_dim(shrunk, tensor_index * rank_block, rank_block, 1)
    chosen = slot[:, None] == jnp.arange(owner_count, dtype=jnp.int32)[None, :]
    spread = jnp.where(chosen[:, None, :], shrunk[:, :, None], jnp.zeros((), bf16))
    total = jnp.dot(rows, base_up_weight, preferred_element_type=f32)
    total = total + jnp.dot(
        spread.reshape(-1, rank_block * owner_count),
        expand.reshape(rank_block * owner_count, columns),
        preferred_element_type=f32,
    )
    return lax.psum_scatter(total, "tensor", scatter_dimension=0, tiled=True).astype(bf16)


vmem = pl.BlockSpec(memory_space=pltpu.VMEM)
smem = pl.BlockSpec(memory_space=pltpu.SMEM)
anywhere = pl.BlockSpec(memory_space=pl.ANY)


def kernel_call(kernel, name, flops, moved, mib, **specs):
    return pl.pallas_call(
        kernel,
        cost_estimate=pl.CostEstimate(flops=flops, bytes_accessed=moved, transcendentals=0),
        compiler_params=pltpu.CompilerParams(vmem_limit_bytes=mib << 20),
        name=name,
        **specs,
    )


def cut_kernel(owner_count, half_width, expand, *refs):
    pieces, sem = refs[:-1], refs[-1]
    g, a = lax.axis_index("groups"), lax.axis_index("adapter")
    copies = []
    for n, piece in enumerate(pieces):
        to = lax.rem(a - (n + 1) + owner_count, owner_count)
        start = pl.multiple_of((2 * to + g) * half_width, half_width)
        copies.append(
            pltpu.make_async_copy(expand.at[0, :, pl.ds(start, half_width)], piece, sem.at[n])
        )
    for copy in copies:
        copy.start()
    for copy in copies:
        copy.wait()


def load_kernel(parts, weight, expand, after, held, own, sem):
    a = lax.axis_index("adapter")
    depth, columns = held.shape
    step = depth // parts
    copies = []
    for n in range(parts):
        span = pl.ds(n * step, step)
        copies.append(pltpu.make_async_copy(weight.at[span], held.at[span], sem.at[n]))
    start = pl.multiple_of(a * columns, columns)
    copies.append(
        pltpu.make_async_copy(expand.at[0, :, pl.ds(start, columns)], own, sem.at[parts])
    )
    for copy in copies:
        copy.start()
    for copy in copies:
        copy.wait()


def gather_kernel(owner_count, slots, index, *refs):
    blocks = refs[:owner_count]
    shrink, after, rows_out = refs[owner_count : owner_count + 3]
    parts_out = refs[owner_count + 3 : owner_count + 7]
    rows = refs[owner_count + 7]
    a, t = lax.axis_index("adapter"), lax.axis_index("tensor")
    height = blocks[0].shape[0]
    for j in range(owner_count):
        where = lax.rem(a + j, owner_count)
        rows[pl.ds(pl.multiple_of(where * height, height), height), :] = blocks[j][...]
    quarter = rows.shape[0] // 4
    for i, flip in enumerate((0, 2, 1, 3)):
        start = pl.multiple_of(lax.bitwise_xor(t, flip) * quarter, quarter)
        rows_out[i * quarter : (i + 1) * quarter, :] = rows[pl.ds(start, quarter), :]
    product = lax.dot_general(
        shrink[...], rows[...], (((1,), (1,)), ((), ())), preferred_element_type=f32
    )
    named = index[...]
    slot = jnp.zeros_like(named)
    for k in range(slots.shape[0]):
        slot = jnp.where(named == k, slots[k], slot)
    product = jnp.where(slot == a, product, 0.0)
    rank_block = parts_out[0].shape[0]
    for m in range(4):
        for block in range(4):
            @pl.when(lax.bitwise_xor(t, m) == block)
            def _():
                parts_out[m][...] = product[block * rank_block : (block + 1) * rank_block, :]


def base_kernel(flip, block, rows, weight, after, total):
    half = lax.bitwise_xor(lax.axis_index("groups"), flip)
    half_width = total.shape[1]

    @pl.loop(0, half_width // block)
    def _(i):
        column = pl.multiple_of(i * block, block)
        source = pl.multiple_of(half * half_width + column, block)
        total[:, pl.ds(column, block)] = jnp.dot(
            rows[...], weight[:, pl.ds(source, block)], preferred_element_type=f32
        )


def delta_kernel(flip, block, base, own, *refs):
    keep, send, flat, ordered = refs[-4:]
    owner_count = (len(refs) - 4 + 1) // 2
    others = refs[: owner_count - 1]
    shrunk = refs[owner_count - 1 : 2 * owner_count - 1]
    t = lax.axis_index("tensor")
    half = lax.bitwise_xor(lax.axis_index("groups"), flip)
    row_count, half_width = base.shape
    quarter = row_count // 4
    stacked = jnp.concatenate([part[...].astype(f32) for part in shrunk], axis=0)
    flat[...] = stacked.T
    for i, turn in enumerate((0, 2, 1, 3)):
        start = pl.multiple_of(lax.bitwise_xor(t, turn) * quarter, quarter)
        ordered[i * quarter : (i + 1) * quarter, :] = flat[pl.ds(start, quarter), :].astype(bf16)
    left = ordered[...]
    for column in range(0, half_width, block):
        span = pl.ds(column, block)
        source = pl.multiple_of(half * half_width + column, block)
        expand = jnp.concatenate(
            [own[:, pl.ds(source, block)]] + [part[:, span] for part in others], axis=0
        )
        total = base[:, span] + jnp.dot(left, expand, preferred_element_type=f32)
        keep[:, span] = total[: row_count // 2]
        send[:, span] = total[row_count // 2 :]


def column_block(width):
    for size in (512, 256, 128):
        if width % size == 0:
            return size


def paired(
    tokens,
    base_up_weight,
    adapter_shrink_weight,
    adapter_expand_weight,
    row_adapter_index,
    adapter_slot_index,
):
    owner_count = lax.axis_size("adapter")
    g = lax.axis_index("groups")
    height, depth = tokens.shape
    row_count = height * owner_count
    columns = base_up_weight.shape[1]
    half_width = columns // 2
    rank_block = adapter_expand_weight.shape[1]
    rank = adapter_shrink_weight.shape[2]
    block = column_block(half_width)

    def from_owner(x, j):
        return lax.ppermute(x, "adapter", [(s, (s - j) % owner_count) for s in range(owner_count)])

    def from_tensor(x, m):
        return lax.ppermute(x, "tensor", [(s, s ^ m) for s in range(4)])

    def from_group(x):
        return lax.ppermute(x, "groups", [(0, 1), (1, 0)])

    weight = pltpu.with_memory_space_constraint(base_up_weight, pltpu.HBM)
    expand = pltpu.with_memory_space_constraint(adapter_expand_weight, pltpu.HBM)
    others = range(1, owner_count)
    blocks = [tokens] + [from_owner(tokens, j) for j in others]

    pieces = kernel_call(
        functools.partial(cut_kernel, owner_count, half_width),
        "cut_expand",
        1,
        1,
        1,
        in_specs=[anywhere],
        out_specs=[vmem] * (owner_count - 1),
        out_shape=[pltpu.VMEM((rank_block, half_width), bf16)] * (owner_count - 1),
        scratch_shapes=[pltpu.SemaphoreType.DMA((owner_count - 1,))],
    )(expand)
    near = [from_owner(piece, j) for piece, j in zip(pieces, others)]

    parts = 8
    held, own = kernel_call(
        functools.partial(load_kernel, parts),
        "load_weights",
        1,
        1,
        1,
        in_specs=[anywhere] * 3,
        out_specs=[vmem] * 2,
        out_shape=[pltpu.VMEM((depth, columns), bf16), pltpu.VMEM((rank_block, columns), bf16)],
        scratch_shapes=[pltpu.SemaphoreType.DMA((parts + 1,))],
    )(weight, expand, pieces[0])

    gathered = kernel_call(
        functools.partial(gather_kernel, owner_count),
        "gather_rows",
        2 * row_count * depth * rank,
        4 * row_count * depth + 2 * depth * rank,
        4,
        in_specs=[smem, vmem] + [vmem] * (owner_count + 1) + [anywhere],
        out_specs=[vmem] * 5,
        out_shape=[jax.ShapeDtypeStruct((row_count, depth), bf16)]
        + [jax.ShapeDtypeStruct((rank_block, row_count), f32)] * 4,
        scratch_shapes=[pltpu.VMEM((row_count, depth), bf16)],
    )(
        adapter_slot_index,
        row_adapter_index.reshape(1, row_count),
        *blocks,
        adapter_shrink_weight[0].T,
        own,
    )
    rows, shrink_parts = gathered[0], gathered[1:]

    def base_half(flip, after):
        return kernel_call(
            functools.partial(base_kernel, flip, block),
            "base_half",
            2 * row_count * depth * half_width,
            2 * depth * half_width,
            4,
            in_specs=[vmem, vmem, anywhere],
            out_specs=vmem,
            out_shape=jax.ShapeDtypeStruct((row_count, half_width), f32),
        )(rows, held, after)

    def delta_half(flip, base, expand, shrunk):
        return kernel_call(
            functools.partial(delta_kernel, flip, block),
            "delta_half",
            2 * row_count * rank_block * owner_count * half_width,
            12 * row_count * half_width,
            8,
            in_specs=[vmem] * (2 + 2 * owner_count - 1),
            out_specs=[vmem] * 2,
            out_shape=[jax.ShapeDtypeStruct((row_count // 2, half_width), f32)] * 2,
            scratch_shapes=[
                pltpu.VMEM((row_count, rank_block * owner_count), f32),
                pltpu.VMEM((row_count, rank_block * owner_count), bf16),
            ],
        )(base, own, *expand, *shrunk)

    base_first = base_half(0, shrink_parts[0])
    received = [from_tensor(shrink_parts[m], m) for m in (1, 2, 3)]
    *received, base_first = lax.optimization_barrier((*received, base_first))
    shrunk = shrink_parts[0] + received[0] + received[1] + received[2]
    shrunk = (adapter_scale * shrunk).astype(bf16)
    base_second = base_half(1, shrunk)
    shrunk = [shrunk] + [from_owner(shrunk, j) for j in others]
    *near, base_second = lax.optimization_barrier((*near, base_second))
    far = [from_group(x) for x in near]

    halves = []
    for flip, base, pieces in ((0, base_first, near), (1, base_second, far)):
        keep, send = delta_half(flip, base, pieces, shrunk)
        both = keep + from_tensor(send, 1)
        middle = row_count // 4
        crossed = from_tensor(both[middle:].astype(bf16), 2)
        halves.append((both[:middle] + crossed.astype(f32)).astype(bf16))
    first = jnp.where(g == 0, halves[0], halves[1])
    second = jnp.where(g == 0, halves[1], halves[0])
    return jnp.concatenate([first, second], axis=1)


def on_device(tokens, base_up_weight, adapter_shrink_weight, adapter_expand_weight, *index):
    pairs = lax.axis_size("groups") == 2 and lax.axis_size("tensor") == 4
    few = lax.axis_size("adapter") <= 8
    even = base_up_weight.shape[1] % (2 * lane) == 0 and tokens.shape[0] % 16 == 0
    arrange = paired if pairs and few and even else general
    return arrange(
        tokens, base_up_weight, adapter_shrink_weight, adapter_expand_weight, *index
    )


def solution(mesh):
    placed = (
        P(("groups", "adapter"), "tensor"),
        P("tensor", "adapter"),
        P("adapter", "tensor", None),
        P("adapter", "tensor", None),
        P("groups", None),
        P(),
    )
    return jax.shard_map(
        on_device,
        mesh=mesh,
        in_specs=placed,
        out_specs=P(("groups", "tensor"), "adapter"),
        check_vma=False,
    )
```

```python
import functools

import jax
import jax.numpy as jnp
from jax import lax
from jax.experimental import pallas as pl
from jax.experimental.pallas import tpu as pltpu
from jax.sharding import PartitionSpec as P

adapter_scale = 0.5
lane = 128
f32 = jnp.float32
bf16 = jnp.bfloat16


def general(
    tokens,
    base_up_weight,
    adapter_shrink_weight,
    adapter_expand_weight,
    row_adapter_index,
    adapter_slot_index,
):
    owner_count = lax.axis_size("adapter")
    owner_index = lax.axis_index("adapter")
    tensor_index = lax.axis_index("tensor")
    rank_block = adapter_expand_weight.shape[1]
    columns = base_up_weight.shape[1]
    slot = jnp.take(adapter_slot_index, row_adapter_index[:, 0], axis=0)
    rows = lax.all_gather(tokens, "adapter", axis=0, tiled=True)
    expand = adapter_expand_weight[0].reshape(rank_block, owner_count, columns)
    expand = lax.all_to_all(expand, "adapter", split_axis=1, concat_axis=1, tiled=True)
    shrunk = jnp.dot(rows, adapter_shrink_weight[0], preferred_element_type=f32)
    shrunk = jnp.where((slot == owner_index)[:, None], shrunk, 0.0)
    shrunk = lax.psum(shrunk, ("adapter", "tensor"))
    shrunk = (adapter_scale * shrunk).astype(bf16)
    shrunk = lax.dynamic_slice_in_dim(shrunk, tensor_index * rank_block, rank_block, 1)
    chosen = slot[:, None] == jnp.arange(owner_count, dtype=jnp.int32)[None, :]
    spread = jnp.where(chosen[:, None, :], shrunk[:, :, None], jnp.zeros((), bf16))
    total = jnp.dot(rows, base_up_weight, preferred_element_type=f32)
    total = total + jnp.dot(
        spread.reshape(-1, rank_block * owner_count),
        expand.reshape(rank_block * owner_count, columns),
        preferred_element_type=f32,
    )
    return lax.psum_scatter(total, "tensor", scatter_dimension=0, tiled=True).astype(bf16)


vmem = pl.BlockSpec(memory_space=pltpu.VMEM)
smem = pl.BlockSpec(memory_space=pltpu.SMEM)
anywhere = pl.BlockSpec(memory_space=pl.ANY)


def kernel_call(kernel, name, flops, moved, mib, **specs):
    return pl.pallas_call(
        kernel,
        cost_estimate=pl.CostEstimate(flops=flops, bytes_accessed=moved, transcendentals=0),
        compiler_params=pltpu.CompilerParams(vmem_limit_bytes=mib << 20),
        name=name,
        **specs,
    )


def cut_kernel(expand, *refs):
    chunks, sem = refs[:-1], refs[-1]
    g = lax.axis_index("groups")
    owner_count, _, width = chunks[0].shape
    copies = []
    for n, chunk in enumerate(chunks):
        for to in range(owner_count):
            start = pl.multiple_of(((2 * to + g) * len(chunks) + n) * width, width)
            copies.append(
                pltpu.make_async_copy(
                    expand.at[0, :, pl.ds(start, width)], chunk.at[to], sem.at[n, to]
                )
            )
    for copy in copies:
        copy.start()
    for copy in copies:
        copy.wait()


def gather_kernel(owner_count, slots, index, *refs):
    blocks = refs[:owner_count]
    shrink, after, rows_out = refs[owner_count : owner_count + 3]
    parts_out = refs[owner_count + 3 : owner_count + 7]
    rows = refs[owner_count + 7]
    a, t = lax.axis_index("adapter"), lax.axis_index("tensor")
    height = blocks[0].shape[0]
    for j in range(owner_count):
        where = lax.rem(a + j, owner_count)
        rows[pl.ds(pl.multiple_of(where * height, height), height), :] = blocks[j][...]
    quarter = rows.shape[0] // 4
    for i, flip in enumerate((0, 2, 1, 3)):
        start = pl.multiple_of(lax.bitwise_xor(t, flip) * quarter, quarter)
        rows_out[i * quarter : (i + 1) * quarter, :] = rows[pl.ds(start, quarter), :]
    product = lax.dot_general(
        shrink[...], rows[...], (((1,), (1,)), ((), ())), preferred_element_type=f32
    )
    named = index[...]
    slot = jnp.zeros_like(named)
    for k in range(slots.shape[0]):
        slot = jnp.where(named == k, slots[k], slot)
    product = jnp.where(slot == a, product, 0.0)
    rank_block = parts_out[0].shape[0]
    for m in range(4):
        for block in range(4):
            @pl.when(lax.bitwise_xor(t, m) == block)
            def _():
                parts_out[m][...] = product[block * rank_block : (block + 1) * rank_block, :]


def weight_copies(flip, block, weight, first, count, target, sem):
    half = lax.bitwise_xor(lax.axis_index("groups"), flip)
    half_width = weight.shape[1] // 2
    copies = []
    for n in range(count):
        start = pl.multiple_of(half * half_width + (first + n) * block, block)
        copies.append(
            pltpu.make_async_copy(weight.at[:, pl.ds(start, block)], target.at[n], sem.at[n])
        )
    return copies


def load_kernel(block, counts, weight, after, held, sem):
    copies, at = [], 0
    for flip, count in enumerate(counts):
        if count == 0:
            continue
        span = pl.ds(at, count)
        copies += weight_copies(flip, block, weight, 0, count, held.at[span], sem.at[span])
        at += count
    for copy in copies:
        copy.start()
    for copy in copies:
        copy.wait()


def base_kernel(flip, block, first, held_count, rows, weight, *refs):
    *held, _, total, streamed, sem = refs
    stream_count = streamed.shape[0]
    copies = weight_copies(flip, block, weight, held_count, stream_count, streamed, sem)
    for copy in copies:
        copy.start()
    for n in range(held_count):
        total[:, n * block : (n + 1) * block] = jnp.dot(
            rows[...], held[0][first + n], preferred_element_type=f32
        )
    for n in range(stream_count):
        copies[n].wait()
        at = (held_count + n) * block
        total[:, at : at + block] = jnp.dot(
            rows[...], streamed[n], preferred_element_type=f32
        )


def delta_kernel(owner_count, block, base, *refs):
    shrunk, chunks = refs[:owner_count], refs[owner_count:-5]
    keep, send, flat, ordered = refs[-4:]
    a, t = lax.axis_index("adapter"), lax.axis_index("tensor")
    row_count = base.shape[0]
    quarter = row_count // 4
    rank_block = shrunk[0].shape[0]
    for j in range(owner_count):
        start = pl.multiple_of(lax.rem(a + j, owner_count) * rank_block, rank_block)
        flat[pl.ds(start, rank_block), :] = shrunk[j][...].astype(f32)
    turned = flat[...].T
    flat[...] = turned
    for i, turn in enumerate((0, 2, 1, 3)):
        start = pl.multiple_of(lax.bitwise_xor(t, turn) * quarter, quarter)
        ordered[i * quarter : (i + 1) * quarter, :] = flat[pl.ds(start, quarter), :].astype(bf16)
    left = ordered[...]
    at = 0
    for chunk in chunks:
        for column in range(0, chunk.shape[1], block):
            total = base[:, at : at + block] + jnp.dot(
                left, chunk[:, column : column + block], preferred_element_type=f32
            )
            keep[:, at : at + block] = total[: row_count // 2]
            send[:, at : at + block] = total[row_count // 2 :]
            at += block


def column_block(width):
    for size in (512, 256, 128):
        if width % size == 0:
            return size


def paired(
    tokens,
    base_up_weight,
    adapter_shrink_weight,
    adapter_expand_weight,
    row_adapter_index,
    adapter_slot_index,
):
    owner_count = lax.axis_size("adapter")
    g = lax.axis_index("groups")
    height, depth = tokens.shape
    row_count = height * owner_count
    columns = base_up_weight.shape[1]
    half_width = columns // 2
    rank_block = adapter_expand_weight.shape[1]
    rank = adapter_shrink_weight.shape[2]
    block = column_block(half_width)

    def from_owner(x, j):
        return lax.ppermute(x, "adapter", [(s, (s - j) % owner_count) for s in range(owner_count)])

    def from_tensor(x, m):
        return lax.ppermute(x, "tensor", [(s, s ^ m) for s in range(4)])

    def from_group(x):
        return lax.ppermute(x, "groups", [(0, 1), (1, 0)])

    weight = pltpu.with_memory_space_constraint(base_up_weight, pltpu.HBM)
    expand = pltpu.with_memory_space_constraint(adapter_expand_weight, pltpu.HBM)
    others = range(1, owner_count)
    blocks = [tokens] + [from_owner(tokens, j) for j in others]

    chunk_count = 1
    width = half_width // chunk_count
    chunks = kernel_call(
        cut_kernel,
        "cut_expand",
        1,
        1,
        1,
        in_specs=[anywhere],
        out_specs=vmem,
        out_shape=pltpu.VMEM((owner_count, rank_block, width), bf16),
        scratch_shapes=[pltpu.SemaphoreType.DMA((chunk_count, owner_count))],
    )(expand)
    near = lax.all_to_all(chunks, "adapter", split_axis=0, concat_axis=0, tiled=True)

    block_count = half_width // block
    counts = [block_count - 1, 0]
    held = kernel_call(
        functools.partial(load_kernel, block, counts),
        "load_weights",
        1,
        1,
        1,
        in_specs=[anywhere] * 2,
        out_specs=vmem,
        out_shape=pltpu.VMEM((sum(counts), depth, block), bf16),
        scratch_shapes=[pltpu.SemaphoreType.DMA((sum(counts),))],
    )(weight, chunks)

    gathered = kernel_call(
        functools.partial(gather_kernel, owner_count),
        "gather_rows",
        2 * row_count * depth * rank,
        4 * row_count * depth + 2 * depth * rank,
        4,
        in_specs=[smem, vmem] + [vmem] * (owner_count + 1) + [anywhere],
        out_specs=[vmem] * 5,
        out_shape=[jax.ShapeDtypeStruct((row_count, depth), bf16)]
        + [jax.ShapeDtypeStruct((rank_block, row_count), f32)] * 4,
        scratch_shapes=[pltpu.VMEM((row_count, depth), bf16)],
    )(
        adapter_slot_index,
        row_adapter_index.reshape(1, row_count),
        *blocks,
        adapter_shrink_weight[0].T,
        held,
    )
    rows, shrink_parts = gathered[0], gathered[1:]

    def base_half(flip, after):
        stream_count = block_count - counts[flip]
        kept = [held] if counts[flip] else []
        return kernel_call(
            functools.partial(base_kernel, flip, block, sum(counts[:flip]), counts[flip]),
            "base_half",
            2 * row_count * depth * half_width,
            2 * depth * half_width,
            4 + (stream_count * depth * block * 2 >> 20),
            in_specs=[vmem, anywhere] + [vmem] * len(kept) + [anywhere],
            out_specs=vmem,
            out_shape=jax.ShapeDtypeStruct((row_count, half_width), f32),
            scratch_shapes=[
                pltpu.VMEM((stream_count, depth, block), bf16),
                pltpu.SemaphoreType.DMA((stream_count,)),
            ],
        )(rows, weight, *kept, after)

    def delta_half(base, shrunk, chunks, after):
        return kernel_call(
            functools.partial(delta_kernel, owner_count, column_block(width)),
            "delta_half",
            2 * row_count * rank_block * owner_count * half_width,
            12 * row_count * half_width,
            8,
            in_specs=[vmem] * (1 + owner_count + chunk_count) + [anywhere],
            out_specs=[vmem] * 2,
            out_shape=[jax.ShapeDtypeStruct((row_count // 2, half_width), f32)] * 2,
            scratch_shapes=[
                pltpu.VMEM((rank_block * owner_count, row_count), f32),
                pltpu.VMEM((row_count, rank_block * owner_count), bf16),
            ],
        )(base, *shrunk, chunks.reshape(owner_count * rank_block, width), after)

    base_first = base_half(0, shrink_parts[0])
    received = [from_tensor(shrink_parts[m], m) for m in (1, 2, 3)]
    *received, near, base_first = lax.optimization_barrier((*received, near, base_first))
    shrunk = shrink_parts[0] + received[0] + received[1] + received[2]
    shrunk = (adapter_scale * shrunk).astype(bf16)
    base_second = base_half(1, shrunk)
    shrunk = [shrunk] + [from_owner(shrunk, j) for j in others]
    far = from_group(near)

    halves = []
    after = shrunk[0]
    middle = row_count // 4
    for base, chunks in ((base_first, near), (base_second, far)):
        keep, send = delta_half(base, shrunk, chunks, after)
        both = keep + from_tensor(send, 1)
        after = both[middle:].astype(bf16)
        crossed = from_tensor(after, 2)
        halves.append((both[:middle] + crossed.astype(f32)).astype(bf16))
    first = jnp.where(g == 0, halves[0], halves[1])
    second = jnp.where(g == 0, halves[1], halves[0])
    return jnp.concatenate([first, second], axis=1)


def on_device(tokens, base_up_weight, adapter_shrink_weight, adapter_expand_weight, *index):
    pairs = lax.axis_size("groups") == 2 and lax.axis_size("tensor") == 4
    few = lax.axis_size("adapter") <= 8
    even = base_up_weight.shape[1] % (2 * lane) == 0 and tokens.shape[0] % 16 == 0
    arrange = paired if pairs and few and even else general
    return arrange(
        tokens, base_up_weight, adapter_shrink_weight, adapter_expand_weight, *index
    )


def solution(mesh):
    placed = (
        P(("groups", "adapter"), "tensor"),
        P("tensor", "adapter"),
        P("adapter", "tensor", None),
        P("adapter", "tensor", None),
        P("groups", None),
        P(),
    )
    return jax.shard_map(
        on_device,
        mesh=mesh,
        in_specs=placed,
        out_specs=P(("groups", "tensor"), "adapter"),
        check_vma=False,
    )
```

```python
import functools

import jax
import jax.numpy as jnp
from jax import lax
from jax.experimental import pallas as pl
from jax.experimental.pallas import tpu as pltpu
from jax.sharding import PartitionSpec as P

adapter_scale = 0.5
lane = 128
f32 = jnp.float32
bf16 = jnp.bfloat16


def general(
    tokens,
    base_up_weight,
    adapter_shrink_weight,
    adapter_expand_weight,
    row_adapter_index,
    adapter_slot_index,
):
    owner_count = lax.axis_size("adapter")
    owner_index = lax.axis_index("adapter")
    tensor_index = lax.axis_index("tensor")
    rank_block = adapter_expand_weight.shape[1]
    columns = base_up_weight.shape[1]
    slot = jnp.take(adapter_slot_index, row_adapter_index[:, 0], axis=0)
    rows = lax.all_gather(tokens, "adapter", axis=0, tiled=True)
    expand = adapter_expand_weight[0].reshape(rank_block, owner_count, columns)
    expand = lax.all_to_all(expand, "adapter", split_axis=1, concat_axis=1, tiled=True)
    shrunk = jnp.dot(rows, adapter_shrink_weight[0], preferred_element_type=f32)
    shrunk = jnp.where((slot == owner_index)[:, None], shrunk, 0.0)
    shrunk = lax.psum(shrunk, ("adapter", "tensor"))
    shrunk = (adapter_scale * shrunk).astype(bf16)
    shrunk = lax.dynamic_slice_in_dim(shrunk, tensor_index * rank_block, rank_block, 1)
    chosen = slot[:, None] == jnp.arange(owner_count, dtype=jnp.int32)[None, :]
    spread = jnp.where(chosen[:, None, :], shrunk[:, :, None], jnp.zeros((), bf16))
    total = jnp.dot(rows, base_up_weight, preferred_element_type=f32)
    total = total + jnp.dot(
        spread.reshape(-1, rank_block * owner_count),
        expand.reshape(rank_block * owner_count, columns),
        preferred_element_type=f32,
    )
    return lax.psum_scatter(total, "tensor", scatter_dimension=0, tiled=True).astype(bf16)


vmem = pl.BlockSpec(memory_space=pltpu.VMEM)
smem = pl.BlockSpec(memory_space=pltpu.SMEM)
anywhere = pl.BlockSpec(memory_space=pl.ANY)


def kernel_call(kernel, name, flops, moved, mib, **specs):
    return pl.pallas_call(
        kernel,
        cost_estimate=pl.CostEstimate(flops=flops, bytes_accessed=moved, transcendentals=0),
        compiler_params=pltpu.CompilerParams(vmem_limit_bytes=mib << 20),
        name=name,
        **specs,
    )


def cut_kernel(owner_count, offsets, far_width, expand, *refs):
    pieces, sem = refs[:-1], refs[-1]
    g, a = lax.axis_index("groups"), lax.axis_index("adapter")
    near_width = pieces[0].shape[1]
    columns = near_width + far_width
    copies = []
    for n, (j, piece) in enumerate(zip(offsets, pieces)):
        to = lax.rem(a - j + owner_count, owner_count)
        start = pl.multiple_of(to * columns + g * far_width, lane)
        copies.append(
            pltpu.make_async_copy(expand.at[0, :, pl.ds(start, near_width)], piece, sem.at[n])
        )
    for copy in copies:
        copy.start()
    for copy in copies:
        copy.wait()


def weight_copies(start, block, weight, target, sem):
    copies = []
    for n in range(target.shape[0]):
        span = pl.ds(pl.multiple_of(start + n * block, lane), block)
        copies.append(pltpu.make_async_copy(weight.at[:, span], target.at[n], sem.at[n]))
    return copies


def load_kernel(starts, counts, block, weight, expand, after, held, own, sem, own_sem):
    a = lax.axis_index("adapter")
    columns = own.shape[1]
    copies, at = [], 0
    for start_of, count in zip(starts, counts):
        span = pl.ds(at, count)
        copies += weight_copies(start_of(), block, weight, held.at[span], sem.at[span])
        at += count
    start = pl.multiple_of(a * columns, columns)
    copies.append(pltpu.make_async_copy(expand.at[0, :, pl.ds(start, columns)], own, own_sem))
    for copy in copies:
        copy.start()
    for copy in copies:
        copy.wait()


def gather_kernel(owner_count, slots, index, *refs):
    blocks = refs[:owner_count]
    shrink, _, rows_out, keep, send, rows, partial = refs[owner_count:]
    a, t = lax.axis_index("adapter"), lax.axis_index("tensor")
    height = blocks[0].shape[0]
    for j in range(owner_count):
        where = lax.rem(a + j, owner_count)
        rows[pl.ds(pl.multiple_of(where * height, height), height), :] = blocks[j][...]
    quarter = rows.shape[0] // 4
    for i, flip in enumerate((0, 2, 1, 3)):
        start = pl.multiple_of(lax.bitwise_xor(t, flip) * quarter, quarter)
        rows_out[i * quarter : (i + 1) * quarter, :] = rows[pl.ds(start, quarter), :]
    product = lax.dot_general(
        shrink[...], rows[...], (((1,), (1,)), ((), ())), preferred_element_type=f32
    )
    partial[...] = jnp.where(slot_of(index, slots) == a, product, 0.0)
    rank_block = partial.shape[0] // 4
    for i, flip in enumerate((0, 2, 1, 3)):
        start = pl.multiple_of(lax.bitwise_xor(t, flip) * rank_block, rank_block)
        target = keep if i < 2 else send
        at = i % 2 * rank_block
        target[at : at + rank_block, :] = partial[pl.ds(start, rank_block), :]


def slot_of(index, slots):
    named = index[...]
    slot = jnp.zeros_like(named)
    for k in range(slots.shape[0]):
        slot = jnp.where(named == k, slots[k], slot)
    return slot


def part_start(near_width, far_width, is_far, first):
    g = lax.axis_index("groups")
    return ((1 - g) * near_width if is_far else g * far_width) + first


def base_kernel(start_of, block, first, held_count, rows, weight, held, *refs):
    total, streamed, sem = refs[-3:]
    copies = []
    if held_count * block < total.shape[1]:
        copies = weight_copies(start_of() + held_count * block, block, weight, streamed, sem)
    for copy in copies:
        copy.start()
    for n in range(total.shape[1] // block):
        if n < held_count:
            part = held[first + n]
        else:
            copies[n - held_count].wait()
            part = streamed[n - held_count]
        total[:, n * block : (n + 1) * block] = jnp.dot(
            rows[...], part, preferred_element_type=f32
        )


def forward_kernel(owner_count, far_width, *refs):
    near, packed = refs[: owner_count - 1], refs[-1]
    height, near_width = near[0].shape
    start = pl.multiple_of(lax.axis_index("groups") * (near_width - far_width), lane)
    for n, piece in enumerate(near):
        packed[n * height : (n + 1) * height, :] = piece[:, pl.ds(start, far_width)]


def delta_kernel(owner_count, offsets, start_of, block, base_count, piece_count, slots, index, *refs):
    bases, refs = refs[:base_count], refs[base_count:]
    own, shrunk = refs[:2]
    pieces = refs[2 : 2 + piece_count]
    *outs, flat, ordered = refs[-6:]
    a, t = lax.axis_index("adapter"), lax.axis_index("tensor")
    row_count = bases[0].shape[0]
    quarter = row_count // 4
    slot = slot_of(index, slots)
    merged = shrunk[...].astype(f32)
    spread = [
        jnp.where(slot == lax.rem(a + j, owner_count), merged, 0.0) for j in (0, *offsets)
    ]
    flat[...] = jnp.concatenate(spread, axis=0).T
    for i, turn in enumerate((0, 2, 1, 3)):
        start = pl.multiple_of(lax.bitwise_xor(t, turn) * quarter, quarter)
        ordered[i * quarter : (i + 1) * quarter, :] = flat[pl.ds(start, quarter), :].astype(bf16)
    left = ordered[...]
    at = 0
    for base in bases:
        for column in range(0, base.shape[1], block):
            source = pl.multiple_of(start_of() + at, lane)
            expand = jnp.concatenate(
                [own[:, pl.ds(source, block)]] + [piece[:, at : at + block] for piece in pieces],
                axis=0,
            )
            total = base[:, column : column + block] + jnp.dot(
                left, expand, preferred_element_type=f32
            )
            for n, out in enumerate(outs):
                out[:, at : at + block] = total[n * quarter : (n + 1) * quarter]
            at += block


def column_block(width):
    for size in (512, 256, 128):
        if width % size == 0:
            return size


def paired(
    tokens,
    base_up_weight,
    adapter_shrink_weight,
    adapter_expand_weight,
    row_adapter_index,
    adapter_slot_index,
):
    owner_count = lax.axis_size("adapter")
    g = lax.axis_index("groups")
    height, depth = tokens.shape
    row_count = height * owner_count
    columns = base_up_weight.shape[1]
    rank_block = adapter_expand_weight.shape[1]
    rank = adapter_shrink_weight.shape[2]
    block = column_block(columns)
    block_count = columns // block
    near_count = max(1, block_count * 8 // 14)
    near_width = near_count * block
    far_width = columns - near_width

    def from_owner(x, j):
        return lax.ppermute(x, "adapter", [(s, (s - j) % owner_count) for s in range(owner_count)])

    def from_tensor(x, m):
        return lax.ppermute(x, "tensor", [(s, s ^ m) for s in range(4)])

    def from_mirror(x, m):
        return lax.ppermute(x, "adapter", [(s, s ^ m) for s in range(owner_count)])

    def from_group(x):
        return lax.ppermute(x, "groups", [(0, 1), (1, 0)])

    weight = pltpu.with_memory_space_constraint(base_up_weight, pltpu.HBM)
    expand = pltpu.with_memory_space_constraint(adapter_expand_weight, pltpu.HBM)
    index = row_adapter_index.reshape(1, row_count)
    others = range(1, owner_count)
    offsets = (2, 1, 3)
    blocks = [tokens] + [from_owner(tokens, j) for j in others]

    pieces = kernel_call(
        functools.partial(cut_kernel, owner_count, offsets, far_width),
        "cut_expand",
        1,
        1,
        1,
        in_specs=[anywhere],
        out_specs=[vmem] * (owner_count - 1),
        out_shape=[pltpu.VMEM((rank_block, near_width), bf16)] * (owner_count - 1),
        scratch_shapes=[pltpu.SemaphoreType.DMA((owner_count - 1,))],
    )(expand)

    def split(count):
        return [(0, count - count // 2), (count - count // 2, count // 2)]

    parts = [(False, *span) for span in split(near_count)]
    parts += [(True, *span) for span in split(block_count - near_count)]
    held_counts = [min(part[2], count) for part, count in zip(parts, (4, 2, 1, 1))]
    starts = [
        functools.partial(part_start, near_width, far_width, is_far, first * block)
        for is_far, first, _ in parts
    ]
    held, own = kernel_call(
        functools.partial(load_kernel, starts, held_counts, block),
        "load_weights",
        1,
        1,
        1,
        in_specs=[anywhere] * 3,
        out_specs=[vmem] * 2,
        out_shape=[
            pltpu.VMEM((sum(held_counts), depth, block), bf16),
            pltpu.VMEM((rank_block, columns), bf16),
        ],
        scratch_shapes=[pltpu.SemaphoreType.DMA((sum(held_counts),)), pltpu.SemaphoreType.DMA],
    )(weight, expand, pieces[0])

    near = [from_owner(pieces[0], offsets[0])]
    *late, own = lax.optimization_barrier((*pieces[1:], own))
    near += [from_owner(piece, j) for piece, j in zip(late, offsets[1:])]
    rows, keep, send = kernel_call(
        functools.partial(gather_kernel, owner_count),
        "gather_rows",
        1,
        1,
        4,
        in_specs=[smem, vmem] + [vmem] * (owner_count + 1) + [anywhere],
        out_specs=[vmem] * 3,
        out_shape=[jax.ShapeDtypeStruct((row_count, depth), bf16)]
        + [jax.ShapeDtypeStruct((rank // 2, row_count), f32)] * 2,
        scratch_shapes=[pltpu.VMEM((row_count, depth), bf16), pltpu.VMEM((rank, row_count), f32)],
    )(adapter_slot_index, index, *blocks, adapter_shrink_weight[0].T, own)

    def base_part(n, *after):
        is_far, first, count = parts[n]
        stream_count = max(1, count - held_counts[n])
        return kernel_call(
            functools.partial(base_kernel, starts[n], block, sum(held_counts[:n]), held_counts[n]),
            "base_part",
            1 if is_far else 2 * row_count * depth * count * block,
            1 if is_far else 2 * depth * count * block,
            4 + (stream_count * depth * block * 2 >> 20),
            in_specs=[vmem, anywhere, vmem] + [anywhere] * len(after),
            out_specs=vmem,
            out_shape=jax.ShapeDtypeStruct((row_count, count * block), f32),
            scratch_shapes=[
                pltpu.VMEM((stream_count, depth, block), bf16),
                pltpu.SemaphoreType.DMA((stream_count,)),
            ],
        )(rows, weight, held, *after)

    def delta_part(is_far, bases, pieces, shrunk):
        start_of = functools.partial(part_start, near_width, far_width, is_far, 0)
        width = sum(base.shape[1] for base in bases)
        return kernel_call(
            functools.partial(
                delta_kernel, owner_count, offsets, start_of, block, len(bases), len(pieces)
            ),
            "delta_part",
            1,
            1,
            8,
            in_specs=[smem] + [vmem] * (3 + len(bases) + len(pieces)),
            out_specs=[vmem] * 4,
            out_shape=[jax.ShapeDtypeStruct((row_count // 4, width), f32)] * 4,
            scratch_shapes=[
                pltpu.VMEM((row_count, rank_block * owner_count), f32),
                pltpu.VMEM((row_count, rank_block * owner_count), bf16),
            ],
        )(adapter_slot_index, index, *bases, own, shrunk, *pieces)

    arrived = from_tensor(send, 1)
    base_0 = base_part(0, send)
    arrived, base_0 = lax.optimization_barrier((arrived, base_0))
    pair = keep + arrived
    arrived = from_tensor(pair[rank_block:], 2)
    base_1 = base_part(1, pair)
    arrived, base_1, *near = lax.optimization_barrier((arrived, base_1, *near))
    shrunk = (adapter_scale * (pair[:rank_block] + arrived)).astype(bf16)
    packed = kernel_call(
        functools.partial(forward_kernel, owner_count, far_width),
        "pack_far",
        1,
        1,
        2,
        in_specs=[vmem] * (owner_count - 1),
        out_specs=vmem,
        out_shape=jax.ShapeDtypeStruct(((owner_count - 1) * rank_block, far_width), bf16),
    )(*near)
    far = from_group(packed)
    steps = []
    m = 1
    while m < owner_count:
        steps.append(m)
        m *= 2
    base_far = []
    for m, n in zip(steps, (2, 3)):
        arrived = from_mirror(shrunk, m)
        base = base_part(n, shrunk, packed)
        arrived, base = lax.optimization_barrier((arrived, base))
        base_far.append(base)
        shrunk = shrunk + arrived

    halves = []
    for is_far, bases, pieces in ((False, [base_0, base_1], near), (True, base_far, [far])):
        own_keep, cross_keep, own_send, cross_send = delta_part(is_far, bases, pieces, shrunk)
        cross = cross_keep + from_tensor(cross_send, 1)
        kept = own_keep + from_tensor(own_send, 1)
        crossed = from_tensor(cross.astype(bf16), 2)
        halves.append((kept + crossed.astype(f32)).astype(bf16))
    first = jnp.concatenate(halves, axis=1)
    second = jnp.concatenate(halves[::-1], axis=1)
    return jnp.where(g == 0, first, second)


def on_device(tokens, base_up_weight, adapter_shrink_weight, adapter_expand_weight, *index):
    pairs = lax.axis_size("groups") == 2 and lax.axis_size("tensor") == 4
    few = lax.axis_size("adapter") == 4
    even = base_up_weight.shape[1] % (2 * lane) == 0 and tokens.shape[0] % 16 == 0
    arrange = paired if pairs and few and even else general
    return arrange(
        tokens, base_up_weight, adapter_shrink_weight, adapter_expand_weight, *index
    )


def solution(mesh):
    placed = (
        P(("groups", "adapter"), "tensor"),
        P("tensor", "adapter"),
        P("adapter", "tensor", None),
        P("adapter", "tensor", None),
        P("groups", None),
        P(),
    )
    return jax.shard_map(
        on_device,
        mesh=mesh,
        in_specs=placed,
        out_specs=P(("groups", "tensor"), "adapter"),
        check_vma=False,
    )
```

```python
import functools

import jax
import jax.numpy as jnp
from jax import lax
from jax.experimental import pallas as pl
from jax.experimental.pallas import tpu as pltpu
from jax.sharding import PartitionSpec as P

adapter_scale = 0.5
lane = 128
f32 = jnp.float32
bf16 = jnp.bfloat16


def general(
    tokens,
    base_up_weight,
    adapter_shrink_weight,
    adapter_expand_weight,
    row_adapter_index,
    adapter_slot_index,
):
    owner_count = lax.axis_size("adapter")
    owner_index = lax.axis_index("adapter")
    tensor_index = lax.axis_index("tensor")
    rank_block = adapter_expand_weight.shape[1]
    columns = base_up_weight.shape[1]
    slot = jnp.take(adapter_slot_index, row_adapter_index[:, 0], axis=0)
    rows = lax.all_gather(tokens, "adapter", axis=0, tiled=True)
    expand = adapter_expand_weight[0].reshape(rank_block, owner_count, columns)
    expand = lax.all_to_all(expand, "adapter", split_axis=1, concat_axis=1, tiled=True)
    shrunk = jnp.dot(rows, adapter_shrink_weight[0], preferred_element_type=f32)
    shrunk = jnp.where((slot == owner_index)[:, None], shrunk, 0.0)
    shrunk = lax.psum(shrunk, ("adapter", "tensor"))
    shrunk = (adapter_scale * shrunk).astype(bf16)
    shrunk = lax.dynamic_slice_in_dim(shrunk, tensor_index * rank_block, rank_block, 1)
    chosen = slot[:, None] == jnp.arange(owner_count, dtype=jnp.int32)[None, :]
    spread = jnp.where(chosen[:, None, :], shrunk[:, :, None], jnp.zeros((), bf16))
    total = jnp.dot(rows, base_up_weight, preferred_element_type=f32)
    total = total + jnp.dot(
        spread.reshape(-1, rank_block * owner_count),
        expand.reshape(rank_block * owner_count, columns),
        preferred_element_type=f32,
    )
    return lax.psum_scatter(total, "tensor", scatter_dimension=0, tiled=True).astype(bf16)


vmem = pl.BlockSpec(memory_space=pltpu.VMEM)
anywhere = pl.BlockSpec(memory_space=pl.ANY)


def kernel_call(kernel, name, flops, moved, mib, **specs):
    return pl.pallas_call(
        kernel,
        cost_estimate=pl.CostEstimate(flops=flops, bytes_accessed=moved, transcendentals=0),
        compiler_params=pltpu.CompilerParams(vmem_limit_bytes=mib << 20),
        name=name,
        **specs,
    )


def cut_kernel(owner_count, offsets, far_width, tokens, expand, *refs):
    pieces, sem = refs[:-1], refs[-1]
    g, a = lax.axis_index("groups"), lax.axis_index("adapter")
    depth = tokens.shape[1]
    near_width = pieces[-1].shape[1]
    columns = near_width + far_width
    copies = [pltpu.make_async_copy(tokens, pieces[0].at[:, pl.ds(0, depth)], sem.at[len(pieces)])]
    for n, (j, piece) in enumerate(zip(offsets, pieces)):
        to = lax.rem(a - j + owner_count, owner_count)
        start = pl.multiple_of(to * columns + g * far_width, lane)
        target = piece.at[:, pl.ds(depth, near_width)] if n == 0 else piece
        copies.append(
            pltpu.make_async_copy(expand.at[0, :, pl.ds(start, near_width)], target, sem.at[n])
        )
    for copy in copies:
        copy.start()
    for copy in copies:
        copy.wait()


def weight_copies(start, block, weight, target, sem):
    copies = []
    for n in range(target.shape[0]):
        span = pl.ds(pl.multiple_of(start + n * block, lane), block)
        copies.append(pltpu.make_async_copy(weight.at[:, span], target.at[n], sem.at[n]))
    return copies


def load_kernel(starts, counts, block, weight, expand, after, held, own, sem, own_sem):
    a = lax.axis_index("adapter")
    columns = own.shape[1]
    copies, at = [], 0
    for start_of, count in zip(starts, counts):
        span = pl.ds(at, count)
        copies += weight_copies(start_of(), block, weight, held.at[span], sem.at[span])
        at += count
    start = pl.multiple_of(a * columns, columns)
    copies.append(pltpu.make_async_copy(expand.at[0, :, pl.ds(start, columns)], own, own_sem))
    for copy in copies:
        copy.start()
    for copy in copies:
        copy.wait()


def gather_kernel(offsets, slots, index, *refs):
    owner_count = len(offsets)
    blocks = refs[:owner_count]
    shrink, _, rows_out, keep, send, slot_out, rows, partial = refs[owner_count:]
    a, t = lax.axis_index("adapter"), lax.axis_index("tensor")
    height, depth = blocks[0].shape
    for j, part in zip(offsets, blocks):
        where = lax.rem(a + j, owner_count)
        rows[pl.ds(pl.multiple_of(where * height, height), height), :] = part[:, :depth]
    quarter = rows.shape[0] // 4
    for i, flip in enumerate((0, 2, 1, 3)):
        start = pl.multiple_of(lax.bitwise_xor(t, flip) * quarter, quarter)
        rows_out[i * quarter : (i + 1) * quarter, :] = rows[pl.ds(start, quarter), :]
    product = lax.dot_general(
        shrink[...], rows[...], (((1,), (1,)), ((), ())), preferred_element_type=f32
    )
    named, table = index[...], slots[...]
    slot = jnp.zeros_like(named)
    for k in range(table.shape[1]):
        slot = jnp.where(named == k, table[:, k : k + 1], slot)
    slot_out[...] = slot
    partial[...] = jnp.where(slot == a, product, 0.0)
    rank_block = partial.shape[0] // 4
    for i, flip in enumerate((0, 2, 1, 3)):
        start = pl.multiple_of(lax.bitwise_xor(t, flip) * rank_block, rank_block)
        target = keep if i < 2 else send
        at = i % 2 * rank_block
        target[at : at + rank_block, :] = partial[pl.ds(start, rank_block), :]


def part_start(near_width, far_width, is_far, first):
    g = lax.axis_index("groups")
    return ((1 - g) * near_width if is_far else g * far_width) + first


def base_kernel(start_of, block, first, held_count, rows, weight, held, *refs):
    total, streamed, sem = refs[-3:]
    copies = []
    if held_count * block < total.shape[1]:
        copies = weight_copies(start_of() + held_count * block, block, weight, streamed, sem)
    for copy in copies:
        copy.start()
    for n in range(total.shape[1] // block):
        if n < held_count:
            part = held[first + n]
        else:
            copies[n - held_count].wait()
            part = streamed[n - held_count]
        total[:, n * block : (n + 1) * block] = jnp.dot(
            rows[...], part, preferred_element_type=f32
        )


def forward_kernel(far_width, *refs):
    *near, packed = refs
    height, near_width = near[-1].shape
    start = pl.multiple_of(lax.axis_index("groups") * (near_width - far_width), lane)
    for n, piece in enumerate(near):
        skip = piece.shape[1] - near_width
        packed[n * height : (n + 1) * height, :] = piece[:, pl.ds(start + skip, far_width)]


def delta_kernel(owner_count, offsets, start_of, block, base_count, piece_count, slot, *refs):
    bases, refs = refs[:base_count], refs[base_count:]
    own, shrunk = refs[:2]
    pieces = refs[2 : 2 + piece_count]
    width = sum(base.shape[1] for base in bases)
    *outs, flat, ordered = refs[-6:]
    a, t = lax.axis_index("adapter"), lax.axis_index("tensor")
    row_count = bases[0].shape[0]
    quarter = row_count // 4
    slot = slot[...]
    merged = shrunk[...].astype(f32)
    spread = [
        jnp.where(slot == lax.rem(a + j, owner_count), merged, 0.0) for j in (0, *offsets)
    ]
    flat[...] = jnp.concatenate(spread, axis=0).T
    for i, turn in enumerate((0, 2, 1, 3)):
        start = pl.multiple_of(lax.bitwise_xor(t, turn) * quarter, quarter)
        ordered[i * quarter : (i + 1) * quarter, :] = flat[pl.ds(start, quarter), :].astype(bf16)
    left = ordered[...]
    at = 0
    for base in bases:
        for column in range(0, base.shape[1], block):
            source = pl.multiple_of(start_of() + at, lane)
            expand = jnp.concatenate(
                [own[:, pl.ds(source, block)]]
                + [piece[:, pl.ds(piece.shape[1] - width + at, block)] for piece in pieces],
                axis=0,
            )
            total = base[:, column : column + block] + jnp.dot(
                left, expand, preferred_element_type=f32
            )
            for n, out in enumerate(outs):
                out[:, at : at + block] = total[n * quarter : (n + 1) * quarter]
            at += block


def column_block(width):
    for size in (512, 256, 128):
        if width % size == 0:
            return size


def paired(
    tokens,
    base_up_weight,
    adapter_shrink_weight,
    adapter_expand_weight,
    row_adapter_index,
    adapter_slot_index,
):
    owner_count = lax.axis_size("adapter")
    g = lax.axis_index("groups")
    height, depth = tokens.shape
    row_count = height * owner_count
    columns = base_up_weight.shape[1]
    rank_block = adapter_expand_weight.shape[1]
    rank = adapter_shrink_weight.shape[2]
    block = column_block(columns)
    block_count = columns // block
    near_count = max(1, block_count * 8 // 14)
    near_width = near_count * block
    far_width = columns - near_width

    def from_owner(x, j):
        return lax.ppermute(x, "adapter", [(s, (s - j) % owner_count) for s in range(owner_count)])

    def from_tensor(x, m):
        return lax.ppermute(x, "tensor", [(s, s ^ m) for s in range(4)])

    def from_mirror(x, m):
        return lax.ppermute(x, "adapter", [(s, s ^ m) for s in range(owner_count)])

    def from_group(x):
        return lax.ppermute(x, "groups", [(0, 1), (1, 0)])

    weight = pltpu.with_memory_space_constraint(base_up_weight, pltpu.HBM)
    expand = pltpu.with_memory_space_constraint(adapter_expand_weight, pltpu.HBM)
    index = row_adapter_index.reshape(1, row_count)
    offsets = (2, 1, 3)
    blocks = [from_owner(tokens, j) for j in offsets[1:]]

    pieces = kernel_call(
        functools.partial(cut_kernel, owner_count, offsets, far_width),
        "cut_expand",
        1,
        1,
        1,
        in_specs=[anywhere] * 2,
        out_specs=[vmem] * (owner_count - 1),
        out_shape=[pltpu.VMEM((rank_block, depth + near_width), bf16)]
        + [pltpu.VMEM((rank_block, near_width), bf16)] * (owner_count - 2),
        scratch_shapes=[pltpu.SemaphoreType.DMA((owner_count,))],
    )(tokens, expand)
    near = [from_owner(piece, j) for piece, j in zip(pieces, offsets)]

    def split(count):
        return [(0, count - count // 2), (count - count // 2, count // 2)]

    parts = [(False, *span) for span in split(near_count)]
    parts += [(True, *span) for span in split(block_count - near_count)]
    held_counts = [min(part[2], count) for part, count in zip(parts, (4, 4, 3, 3))]
    starts = [
        functools.partial(part_start, near_width, far_width, is_far, first * block)
        for is_far, first, _ in parts
    ]
    held, own = kernel_call(
        functools.partial(load_kernel, starts, held_counts, block),
        "load_weights",
        1,
        1,
        1,
        in_specs=[anywhere] * 3,
        out_specs=[vmem] * 2,
        out_shape=[
            pltpu.VMEM((sum(held_counts), depth, block), bf16),
            pltpu.VMEM((rank_block, columns), bf16),
        ],
        scratch_shapes=[pltpu.SemaphoreType.DMA((sum(held_counts),)), pltpu.SemaphoreType.DMA],
    )(weight, expand, pieces[0])

    rows, keep, send, slot = kernel_call(
        functools.partial(gather_kernel, (0, *offsets)),
        "gather_rows",
        1,
        1,
        4,
        in_specs=[vmem] * (owner_count + 3) + [anywhere],
        out_specs=[vmem] * 4,
        out_shape=[jax.ShapeDtypeStruct((row_count, depth), bf16)]
        + [jax.ShapeDtypeStruct((rank // 2, row_count), f32)] * 2
        + [jax.ShapeDtypeStruct((1, row_count), jnp.int32)],
        scratch_shapes=[pltpu.VMEM((row_count, depth), bf16), pltpu.VMEM((rank, row_count), f32)],
    )(
        adapter_slot_index.reshape(1, owner_count),
        index,
        tokens,
        near[0],
        *blocks,
        adapter_shrink_weight[0].T,
        own,
    )

    def base_part(n, *after):
        is_far, first, count = parts[n]
        stream_count = max(1, count - held_counts[n])
        return kernel_call(
            functools.partial(base_kernel, starts[n], block, sum(held_counts[:n]), held_counts[n]),
            "base_part",
            1 if is_far else 2 * row_count * depth * count * block,
            1 if is_far else 2 * depth * count * block,
            4 + (stream_count * depth * block * 2 >> 20),
            in_specs=[vmem, anywhere, vmem] + [anywhere] * len(after),
            out_specs=vmem,
            out_shape=jax.ShapeDtypeStruct((row_count, count * block), f32),
            scratch_shapes=[
                pltpu.VMEM((stream_count, depth, block), bf16),
                pltpu.SemaphoreType.DMA((stream_count,)),
            ],
        )(rows, weight, held, *after)

    def delta_part(is_far, bases, pieces):
        start_of = functools.partial(part_start, near_width, far_width, is_far, 0)
        width = sum(base.shape[1] for base in bases)
        return kernel_call(
            functools.partial(
                delta_kernel, owner_count, offsets, start_of, block, len(bases), len(pieces)
            ),
            "delta_part",
            1,
            1,
            8,
            in_specs=[vmem] * (3 + len(bases) + len(pieces)),
            out_specs=[vmem] * 4,
            out_shape=[jax.ShapeDtypeStruct((row_count // 4, width), f32)] * 4,
            scratch_shapes=[
                pltpu.VMEM((row_count, rank_block * owner_count), f32),
                pltpu.VMEM((row_count, rank_block * owner_count), bf16),
            ],
        )(slot, *bases, own, shrunk, *pieces)

    arrived = from_tensor(send, 1)
    base_0 = base_part(0, send)
    arrived, base_0 = lax.optimization_barrier((arrived, base_0))
    pair = keep + arrived
    arrived = from_tensor(pair[rank_block:], 2)
    base_1 = base_part(1, pair)
    arrived, base_1, *near = lax.optimization_barrier((arrived, base_1, *near))
    shrunk = (adapter_scale * (pair[:rank_block] + arrived)).astype(bf16)
    packed = kernel_call(
        functools.partial(forward_kernel, far_width),
        "pack_far",
        1,
        1,
        2,
        in_specs=[vmem] * (owner_count - 1),
        out_specs=vmem,
        out_shape=jax.ShapeDtypeStruct(((owner_count - 1) * rank_block, far_width), bf16),
    )(*near)
    far = from_group(packed)
    steps = []
    m = 1
    while m < owner_count:
        steps.append(m)
        m *= 2
    base_far = []
    for m, n in zip(steps, (2, 3)):
        arrived = from_mirror(shrunk, m)
        base = base_part(n, shrunk, packed)
        arrived, base = lax.optimization_barrier((arrived, base))
        base_far.append(base)
        shrunk = shrunk + arrived

    halves = []
    for is_far, bases, pieces in ((False, [base_0, base_1], near), (True, base_far, [far])):
        own_keep, cross_keep, own_send, cross_send = delta_part(is_far, bases, pieces)
        cross = (cross_keep + from_tensor(cross_send, 1)).astype(bf16)
        kept = own_keep + from_tensor(own_send, 1)
        crossed = from_tensor(cross, 2)
        halves.append((kept + crossed.astype(f32)).astype(bf16))
    first = jnp.concatenate(halves, axis=1)
    second = jnp.concatenate(halves[::-1], axis=1)
    return jnp.where(g == 0, first, second)


def on_device(tokens, base_up_weight, adapter_shrink_weight, adapter_expand_weight, *index):
    pairs = lax.axis_size("groups") == 2 and lax.axis_size("tensor") == 4
    few = lax.axis_size("adapter") == 4
    even = base_up_weight.shape[1] % (2 * lane) == 0 and tokens.shape[0] % 16 == 0
    arrange = paired if pairs and few and even else general
    return arrange(
        tokens, base_up_weight, adapter_shrink_weight, adapter_expand_weight, *index
    )


def solution(mesh):
    placed = (
        P(("groups", "adapter"), "tensor"),
        P("tensor", "adapter"),
        P("adapter", "tensor", None),
        P("adapter", "tensor", None),
        P("groups", None),
        P(),
    )
    return jax.shard_map(
        on_device,
        mesh=mesh,
        in_specs=placed,
        out_specs=P(("groups", "tensor"), "adapter"),
        check_vma=False,
    )
```

```python
import functools

import jax
import jax.numpy as jnp
from jax import lax
from jax.experimental import pallas as pl
from jax.experimental.pallas import tpu as pltpu
from jax.sharding import PartitionSpec as P

adapter_scale = 0.5
lane = 128
f32 = jnp.float32
bf16 = jnp.bfloat16


def general(
    tokens,
    base_up_weight,
    adapter_shrink_weight,
    adapter_expand_weight,
    row_adapter_index,
    adapter_slot_index,
):
    owner_count = lax.axis_size("adapter")
    owner_index = lax.axis_index("adapter")
    tensor_index = lax.axis_index("tensor")
    rank_block = adapter_expand_weight.shape[1]
    columns = base_up_weight.shape[1]
    slot = jnp.take(adapter_slot_index, row_adapter_index[:, 0], axis=0)
    rows = lax.all_gather(tokens, "adapter", axis=0, tiled=True)
    expand = adapter_expand_weight[0].reshape(rank_block, owner_count, columns)
    expand = lax.all_to_all(expand, "adapter", split_axis=1, concat_axis=1, tiled=True)
    shrunk = jnp.dot(rows, adapter_shrink_weight[0], preferred_element_type=f32)
    shrunk = jnp.where((slot == owner_index)[:, None], shrunk, 0.0)
    shrunk = lax.psum(shrunk, ("adapter", "tensor"))
    shrunk = (adapter_scale * shrunk).astype(bf16)
    shrunk = lax.dynamic_slice_in_dim(shrunk, tensor_index * rank_block, rank_block, 1)
    chosen = slot[:, None] == jnp.arange(owner_count, dtype=jnp.int32)[None, :]
    spread = jnp.where(chosen[:, None, :], shrunk[:, :, None], jnp.zeros((), bf16))
    total = jnp.dot(rows, base_up_weight, preferred_element_type=f32)
    total = total + jnp.dot(
        spread.reshape(-1, rank_block * owner_count),
        expand.reshape(rank_block * owner_count, columns),
        preferred_element_type=f32,
    )
    return lax.psum_scatter(total, "tensor", scatter_dimension=0, tiled=True).astype(bf16)


vmem = pl.BlockSpec(memory_space=pltpu.VMEM)
anywhere = pl.BlockSpec(memory_space=pl.ANY)


def kernel_call(kernel, name, flops, moved, mib, **specs):
    return pl.pallas_call(
        kernel,
        cost_estimate=pl.CostEstimate(flops=flops, bytes_accessed=moved, transcendentals=0),
        compiler_params=pltpu.CompilerParams(vmem_limit_bytes=mib << 20),
        name=name,
        **specs,
    )


def cut_kernel(owner_count, offsets, far_width, small_count, expand, *refs):
    small, refs = refs[:small_count], refs[small_count:]
    *pieces, own = refs[: owner_count]
    loaded, sem = refs[owner_count:-1], refs[-1]
    g, a = lax.axis_index("groups"), lax.axis_index("adapter")
    near_width = pieces[0].shape[1]
    columns = near_width + far_width
    start = pl.multiple_of(a * columns, lane)
    copies = [
        pltpu.make_async_copy(expand.at[0, :, pl.ds(start, columns)], own, sem.at[len(pieces)])
    ]
    for n, (j, piece) in enumerate(zip(offsets, pieces)):
        to = lax.rem(a - j + owner_count, owner_count)
        start = pl.multiple_of(to * columns + g * far_width, lane)
        copies.append(
            pltpu.make_async_copy(expand.at[0, :, pl.ds(start, near_width)], piece, sem.at[n])
        )
    for n, (source, target) in enumerate(zip(small, loaded)):
        copies.append(pltpu.make_async_copy(source, target, sem.at[owner_count + n]))
    for copy in copies:
        copy.start()
    for copy in copies:
        copy.wait()


def weight_copies(start, block, weight, target, sem):
    band_count = sem.shape[1]
    band = weight.shape[0] // band_count
    blocks = []
    for n in range(target.shape[0]):
        span = pl.ds(pl.multiple_of(start + n * block, lane), block)
        bands = []
        for m in range(band_count):
            rows = pl.ds(m * band, band)
            bands.append(
                pltpu.make_async_copy(
                    weight.at[rows, span], target.at[n, rows], sem.at[n, m]
                )
            )
        blocks.append(bands)
    return blocks


def gather_kernel(offsets, slots, index, *refs):
    owner_count = len(offsets)
    blocks = refs[:owner_count]
    shrink, rows_out, keep, send, slot_out, rows, partial = refs[owner_count:]
    a, t = lax.axis_index("adapter"), lax.axis_index("tensor")
    height, depth = blocks[0].shape
    for j, part in zip(offsets, blocks):
        where = lax.rem(a + j, owner_count)
        rows[pl.ds(pl.multiple_of(where * height, height), height), :] = part[:, :depth]
    quarter = rows.shape[0] // 4
    for i, flip in enumerate((0, 2, 1, 3)):
        start = pl.multiple_of(lax.bitwise_xor(t, flip) * quarter, quarter)
        rows_out[i * quarter : (i + 1) * quarter, :] = rows[pl.ds(start, quarter), :]
    product = lax.dot_general(
        shrink[...], rows[...], (((1,), (1,)), ((), ())), preferred_element_type=f32
    )
    named, table = index[...], slots[...]
    slot = jnp.zeros_like(named)
    for k in range(table.shape[1]):
        slot = jnp.where(named == k, table[:, k : k + 1], slot)
    slot_out[...] = slot
    partial[...] = jnp.where(slot == a, product, 0.0)
    rank_block = partial.shape[0] // 4
    for i, flip in enumerate((0, 2, 1, 3)):
        start = pl.multiple_of(lax.bitwise_xor(t, flip) * rank_block, rank_block)
        target = keep if i < 2 else send
        at = i % 2 * rank_block
        target[at : at + rank_block, :] = partial[pl.ds(start, rank_block), :]


def part_start(near_width, far_width, is_far, first):
    g = lax.axis_index("groups")
    return ((1 - g) * near_width if is_far else g * far_width) + first


def base_kernel(start_of, block, rows, weight, *refs):
    total, streamed, sem = refs[-3:]
    copies = weight_copies(start_of(), block, weight, streamed, sem)
    for bands in copies:
        for copy in bands:
            copy.start()
    for n, bands in enumerate(copies):
        for copy in bands:
            copy.wait()
        total[:, n * block : (n + 1) * block] = jnp.dot(
            rows[...], streamed[n], preferred_element_type=f32
        )


def forward_kernel(far_width, *refs):
    *near, packed = refs
    height, near_width = near[-1].shape
    start = pl.multiple_of(lax.axis_index("groups") * (near_width - far_width), lane)
    for n, piece in enumerate(near):
        skip = piece.shape[1] - near_width
        packed[n * height : (n + 1) * height, :] = piece[:, pl.ds(start + skip, far_width)]


def delta_kernel(owner_count, offsets, start_of, block, base_count, piece_count, slot, *refs):
    bases, refs = refs[:base_count], refs[base_count:]
    own, shrunk = refs[:2]
    pieces = refs[2 : 2 + piece_count]
    width = sum(base.shape[1] for base in bases)
    *outs, flat, ordered = refs[-6:]
    a, t = lax.axis_index("adapter"), lax.axis_index("tensor")
    row_count = bases[0].shape[0]
    quarter = row_count // 4
    slot = slot[...]
    merged = shrunk[...].astype(f32)
    spread = [
        jnp.where(slot == lax.rem(a + j, owner_count), merged, 0.0) for j in (0, *offsets)
    ]
    flat[...] = jnp.concatenate(spread, axis=0).T
    for i, turn in enumerate((0, 2, 1, 3)):
        start = pl.multiple_of(lax.bitwise_xor(t, turn) * quarter, quarter)
        ordered[i * quarter : (i + 1) * quarter, :] = flat[pl.ds(start, quarter), :].astype(bf16)
    left = ordered[...]
    at = 0
    for base in bases:
        for column in range(0, base.shape[1], block):
            source = pl.multiple_of(start_of() + at, lane)
            expand = jnp.concatenate(
                [own[:, pl.ds(source, block)]]
                + [piece[:, pl.ds(piece.shape[1] - width + at, block)] for piece in pieces],
                axis=0,
            )
            total = base[:, column : column + block] + jnp.dot(
                left, expand, preferred_element_type=f32
            )
            for n, out in enumerate(outs):
                out[:, at : at + block] = total[n * quarter : (n + 1) * quarter]
            at += block


def column_block(width):
    for size in (512, 256, 128):
        if width % size == 0:
            return size


def paired(
    tokens,
    base_up_weight,
    adapter_shrink_weight,
    adapter_expand_weight,
    row_adapter_index,
    adapter_slot_index,
):
    owner_count = lax.axis_size("adapter")
    g = lax.axis_index("groups")
    height, depth = tokens.shape
    row_count = height * owner_count
    columns = base_up_weight.shape[1]
    rank_block = adapter_expand_weight.shape[1]
    rank = adapter_shrink_weight.shape[2]
    block = column_block(columns)
    block_count = columns // block
    near_count = max(1, block_count * 8 // 14)
    near_width = near_count * block
    far_width = columns - near_width

    def from_owner(x, j):
        return lax.ppermute(x, "adapter", [(s, (s - j) % owner_count) for s in range(owner_count)])

    def from_tensor(x, m):
        return lax.ppermute(x, "tensor", [(s, s ^ m) for s in range(4)])

    def from_mirror(x, m):
        return lax.ppermute(x, "adapter", [(s, s ^ m) for s in range(owner_count)])

    def from_group(x):
        return lax.ppermute(x, "groups", [(0, 1), (1, 0)])

    weight = pltpu.with_memory_space_constraint(base_up_weight, pltpu.HBM)
    expand = pltpu.with_memory_space_constraint(adapter_expand_weight, pltpu.HBM)
    offsets = (2, 1, 3)
    blocks = [from_owner(tokens, j) for j in offsets]

    small = [
        pltpu.with_memory_space_constraint(x, pltpu.HBM)
        for x in (
            adapter_slot_index.reshape(1, owner_count),
            row_adapter_index.reshape(1, row_count),
            tokens,
            adapter_shrink_weight[0].T,
        )
    ]
    cut = kernel_call(
        functools.partial(cut_kernel, owner_count, offsets, far_width, len(small)),
        "cut_expand",
        1,
        1,
        1,
        in_specs=[anywhere] * (1 + len(small)),
        out_specs=[vmem] * (owner_count + len(small)),
        out_shape=[pltpu.VMEM((rank_block, near_width), bf16)] * (owner_count - 1)
        + [pltpu.VMEM((rank_block, columns), bf16)]
        + [pltpu.VMEM(x.shape, x.dtype) for x in small],
        scratch_shapes=[pltpu.SemaphoreType.DMA((owner_count + len(small),))],
    )(expand, *small)
    pieces, own = cut[: owner_count - 1], cut[owner_count - 1]
    slots, index, mine, shrink = cut[owner_count:]
    near = [from_owner(piece, j) for piece, j in zip(pieces, offsets)]

    def split(count):
        return [(0, count - count // 2), (count - count // 2, count // 2)]

    parts = [(False, *span) for span in split(near_count)]
    parts += [(True, *span) for span in split(block_count - near_count)]
    starts = [
        functools.partial(part_start, near_width, far_width, is_far, first * block)
        for is_far, first, _ in parts
    ]
    bands = 4
    rows, keep, send, slot = kernel_call(
        functools.partial(gather_kernel, (0, *offsets)),
        "gather_rows",
        1,
        1,
        4,
        in_specs=[vmem] * (owner_count + 3),
        out_specs=[vmem] * 4,
        out_shape=[jax.ShapeDtypeStruct((row_count, depth), bf16)]
        + [jax.ShapeDtypeStruct((rank // 2, row_count), f32)] * 2
        + [jax.ShapeDtypeStruct((1, row_count), jnp.int32)],
        scratch_shapes=[pltpu.VMEM((row_count, depth), bf16), pltpu.VMEM((rank, row_count), f32)],
    )(
        slots,
        index,
        mine,
        *blocks,
        shrink,
    )

    def base_part(n, *after):
        is_far, first, count = parts[n]
        return kernel_call(
            functools.partial(base_kernel, starts[n], block),
            "base_part",
            1 if is_far else 2 * row_count * depth * count * block,
            1 if is_far else 2 * depth * count * block,
            4 + (count * depth * block * 2 >> 20),
            in_specs=[vmem, anywhere] + [anywhere] * len(after),
            out_specs=vmem,
            out_shape=jax.ShapeDtypeStruct((row_count, count * block), f32),
            scratch_shapes=[
                pltpu.VMEM((count, depth, block), bf16),
                pltpu.SemaphoreType.DMA((count, bands)),
            ],
        )(rows, weight, *after)

    def delta_part(is_far, bases, pieces):
        start_of = functools.partial(part_start, near_width, far_width, is_far, 0)
        width = sum(base.shape[1] for base in bases)
        return kernel_call(
            functools.partial(
                delta_kernel, owner_count, offsets, start_of, block, len(bases), len(pieces)
            ),
            "delta_part",
            1,
            1,
            8,
            in_specs=[vmem] * (3 + len(bases) + len(pieces)),
            out_specs=[vmem] * 4,
            out_shape=[jax.ShapeDtypeStruct((row_count // 4, width), f32)] * 4,
            scratch_shapes=[
                pltpu.VMEM((row_count, rank_block * owner_count), f32),
                pltpu.VMEM((row_count, rank_block * owner_count), bf16),
            ],
        )(slot, *bases, own, shrunk, *pieces)

    arrived = from_tensor(send, 1)
    base_0 = base_part(0, send)
    arrived, base_0 = lax.optimization_barrier((arrived, base_0))
    pair = keep + arrived
    arrived = from_tensor(pair[rank_block:], 2)
    base_1 = base_part(1, pair)
    arrived, base_1, *near = lax.optimization_barrier((arrived, base_1, *near))
    shrunk = (adapter_scale * (pair[:rank_block] + arrived)).astype(bf16)
    packed = kernel_call(
        functools.partial(forward_kernel, far_width),
        "pack_far",
        1,
        1,
        2,
        in_specs=[vmem] * (owner_count - 1),
        out_specs=vmem,
        out_shape=jax.ShapeDtypeStruct(((owner_count - 1) * rank_block, far_width), bf16),
    )(*near)
    far = from_group(packed)
    steps = []
    m = 1
    while m < owner_count:
        steps.append(m)
        m *= 2
    base_far = []
    for m, n in zip(steps, (2, 3)):
        arrived = from_mirror(shrunk, m)
        base = base_part(n, shrunk, packed)
        arrived, base = lax.optimization_barrier((arrived, base))
        base_far.append(base)
        shrunk = shrunk + arrived

    halves = []
    for is_far, bases, pieces in ((False, [base_0, base_1], near), (True, base_far, [far])):
        own_keep, cross_keep, own_send, cross_send = delta_part(is_far, bases, pieces)
        cross = (cross_keep + from_tensor(cross_send, 1)).astype(bf16)
        kept = own_keep + from_tensor(own_send, 1)
        crossed = from_tensor(cross, 2)
        halves.append((kept + crossed.astype(f32)).astype(bf16))
    first = jnp.concatenate(halves, axis=1)
    second = jnp.concatenate(halves[::-1], axis=1)
    return jnp.where(g == 0, first, second)


def on_device(tokens, base_up_weight, adapter_shrink_weight, adapter_expand_weight, *index):
    pairs = lax.axis_size("groups") == 2 and lax.axis_size("tensor") == 4
    few = lax.axis_size("adapter") == 4
    even = base_up_weight.shape[1] % (2 * lane) == 0 and tokens.shape[0] % 16 == 0
    arrange = paired if pairs and few and even else general
    return arrange(
        tokens, base_up_weight, adapter_shrink_weight, adapter_expand_weight, *index
    )


def solution(mesh):
    placed = (
        P(("groups", "adapter"), "tensor"),
        P("tensor", "adapter"),
        P("adapter", "tensor", None),
        P("adapter", "tensor", None),
        P("groups", None),
        P(),
    )
    return jax.shard_map(
        on_device,
        mesh=mesh,
        in_specs=placed,
        out_specs=P(("groups", "tensor"), "adapter"),
        check_vma=False,
    )
```

```python
import functools

import jax
import jax.numpy as jnp
from jax import lax
from jax.experimental import pallas as pl
from jax.experimental.pallas import tpu as pltpu
from jax.sharding import PartitionSpec as P

adapter_scale = 0.5
lane = 128
f32 = jnp.float32
bf16 = jnp.bfloat16


def general(
    tokens,
    base_up_weight,
    adapter_shrink_weight,
    adapter_expand_weight,
    row_adapter_index,
    adapter_slot_index,
):
    owner_count = lax.axis_size("adapter")
    owner_index = lax.axis_index("adapter")
    tensor_index = lax.axis_index("tensor")
    rank_block = adapter_expand_weight.shape[1]
    columns = base_up_weight.shape[1]
    slot = jnp.take(adapter_slot_index, row_adapter_index[:, 0], axis=0)
    rows = lax.all_gather(tokens, "adapter", axis=0, tiled=True)
    expand = adapter_expand_weight[0].reshape(rank_block, owner_count, columns)
    expand = lax.all_to_all(expand, "adapter", split_axis=1, concat_axis=1, tiled=True)
    shrunk = jnp.dot(rows, adapter_shrink_weight[0], preferred_element_type=f32)
    shrunk = jnp.where((slot == owner_index)[:, None], shrunk, 0.0)
    shrunk = lax.psum(shrunk, ("adapter", "tensor"))
    shrunk = (adapter_scale * shrunk).astype(bf16)
    shrunk = lax.dynamic_slice_in_dim(shrunk, tensor_index * rank_block, rank_block, 1)
    chosen = slot[:, None] == jnp.arange(owner_count, dtype=jnp.int32)[None, :]
    spread = jnp.where(chosen[:, None, :], shrunk[:, :, None], jnp.zeros((), bf16))
    total = jnp.dot(rows, base_up_weight, preferred_element_type=f32)
    total = total + jnp.dot(
        spread.reshape(-1, rank_block * owner_count),
        expand.reshape(rank_block * owner_count, columns),
        preferred_element_type=f32,
    )
    return lax.psum_scatter(total, "tensor", scatter_dimension=0, tiled=True).astype(bf16)


vmem = pl.BlockSpec(memory_space=pltpu.VMEM)
anywhere = pl.BlockSpec(memory_space=pl.ANY)


def kernel_call(kernel, name, flops, moved, mib, **specs):
    return pl.pallas_call(
        kernel,
        cost_estimate=pl.CostEstimate(flops=flops, bytes_accessed=moved, transcendentals=0),
        compiler_params=pltpu.CompilerParams(vmem_limit_bytes=mib << 20),
        name=name,
        **specs,
    )


def cut_kernel(owner_count, offsets, far_width, start_of, block, small_count, expand, weight, *refs):
    small, refs = refs[:small_count], refs[small_count:]
    *pieces, own = refs[: owner_count]
    *loaded, held, sem, held_sem = refs[owner_count:]
    g, a = lax.axis_index("groups"), lax.axis_index("adapter")
    near_width = pieces[0].shape[1]
    columns = near_width + far_width
    start = pl.multiple_of(a * columns, lane)
    copies = [
        pltpu.make_async_copy(expand.at[0, :, pl.ds(start, columns)], own, sem.at[len(pieces)])
    ]
    for n, (j, piece) in enumerate(zip(offsets, pieces)):
        to = lax.rem(a - j + owner_count, owner_count)
        start = pl.multiple_of(to * columns + g * far_width, lane)
        copies.append(
            pltpu.make_async_copy(expand.at[0, :, pl.ds(start, near_width)], piece, sem.at[n])
        )
    for n, (source, target) in enumerate(zip(small, loaded)):
        copies.append(pltpu.make_async_copy(source, target, sem.at[owner_count + n]))
    for bands in weight_copies(start_of(), block, weight, held, held_sem):
        copies += bands
    for copy in copies:
        copy.start()
    for copy in copies:
        copy.wait()


def weight_copies(start, block, weight, target, sem):
    band_count = sem.shape[1]
    band = weight.shape[0] // band_count
    blocks = []
    for n in range(target.shape[0]):
        span = pl.ds(pl.multiple_of(start + n * block, lane), block)
        bands = []
        for m in range(band_count):
            rows = pl.ds(m * band, band)
            bands.append(
                pltpu.make_async_copy(
                    weight.at[rows, span], target.at[n, rows], sem.at[n, m]
                )
            )
        blocks.append(bands)
    return blocks


def gather_kernel(offsets, slots, index, *refs):
    owner_count = len(offsets)
    blocks = refs[:owner_count]
    shrink, rows_out, keep, send, slot_out, rows, partial = refs[owner_count:]
    a, t = lax.axis_index("adapter"), lax.axis_index("tensor")
    height, depth = blocks[0].shape
    for j, part in zip(offsets, blocks):
        where = lax.rem(a + j, owner_count)
        rows[pl.ds(pl.multiple_of(where * height, height), height), :] = part[:, :depth]
    quarter = rows.shape[0] // 4
    for i, flip in enumerate((0, 2, 1, 3)):
        start = pl.multiple_of(lax.bitwise_xor(t, flip) * quarter, quarter)
        rows_out[i * quarter : (i + 1) * quarter, :] = rows[pl.ds(start, quarter), :]
    product = lax.dot_general(
        shrink[...], rows[...], (((1,), (1,)), ((), ())), preferred_element_type=f32
    )
    named, table = index[...], slots[...]
    slot = jnp.zeros_like(named)
    for k in range(table.shape[1]):
        slot = jnp.where(named == k, table[:, k : k + 1], slot)
    slot_out[...] = slot
    partial[...] = jnp.where(slot == a, product, 0.0)
    rank_block = partial.shape[0] // 4
    for i, flip in enumerate((0, 2, 1, 3)):
        start = pl.multiple_of(lax.bitwise_xor(t, flip) * rank_block, rank_block)
        target = keep if i < 2 else send
        at = i % 2 * rank_block
        target[at : at + rank_block, :] = partial[pl.ds(start, rank_block), :]


def part_start(near_width, far_width, is_far, first):
    g = lax.axis_index("groups")
    return ((1 - g) * near_width if is_far else g * far_width) + first


def base_kernel(next_start_of, block, rows, weight, held, *refs):
    copies = []
    if next_start_of is None:
        total = refs[-1]
    else:
        total, ahead, sem = refs[-3:]
        for bands in weight_copies(next_start_of(), block, weight, ahead, sem):
            copies += bands
    for copy in copies:
        copy.start()
    for n in range(held.shape[0]):
        total[:, n * block : (n + 1) * block] = jnp.dot(
            rows[...], held[n], preferred_element_type=f32
        )
    for copy in copies:
        copy.wait()


def forward_kernel(far_width, *refs):
    *near, packed = refs
    height, near_width = near[-1].shape
    start = pl.multiple_of(lax.axis_index("groups") * (near_width - far_width), lane)
    for n, piece in enumerate(near):
        skip = piece.shape[1] - near_width
        packed[n * height : (n + 1) * height, :] = piece[:, pl.ds(start + skip, far_width)]


def delta_kernel(owner_count, offsets, start_of, block, base_count, piece_count, slot, *refs):
    bases, refs = refs[:base_count], refs[base_count:]
    own, shrunk = refs[:2]
    pieces = refs[2 : 2 + piece_count]
    width = sum(base.shape[1] for base in bases)
    *outs, flat, ordered = refs[-6:]
    a, t = lax.axis_index("adapter"), lax.axis_index("tensor")
    row_count = bases[0].shape[0]
    quarter = row_count // 4
    slot = slot[...]
    merged = shrunk[...].astype(f32)
    spread = [
        jnp.where(slot == lax.rem(a + j, owner_count), merged, 0.0) for j in (0, *offsets)
    ]
    flat[...] = jnp.concatenate(spread, axis=0).T
    for i, turn in enumerate((0, 2, 1, 3)):
        start = pl.multiple_of(lax.bitwise_xor(t, turn) * quarter, quarter)
        ordered[i * quarter : (i + 1) * quarter, :] = flat[pl.ds(start, quarter), :].astype(bf16)
    left = ordered[...]
    at = 0
    for base in bases:
        for column in range(0, base.shape[1], block):
            source = pl.multiple_of(start_of() + at, lane)
            expand = jnp.concatenate(
                [own[:, pl.ds(source, block)]]
                + [piece[:, pl.ds(piece.shape[1] - width + at, block)] for piece in pieces],
                axis=0,
            )
            total = base[:, column : column + block] + jnp.dot(
                left, expand, preferred_element_type=f32
            )
            for n, out in enumerate(outs):
                out[:, at : at + block] = total[n * quarter : (n + 1) * quarter]
            at += block


def column_block(width):
    for size in (512, 256, 128):
        if width % size == 0:
            return size


def paired(
    tokens,
    base_up_weight,
    adapter_shrink_weight,
    adapter_expand_weight,
    row_adapter_index,
    adapter_slot_index,
):
    owner_count = lax.axis_size("adapter")
    g = lax.axis_index("groups")
    height, depth = tokens.shape
    row_count = height * owner_count
    columns = base_up_weight.shape[1]
    rank_block = adapter_expand_weight.shape[1]
    rank = adapter_shrink_weight.shape[2]
    block = column_block(columns)
    block_count = columns // block
    near_count = max(1, block_count * 8 // 14)
    near_width = near_count * block
    far_width = columns - near_width

    def from_owner(x, j):
        return lax.ppermute(x, "adapter", [(s, (s - j) % owner_count) for s in range(owner_count)])

    def from_tensor(x, m):
        return lax.ppermute(x, "tensor", [(s, s ^ m) for s in range(4)])

    def from_mirror(x, m):
        return lax.ppermute(x, "adapter", [(s, s ^ m) for s in range(owner_count)])

    def from_group(x):
        return lax.ppermute(x, "groups", [(0, 1), (1, 0)])

    weight = pltpu.with_memory_space_constraint(base_up_weight, pltpu.HBM)
    expand = pltpu.with_memory_space_constraint(adapter_expand_weight, pltpu.HBM)
    offsets = (2, 1, 3)
    blocks = [from_owner(tokens, j) for j in offsets]

    def split(count):
        return [(0, count - count // 2), (count - count // 2, count // 2)]

    parts = [(False, *span) for span in split(near_count)]
    parts += [(True, *span) for span in split(block_count - near_count)]
    starts = [
        functools.partial(part_start, near_width, far_width, is_far, first * block)
        for is_far, first, _ in parts
    ]
    bands = 4
    small = [
        pltpu.with_memory_space_constraint(x, pltpu.HBM)
        for x in (
            adapter_slot_index.reshape(1, owner_count),
            row_adapter_index.reshape(1, row_count),
            tokens,
            adapter_shrink_weight[0].T,
        )
    ]
    cut = kernel_call(
        functools.partial(
            cut_kernel, owner_count, offsets, far_width, starts[0], block, len(small)
        ),
        "cut_expand",
        1,
        1,
        1,
        in_specs=[anywhere] * (2 + len(small)),
        out_specs=[vmem] * (owner_count + len(small) + 1),
        out_shape=[pltpu.VMEM((rank_block, near_width), bf16)] * (owner_count - 1)
        + [pltpu.VMEM((rank_block, columns), bf16)]
        + [pltpu.VMEM(x.shape, x.dtype) for x in small]
        + [pltpu.VMEM((parts[0][2], depth, block), bf16)],
        scratch_shapes=[
            pltpu.SemaphoreType.DMA((owner_count + len(small),)),
            pltpu.SemaphoreType.DMA((parts[0][2], bands)),
        ],
    )(expand, weight, *small)
    pieces, own = cut[: owner_count - 1], cut[owner_count - 1]
    slots, index, mine, shrink, held = cut[owner_count:]
    near = [from_owner(piece, j) for piece, j in zip(pieces, offsets)]

    rows, keep, send, slot = kernel_call(
        functools.partial(gather_kernel, (0, *offsets)),
        "gather_rows",
        1,
        1,
        4,
        in_specs=[vmem] * (owner_count + 3),
        out_specs=[vmem] * 4,
        out_shape=[jax.ShapeDtypeStruct((row_count, depth), bf16)]
        + [jax.ShapeDtypeStruct((rank // 2, row_count), f32)] * 2
        + [jax.ShapeDtypeStruct((1, row_count), jnp.int32)],
        scratch_shapes=[pltpu.VMEM((row_count, depth), bf16), pltpu.VMEM((rank, row_count), f32)],
    )(
        slots,
        index,
        mine,
        *blocks,
        shrink,
    )

    def base_part(n, held, *after):
        is_far, _, count = parts[n]
        ahead, next_start_of = [], None
        if n + 1 < len(parts):
            ahead = [pltpu.VMEM((parts[n + 1][2], depth, block), bf16)]
            next_start_of = starts[n + 1]
        return kernel_call(
            functools.partial(base_kernel, next_start_of, block),
            "base_part",
            1 if is_far else 2 * row_count * depth * count * block,
            1 if is_far else 2 * depth * count * block,
            4,
            in_specs=[vmem, anywhere, vmem] + [anywhere] * len(after),
            out_specs=[vmem] * (1 + len(ahead)),
            out_shape=[jax.ShapeDtypeStruct((row_count, count * block), f32)] + ahead,
            scratch_shapes=[pltpu.SemaphoreType.DMA((x.shape[0], bands)) for x in ahead],
        )(rows, weight, held, *after)

    def delta_part(is_far, bases, pieces):
        start_of = functools.partial(part_start, near_width, far_width, is_far, 0)
        width = sum(base.shape[1] for base in bases)
        return kernel_call(
            functools.partial(
                delta_kernel, owner_count, offsets, start_of, block, len(bases), len(pieces)
            ),
            "delta_part",
            1,
            1,
            8,
            in_specs=[vmem] * (3 + len(bases) + len(pieces)),
            out_specs=[vmem] * 4,
            out_shape=[jax.ShapeDtypeStruct((row_count // 4, width), f32)] * 4,
            scratch_shapes=[
                pltpu.VMEM((row_count, rank_block * owner_count), f32),
                pltpu.VMEM((row_count, rank_block * owner_count), bf16),
            ],
        )(slot, *bases, own, shrunk, *pieces)

    arrived = from_tensor(send, 1)
    base_0, held = base_part(0, held, send)
    arrived, base_0 = lax.optimization_barrier((arrived, base_0))
    pair = keep + arrived
    arrived = from_tensor(pair[rank_block:], 2)
    base_1, held = base_part(1, held, pair)
    arrived, base_1, *near = lax.optimization_barrier((arrived, base_1, *near))
    shrunk = (adapter_scale * (pair[:rank_block] + arrived)).astype(bf16)
    packed = kernel_call(
        functools.partial(forward_kernel, far_width),
        "pack_far",
        1,
        1,
        2,
        in_specs=[vmem] * (owner_count - 1),
        out_specs=vmem,
        out_shape=jax.ShapeDtypeStruct(((owner_count - 1) * rank_block, far_width), bf16),
    )(*near)
    far = from_group(packed)
    steps = []
    m = 1
    while m < owner_count:
        steps.append(m)
        m *= 2
    base_far, held = [], [held]
    for m, n in zip(steps, (2, 3)):
        arrived = from_mirror(shrunk, m)
        base, *held = base_part(n, *held, shrunk, packed)
        arrived, base = lax.optimization_barrier((arrived, base))
        base_far.append(base)
        shrunk = shrunk + arrived

    halves = []
    for is_far, bases, pieces in ((False, [base_0, base_1], near), (True, base_far, [far])):
        own_keep, cross_keep, own_send, cross_send = delta_part(is_far, bases, pieces)
        cross = (cross_keep + from_tensor(cross_send, 1)).astype(bf16)
        kept = own_keep + from_tensor(own_send, 1)
        crossed = from_tensor(cross, 2)
        halves.append((kept + crossed.astype(f32)).astype(bf16))
    first = jnp.concatenate(halves, axis=1)
    second = jnp.concatenate(halves[::-1], axis=1)
    return jnp.where(g == 0, first, second)


def on_device(tokens, base_up_weight, adapter_shrink_weight, adapter_expand_weight, *index):
    pairs = lax.axis_size("groups") == 2 and lax.axis_size("tensor") == 4
    few = lax.axis_size("adapter") == 4
    even = base_up_weight.shape[1] % (2 * lane) == 0 and tokens.shape[0] % 16 == 0
    arrange = paired if pairs and few and even else general
    return arrange(
        tokens, base_up_weight, adapter_shrink_weight, adapter_expand_weight, *index
    )


def solution(mesh):
    placed = (
        P(("groups", "adapter"), "tensor"),
        P("tensor", "adapter"),
        P("adapter", "tensor", None),
        P("adapter", "tensor", None),
        P("groups", None),
        P(),
    )
    return jax.shard_map(
        on_device,
        mesh=mesh,
        in_specs=placed,
        out_specs=P(("groups", "tensor"), "adapter"),
        check_vma=False,
    )
```

```python
import functools

import jax
import jax.numpy as jnp
from jax import lax
from jax.experimental import pallas as pl
from jax.experimental.pallas import tpu as pltpu
from jax.sharding import PartitionSpec as P

adapter_scale = 0.5
lane = 128
f32 = jnp.float32
bf16 = jnp.bfloat16


def general(
    tokens,
    base_up_weight,
    adapter_shrink_weight,
    adapter_expand_weight,
    row_adapter_index,
    adapter_slot_index,
):
    owner_count = lax.axis_size("adapter")
    owner_index = lax.axis_index("adapter")
    tensor_index = lax.axis_index("tensor")
    rank_block = adapter_expand_weight.shape[1]
    columns = base_up_weight.shape[1]
    slot = jnp.take(adapter_slot_index, row_adapter_index[:, 0], axis=0)
    rows = lax.all_gather(tokens, "adapter", axis=0, tiled=True)
    expand = adapter_expand_weight[0].reshape(rank_block, owner_count, columns)
    expand = lax.all_to_all(expand, "adapter", split_axis=1, concat_axis=1, tiled=True)
    shrunk = jnp.dot(rows, adapter_shrink_weight[0], preferred_element_type=f32)
    shrunk = jnp.where((slot == owner_index)[:, None], shrunk, 0.0)
    shrunk = lax.psum(shrunk, ("adapter", "tensor"))
    shrunk = (adapter_scale * shrunk).astype(bf16)
    shrunk = lax.dynamic_slice_in_dim(shrunk, tensor_index * rank_block, rank_block, 1)
    chosen = slot[:, None] == jnp.arange(owner_count, dtype=jnp.int32)[None, :]
    spread = jnp.where(chosen[:, None, :], shrunk[:, :, None], jnp.zeros((), bf16))
    total = jnp.dot(rows, base_up_weight, preferred_element_type=f32)
    total = total + jnp.dot(
        spread.reshape(-1, rank_block * owner_count),
        expand.reshape(rank_block * owner_count, columns),
        preferred_element_type=f32,
    )
    return lax.psum_scatter(total, "tensor", scatter_dimension=0, tiled=True).astype(bf16)


vmem = pl.BlockSpec(memory_space=pltpu.VMEM)
anywhere = pl.BlockSpec(memory_space=pl.ANY)


def kernel_call(kernel, name, flops, moved, mib, **specs):
    return pl.pallas_call(
        kernel,
        cost_estimate=pl.CostEstimate(flops=flops, bytes_accessed=moved, transcendentals=0),
        compiler_params=pltpu.CompilerParams(vmem_limit_bytes=mib << 20),
        name=name,
        **specs,
    )


def cut_kernel(owner_count, offsets, far_width, start_of, block, small_count, expand, weight, *refs):
    small, refs = refs[:small_count], refs[small_count:]
    *pieces, own = refs[: owner_count]
    *loaded, held, sem, held_sem = refs[owner_count:]
    g, a = lax.axis_index("groups"), lax.axis_index("adapter")
    near_width = pieces[0].shape[1]
    columns = near_width + far_width
    start = pl.multiple_of(a * columns, lane)
    copies = [
        pltpu.make_async_copy(expand.at[0, :, pl.ds(start, columns)], own, sem.at[len(pieces)])
    ]
    for n, (j, piece) in enumerate(zip(offsets, pieces)):
        to = lax.rem(a - j + owner_count, owner_count)
        start = pl.multiple_of(to * columns + g * far_width, lane)
        copies.append(
            pltpu.make_async_copy(expand.at[0, :, pl.ds(start, near_width)], piece, sem.at[n])
        )
    for n, (source, target) in enumerate(zip(small, loaded)):
        copies.append(pltpu.make_async_copy(source, target, sem.at[owner_count + n]))
    for bands in weight_copies(start_of(), block, weight, held, held_sem):
        copies += bands
    for copy in copies:
        copy.start()
    for copy in copies:
        copy.wait()


def weight_copies(start, block, weight, target, sem):
    band_count = sem.shape[1]
    band = weight.shape[0] // band_count
    blocks = []
    for n in range(target.shape[0]):
        span = pl.ds(pl.multiple_of(start + n * block, lane), block)
        bands = []
        for m in range(band_count):
            rows = pl.ds(m * band, band)
            bands.append(
                pltpu.make_async_copy(
                    weight.at[rows, span], target.at[n, rows], sem.at[n, m]
                )
            )
        blocks.append(bands)
    return blocks


def gather_kernel(offsets, slots, index, *refs):
    owner_count = len(offsets)
    blocks = refs[:owner_count]
    shrink, rows_out, keep, send, slot_out, rows, partial = refs[owner_count:]
    a, t = lax.axis_index("adapter"), lax.axis_index("tensor")
    height, depth = blocks[0].shape
    for j, part in zip(offsets, blocks):
        where = lax.rem(a + j, owner_count)
        rows[pl.ds(pl.multiple_of(where * height, height), height), :] = part[:, :depth]
    quarter = rows.shape[0] // 4
    for i, flip in enumerate((0, 2, 1, 3)):
        start = pl.multiple_of(lax.bitwise_xor(t, flip) * quarter, quarter)
        rows_out[i * quarter : (i + 1) * quarter, :] = rows[pl.ds(start, quarter), :]
    product = lax.dot_general(
        shrink[...], rows[...], (((1,), (1,)), ((), ())), preferred_element_type=f32
    )
    named, table = index[...], slots[...]
    slot = jnp.zeros_like(named)
    for k in range(table.shape[1]):
        slot = jnp.where(named == k, table[:, k : k + 1], slot)
    slot_out[...] = slot
    partial[...] = jnp.where(slot == a, product, 0.0)
    rank_block = partial.shape[0] // 4
    for i, flip in enumerate((0, 2, 1, 3)):
        start = pl.multiple_of(lax.bitwise_xor(t, flip) * rank_block, rank_block)
        target = keep if i < 2 else send
        at = i % 2 * rank_block
        target[at : at + rank_block, :] = partial[pl.ds(start, rank_block), :]


def part_start(near_width, far_width, is_far, first):
    g = lax.axis_index("groups")
    return ((1 - g) * near_width if is_far else g * far_width) + first


def base_kernel(next_start_of, block, rows, weight, held, *refs):
    copies = []
    if next_start_of is None:
        total = refs[-1]
    else:
        total, ahead, sem = refs[-3:]
        for bands in weight_copies(next_start_of(), block, weight, ahead, sem):
            copies += bands
    for copy in copies:
        copy.start()

    @pl.when(lax.axis_index("tensor") >= 0)
    def _():
        for n in range(held.shape[0]):
            total[:, n * block : (n + 1) * block] = jnp.dot(
                rows[...], held[n], preferred_element_type=f32
            )

    for copy in copies:
        copy.wait()


def forward_kernel(far_width, *refs):
    *near, packed = refs
    height, near_width = near[-1].shape
    start = pl.multiple_of(lax.axis_index("groups") * (near_width - far_width), lane)
    for n, piece in enumerate(near):
        skip = piece.shape[1] - near_width
        packed[n * height : (n + 1) * height, :] = piece[:, pl.ds(start + skip, far_width)]


def delta_kernel(owner_count, offsets, start_of, block, base_count, piece_count, slot, *refs):
    bases, refs = refs[:base_count], refs[base_count:]
    own, shrunk = refs[:2]
    pieces = refs[2 : 2 + piece_count]
    width = sum(base.shape[1] for base in bases)
    *outs, flat, ordered = refs[-6:]
    a, t = lax.axis_index("adapter"), lax.axis_index("tensor")
    row_count = bases[0].shape[0]
    quarter = row_count // 4
    slot = slot[...]
    merged = shrunk[...].astype(f32)
    spread = [
        jnp.where(slot == lax.rem(a + j, owner_count), merged, 0.0) for j in (0, *offsets)
    ]
    flat[...] = jnp.concatenate(spread, axis=0).T
    for i, turn in enumerate((0, 2, 1, 3)):
        start = pl.multiple_of(lax.bitwise_xor(t, turn) * quarter, quarter)
        ordered[i * quarter : (i + 1) * quarter, :] = flat[pl.ds(start, quarter), :].astype(bf16)
    left = ordered[...]
    at = 0
    for base in bases:
        for column in range(0, base.shape[1], block):
            source = pl.multiple_of(start_of() + at, lane)
            expand = jnp.concatenate(
                [own[:, pl.ds(source, block)]]
                + [piece[:, pl.ds(piece.shape[1] - width + at, block)] for piece in pieces],
                axis=0,
            )
            total = base[:, column : column + block] + jnp.dot(
                left, expand, preferred_element_type=f32
            )
            for n, out in enumerate(outs):
                out[:, at : at + block] = total[n * quarter : (n + 1) * quarter]
            at += block


def column_block(width):
    for size in (512, 256, 128):
        if width % size == 0:
            return size


def paired(
    tokens,
    base_up_weight,
    adapter_shrink_weight,
    adapter_expand_weight,
    row_adapter_index,
    adapter_slot_index,
):
    owner_count = lax.axis_size("adapter")
    g = lax.axis_index("groups")
    height, depth = tokens.shape
    row_count = height * owner_count
    columns = base_up_weight.shape[1]
    rank_block = adapter_expand_weight.shape[1]
    rank = adapter_shrink_weight.shape[2]
    block = column_block(columns)
    block_count = columns // block
    near_count = max(1, block_count * 8 // 14)
    near_width = near_count * block
    far_width = columns - near_width

    def from_owner(x, j):
        return lax.ppermute(x, "adapter", [(s, (s - j) % owner_count) for s in range(owner_count)])

    def from_tensor(x, m):
        return lax.ppermute(x, "tensor", [(s, s ^ m) for s in range(4)])

    def from_mirror(x, m):
        return lax.ppermute(x, "adapter", [(s, s ^ m) for s in range(owner_count)])

    def from_group(x):
        return lax.ppermute(x, "groups", [(0, 1), (1, 0)])

    weight = pltpu.with_memory_space_constraint(base_up_weight, pltpu.HBM)
    expand = pltpu.with_memory_space_constraint(adapter_expand_weight, pltpu.HBM)
    offsets = (2, 1, 3)
    blocks = [from_owner(tokens, j) for j in offsets]

    def split(count):
        return [(0, count - count // 2), (count - count // 2, count // 2)]

    parts = [(False, *span) for span in split(near_count)]
    parts += [(True, *span) for span in split(block_count - near_count)]
    starts = [
        functools.partial(part_start, near_width, far_width, is_far, first * block)
        for is_far, first, _ in parts
    ]
    bands = 4
    small = [
        pltpu.with_memory_space_constraint(x, pltpu.HBM)
        for x in (
            adapter_slot_index.reshape(1, owner_count),
            row_adapter_index.reshape(1, row_count),
            tokens,
            adapter_shrink_weight[0].T,
        )
    ]
    cut = kernel_call(
        functools.partial(
            cut_kernel, owner_count, offsets, far_width, starts[0], block, len(small)
        ),
        "cut_expand",
        1,
        1,
        1,
        in_specs=[anywhere] * (2 + len(small)),
        out_specs=[vmem] * (owner_count + len(small) + 1),
        out_shape=[pltpu.VMEM((rank_block, near_width), bf16)] * (owner_count - 1)
        + [pltpu.VMEM((rank_block, columns), bf16)]
        + [pltpu.VMEM(x.shape, x.dtype) for x in small]
        + [pltpu.VMEM((parts[0][2], depth, block), bf16)],
        scratch_shapes=[
            pltpu.SemaphoreType.DMA((owner_count + len(small),)),
            pltpu.SemaphoreType.DMA((parts[0][2], bands)),
        ],
    )(expand, weight, *small)
    pieces, own = cut[: owner_count - 1], cut[owner_count - 1]
    slots, index, mine, shrink, held = cut[owner_count:]
    near = [from_owner(piece, j) for piece, j in zip(pieces, offsets)]

    rows, keep, send, slot = kernel_call(
        functools.partial(gather_kernel, (0, *offsets)),
        "gather_rows",
        1,
        1,
        4,
        in_specs=[vmem] * (owner_count + 3),
        out_specs=[vmem] * 4,
        out_shape=[jax.ShapeDtypeStruct((row_count, depth), bf16)]
        + [jax.ShapeDtypeStruct((rank // 2, row_count), f32)] * 2
        + [jax.ShapeDtypeStruct((1, row_count), jnp.int32)],
        scratch_shapes=[pltpu.VMEM((row_count, depth), bf16), pltpu.VMEM((rank, row_count), f32)],
    )(
        slots,
        index,
        mine,
        *blocks,
        shrink,
    )

    def base_part(n, held, *after):
        is_far, _, count = parts[n]
        ahead, next_start_of = [], None
        if n + 1 < len(parts):
            ahead = [pltpu.VMEM((parts[n + 1][2], depth, block), bf16)]
            next_start_of = starts[n + 1]
        return kernel_call(
            functools.partial(base_kernel, next_start_of, block),
            "base_part",
            1 if is_far else 2 * row_count * depth * count * block,
            1 if is_far else 2 * depth * count * block,
            4,
            in_specs=[vmem, anywhere, vmem] + [anywhere] * len(after),
            out_specs=[vmem] * (1 + len(ahead)),
            out_shape=[jax.ShapeDtypeStruct((row_count, count * block), f32)] + ahead,
            scratch_shapes=[pltpu.SemaphoreType.DMA((x.shape[0], bands)) for x in ahead],
        )(rows, weight, held, *after)

    def delta_part(is_far, bases, pieces):
        start_of = functools.partial(part_start, near_width, far_width, is_far, 0)
        width = sum(base.shape[1] for base in bases)
        return kernel_call(
            functools.partial(
                delta_kernel, owner_count, offsets, start_of, block, len(bases), len(pieces)
            ),
            "delta_part",
            1,
            1,
            8,
            in_specs=[vmem] * (3 + len(bases) + len(pieces)),
            out_specs=[vmem] * 4,
            out_shape=[jax.ShapeDtypeStruct((row_count // 4, width), f32)] * 4,
            scratch_shapes=[
                pltpu.VMEM((row_count, rank_block * owner_count), f32),
                pltpu.VMEM((row_count, rank_block * owner_count), bf16),
            ],
        )(slot, *bases, own, shrunk, *pieces)

    arrived = from_tensor(send, 1)
    base_0, held = base_part(0, held, send)
    arrived, base_0 = lax.optimization_barrier((arrived, base_0))
    pair = keep + arrived
    arrived = from_tensor(pair[rank_block:], 2)
    base_1, held = base_part(1, held, pair)
    arrived, base_1, *near = lax.optimization_barrier((arrived, base_1, *near))
    shrunk = (adapter_scale * (pair[:rank_block] + arrived)).astype(bf16)
    packed = kernel_call(
        functools.partial(forward_kernel, far_width),
        "pack_far",
        1,
        1,
        2,
        in_specs=[vmem] * (owner_count - 1),
        out_specs=vmem,
        out_shape=jax.ShapeDtypeStruct(((owner_count - 1) * rank_block, far_width), bf16),
    )(*near)
    far = from_group(packed)
    steps = []
    m = 1
    while m < owner_count:
        steps.append(m)
        m *= 2
    base_far, held = [], [held]
    for m, n in zip(steps, (2, 3)):
        arrived = from_mirror(shrunk, m)
        base, *held = base_part(n, *held, shrunk, packed)
        arrived, base = lax.optimization_barrier((arrived, base))
        base_far.append(base)
        shrunk = shrunk + arrived

    halves = []
    for is_far, bases, pieces in ((False, [base_0, base_1], near), (True, base_far, [far])):
        own_keep, cross_keep, own_send, cross_send = delta_part(is_far, bases, pieces)
        cross = (cross_keep + from_tensor(cross_send, 1)).astype(bf16)
        kept = own_keep + from_tensor(own_send, 1)
        crossed = from_tensor(cross, 2)
        halves.append((kept + crossed.astype(f32)).astype(bf16))
    first = jnp.concatenate(halves, axis=1)
    second = jnp.concatenate(halves[::-1], axis=1)
    return jnp.where(g == 0, first, second)


def on_device(tokens, base_up_weight, adapter_shrink_weight, adapter_expand_weight, *index):
    pairs = lax.axis_size("groups") == 2 and lax.axis_size("tensor") == 4
    few = lax.axis_size("adapter") == 4
    even = base_up_weight.shape[1] % (2 * lane) == 0 and tokens.shape[0] % 16 == 0
    arrange = paired if pairs and few and even else general
    return arrange(
        tokens, base_up_weight, adapter_shrink_weight, adapter_expand_weight, *index
    )


def solution(mesh):
    placed = (
        P(("groups", "adapter"), "tensor"),
        P("tensor", "adapter"),
        P("adapter", "tensor", None),
        P("adapter", "tensor", None),
        P("groups", None),
        P(),
    )
    return jax.shard_map(
        on_device,
        mesh=mesh,
        in_specs=placed,
        out_specs=P(("groups", "tensor"), "adapter"),
        check_vma=False,
    )
```

```python
import functools

import jax
import jax.numpy as jnp
from jax import lax
from jax.experimental import pallas as pl
from jax.experimental.pallas import tpu as pltpu
from jax.sharding import PartitionSpec as P

adapter_scale = 0.5
lane = 128
f32 = jnp.float32
bf16 = jnp.bfloat16


def general(
    tokens,
    base_up_weight,
    adapter_shrink_weight,
    adapter_expand_weight,
    row_adapter_index,
    adapter_slot_index,
):
    owner_count = lax.axis_size("adapter")
    owner_index = lax.axis_index("adapter")
    tensor_index = lax.axis_index("tensor")
    rank_block = adapter_expand_weight.shape[1]
    columns = base_up_weight.shape[1]
    slot = jnp.take(adapter_slot_index, row_adapter_index[:, 0], axis=0)
    rows = lax.all_gather(tokens, "adapter", axis=0, tiled=True)
    expand = adapter_expand_weight[0].reshape(rank_block, owner_count, columns)
    expand = lax.all_to_all(expand, "adapter", split_axis=1, concat_axis=1, tiled=True)
    shrunk = jnp.dot(rows, adapter_shrink_weight[0], preferred_element_type=f32)
    shrunk = jnp.where((slot == owner_index)[:, None], shrunk, 0.0)
    shrunk = lax.psum(shrunk, ("adapter", "tensor"))
    shrunk = (adapter_scale * shrunk).astype(bf16)
    shrunk = lax.dynamic_slice_in_dim(shrunk, tensor_index * rank_block, rank_block, 1)
    chosen = slot[:, None] == jnp.arange(owner_count, dtype=jnp.int32)[None, :]
    spread = jnp.where(chosen[:, None, :], shrunk[:, :, None], jnp.zeros((), bf16))
    total = jnp.dot(rows, base_up_weight, preferred_element_type=f32)
    total = total + jnp.dot(
        spread.reshape(-1, rank_block * owner_count),
        expand.reshape(rank_block * owner_count, columns),
        preferred_element_type=f32,
    )
    return lax.psum_scatter(total, "tensor", scatter_dimension=0, tiled=True).astype(bf16)


vmem = pl.BlockSpec(memory_space=pltpu.VMEM)
anywhere = pl.BlockSpec(memory_space=pl.ANY)


def kernel_call(kernel, name, flops, moved, mib, **specs):
    return pl.pallas_call(
        kernel,
        cost_estimate=pl.CostEstimate(flops=flops, bytes_accessed=moved, transcendentals=0),
        compiler_params=pltpu.CompilerParams(vmem_limit_bytes=mib << 20),
        name=name,
        **specs,
    )


def cut_kernel(
    owner_count, offsets, far_width, start_of, block, numbers, small_count, expand, weight, *refs
):
    small, refs = refs[:small_count], refs[small_count:]
    *pieces, own = refs[: owner_count]
    *loaded, held, sem, held_sem = refs[owner_count:]
    g, a = lax.axis_index("groups"), lax.axis_index("adapter")
    near_width = pieces[0].shape[1]
    columns = near_width + far_width
    start = pl.multiple_of(a * columns, lane)
    copies = [
        pltpu.make_async_copy(expand.at[0, :, pl.ds(start, columns)], own, sem.at[len(pieces)])
    ]
    for n, (j, piece) in enumerate(zip(offsets, pieces)):
        to = lax.rem(a - j + owner_count, owner_count)
        start = pl.multiple_of(to * columns + g * far_width, lane)
        copies.append(
            pltpu.make_async_copy(expand.at[0, :, pl.ds(start, near_width)], piece, sem.at[n])
        )
    for n, (source, target) in enumerate(zip(small, loaded)):
        copies.append(pltpu.make_async_copy(source, target, sem.at[owner_count + n]))
    copies += weight_copies(start_of, block, numbers, weight, held, held_sem)
    for copy in copies:
        copy.start()
    for copy in copies:
        copy.wait()


def block_start(near_width, far_width, block, number):
    g, at = lax.axis_index("groups"), number * block
    return g * far_width + at if at < near_width else (1 - g) * near_width + at - near_width


def weight_copies(start_of, block, numbers, weight, target, sem):
    band_count = sem.shape[1]
    band = weight.shape[0] // band_count
    copies = []
    for n, number in enumerate(numbers):
        span = pl.ds(pl.multiple_of(start_of(number), lane), block)
        for m in range(band_count):
            rows = pl.ds(m * band, band)
            copies.append(
                pltpu.make_async_copy(weight.at[rows, span], target.at[n, rows], sem.at[n, m])
            )
    return copies


def gather_kernel(offsets, slots, index, *refs):
    owner_count = len(offsets)
    blocks = refs[:owner_count]
    shrink, rows_out, keep, send, slot_out, rows, partial = refs[owner_count:]
    a, t = lax.axis_index("adapter"), lax.axis_index("tensor")
    height, depth = blocks[0].shape
    for j, part in zip(offsets, blocks):
        where = lax.rem(a + j, owner_count)
        rows[pl.ds(pl.multiple_of(where * height, height), height), :] = part[:, :depth]
    quarter = rows.shape[0] // 4
    for i, flip in enumerate((0, 2, 1, 3)):
        start = pl.multiple_of(lax.bitwise_xor(t, flip) * quarter, quarter)
        rows_out[i * quarter : (i + 1) * quarter, :] = rows[pl.ds(start, quarter), :]
    product = lax.dot_general(
        shrink[...], rows[...], (((1,), (1,)), ((), ())), preferred_element_type=f32
    )
    named, table = index[...], slots[...]
    slot = jnp.zeros_like(named)
    for k in range(table.shape[1]):
        slot = jnp.where(named == k, table[:, k : k + 1], slot)
    slot_out[...] = slot
    partial[...] = jnp.where(slot == a, product, 0.0)
    rank_block = partial.shape[0] // 4
    for i, flip in enumerate((0, 2, 1, 3)):
        start = pl.multiple_of(lax.bitwise_xor(t, flip) * rank_block, rank_block)
        target = keep if i < 2 else send
        at = i % 2 * rank_block
        target[at : at + rank_block, :] = partial[pl.ds(start, rank_block), :]


def base_kernel(start_of, block, places, numbers, rows, weight, *refs):
    copies = []
    if numbers:
        total, ahead, sem = refs[-3:]
        copies = weight_copies(start_of, block, numbers, weight, ahead, sem)
    else:
        total = refs[-1]
    for copy in copies:
        copy.start()

    @pl.when(lax.axis_index("tensor") >= 0)
    def _():
        for n, (which, index) in enumerate(places):
            total[:, n * block : (n + 1) * block] = jnp.dot(
                rows[...], refs[which][index], preferred_element_type=f32
            )

    for copy in copies:
        copy.wait()


def forward_kernel(far_width, *refs):
    *near, packed = refs
    height, near_width = near[-1].shape
    start = pl.multiple_of(lax.axis_index("groups") * (near_width - far_width), lane)
    for n, piece in enumerate(near):
        skip = piece.shape[1] - near_width
        packed[n * height : (n + 1) * height, :] = piece[:, pl.ds(start + skip, far_width)]


def delta_kernel(owner_count, offsets, start_of, first, block, base_count, piece_count, slot, *refs):
    bases, refs = refs[:base_count], refs[base_count:]
    own, shrunk = refs[:2]
    pieces = refs[2 : 2 + piece_count]
    width = sum(base.shape[1] for base in bases)
    *outs, flat, ordered = refs[-6:]
    a, t = lax.axis_index("adapter"), lax.axis_index("tensor")
    row_count = bases[0].shape[0]
    quarter = row_count // 4
    slot = slot[...]
    merged = shrunk[...].astype(f32)
    spread = [
        jnp.where(slot == lax.rem(a + j, owner_count), merged, 0.0) for j in (0, *offsets)
    ]
    flat[...] = jnp.concatenate(spread, axis=0).T
    for i, turn in enumerate((0, 2, 1, 3)):
        start = pl.multiple_of(lax.bitwise_xor(t, turn) * quarter, quarter)
        ordered[i * quarter : (i + 1) * quarter, :] = flat[pl.ds(start, quarter), :].astype(bf16)
    left = ordered[...]
    at = 0
    for base in bases:
        for column in range(0, base.shape[1], block):
            source = pl.multiple_of(start_of(first + at // block), lane)
            expand = jnp.concatenate(
                [own[:, pl.ds(source, block)]]
                + [piece[:, pl.ds(piece.shape[1] - width + at, block)] for piece in pieces],
                axis=0,
            )
            total = base[:, column : column + block] + jnp.dot(
                left, expand, preferred_element_type=f32
            )
            for n, out in enumerate(outs):
                out[:, at : at + block] = total[n * quarter : (n + 1) * quarter]
            at += block


def column_block(width):
    for size in (512, 256, 128):
        if width % size == 0:
            return size


def paired(
    tokens,
    base_up_weight,
    adapter_shrink_weight,
    adapter_expand_weight,
    row_adapter_index,
    adapter_slot_index,
):
    owner_count = lax.axis_size("adapter")
    g = lax.axis_index("groups")
    height, depth = tokens.shape
    row_count = height * owner_count
    columns = base_up_weight.shape[1]
    rank_block = adapter_expand_weight.shape[1]
    rank = adapter_shrink_weight.shape[2]
    block = column_block(columns)
    block_count = columns // block
    near_count = max(1, block_count * 8 // 14)
    near_width = near_count * block
    far_width = columns - near_width

    def from_owner(x, j):
        return lax.ppermute(x, "adapter", [(s, (s - j) % owner_count) for s in range(owner_count)])

    def from_tensor(x, m):
        return lax.ppermute(x, "tensor", [(s, s ^ m) for s in range(4)])

    def from_mirror(x, m):
        return lax.ppermute(x, "adapter", [(s, s ^ m) for s in range(owner_count)])

    def from_group(x):
        return lax.ppermute(x, "groups", [(0, 1), (1, 0)])

    weight = pltpu.with_memory_space_constraint(base_up_weight, pltpu.HBM)
    expand = pltpu.with_memory_space_constraint(adapter_expand_weight, pltpu.HBM)
    offsets = (2, 1, 3)

    near_half, far_half = near_count - near_count // 2, (block_count - near_count + 1) // 2
    cuts = (0, near_half, near_count, near_count + far_half, block_count)
    parts = list(zip(cuts[:-1], cuts[1:]))
    loads = (0, min(6, block_count), min(10, block_count), block_count, block_count, block_count)
    start_of = functools.partial(block_start, near_width, far_width, block)
    bands = 4

    small = [
        pltpu.with_memory_space_constraint(x, pltpu.HBM)
        for x in (
            adapter_slot_index.reshape(1, owner_count),
            row_adapter_index.reshape(1, row_count),
            tokens,
            adapter_shrink_weight[0].T,
        )
    ]
    cut = kernel_call(
        functools.partial(
            cut_kernel, owner_count, offsets, far_width, start_of, block, range(loads[1]), len(small)
        ),
        "cut_expand",
        1,
        1,
        1,
        in_specs=[anywhere] * (2 + len(small)),
        out_specs=[vmem] * (owner_count + len(small) + 1),
        out_shape=[pltpu.VMEM((rank_block, near_width), bf16)] * (owner_count - 1)
        + [pltpu.VMEM((rank_block, columns), bf16)]
        + [pltpu.VMEM(x.shape, x.dtype) for x in small]
        + [pltpu.VMEM((loads[1], depth, block), bf16)],
        scratch_shapes=[
            pltpu.SemaphoreType.DMA((owner_count + len(small),)),
            pltpu.SemaphoreType.DMA((loads[1], bands)),
        ],
    )(expand, weight, *small)
    pieces, own = cut[: owner_count - 1], cut[owner_count - 1]
    slots, index, mine, shrink, held = cut[owner_count:]
    blocks = [from_owner(mine, j) for j in offsets]
    loaded = [held]
    near = [from_owner(piece, j) for piece, j in zip(pieces, offsets)]

    rows, keep, send, slot = kernel_call(
        functools.partial(gather_kernel, (0, *offsets)),
        "gather_rows",
        1,
        1,
        4,
        in_specs=[vmem] * (owner_count + 3),
        out_specs=[vmem] * 4,
        out_shape=[jax.ShapeDtypeStruct((row_count, depth), bf16)]
        + [jax.ShapeDtypeStruct((rank // 2, row_count), f32)] * 2
        + [jax.ShapeDtypeStruct((1, row_count), jnp.int32)],
        scratch_shapes=[pltpu.VMEM((row_count, depth), bf16), pltpu.VMEM((rank, row_count), f32)],
    )(
        slots,
        index,
        mine,
        *blocks,
        shrink,
    )

    def base_part(n, *after):
        first, last = parts[n]
        numbers = range(loads[n + 1], loads[n + 2])
        places, used = [], []
        for number in range(first, last):
            source = max(k for k in range(len(loads) - 1) if loads[k] <= number)
            if source not in used:
                used.append(source)
            places.append((used.index(source), number - loads[source]))
        near = first < near_count
        out = kernel_call(
            functools.partial(base_kernel, start_of, block, places, numbers),
            "base_part",
            2 * row_count * depth * (last - first) * block if near else 1,
            2 * depth * (last - first) * block if near else 1,
            4,
            in_specs=[vmem, anywhere] + [vmem] * len(used) + [anywhere] * len(after),
            out_specs=[vmem] * (2 if numbers else 1),
            out_shape=[jax.ShapeDtypeStruct((row_count, (last - first) * block), f32)]
            + ([pltpu.VMEM((len(numbers), depth, block), bf16)] if numbers else []),
            scratch_shapes=[pltpu.SemaphoreType.DMA((len(numbers), bands))] if numbers else [],
        )(rows, weight, *[loaded[k] for k in used], *after)
        loaded.append(out[1] if numbers else None)
        return out[0]

    def delta_part(is_far, bases, pieces):
        first = near_count if is_far else 0
        width = sum(base.shape[1] for base in bases)
        return kernel_call(
            functools.partial(
                delta_kernel, owner_count, offsets, start_of, first, block, len(bases), len(pieces)
            ),
            "delta_part",
            1,
            1,
            8,
            in_specs=[vmem] * (3 + len(bases) + len(pieces)),
            out_specs=[vmem] * 4,
            out_shape=[jax.ShapeDtypeStruct((row_count // 4, width), f32)] * 4,
            scratch_shapes=[
                pltpu.VMEM((row_count, rank_block * owner_count), f32),
                pltpu.VMEM((row_count, rank_block * owner_count), bf16),
            ],
        )(slot, *bases, own, shrunk, *pieces)

    arrived = from_tensor(send, 1)
    base_0 = base_part(0, send)
    arrived, base_0 = lax.optimization_barrier((arrived, base_0))
    pair = keep + arrived
    arrived = from_tensor(pair[rank_block:], 2)
    base_1 = base_part(1, pair)
    arrived, base_1, *near = lax.optimization_barrier((arrived, base_1, *near))
    shrunk = (adapter_scale * (pair[:rank_block] + arrived)).astype(bf16)
    packed = kernel_call(
        functools.partial(forward_kernel, far_width),
        "pack_far",
        1,
        1,
        2,
        in_specs=[vmem] * (owner_count - 1),
        out_specs=vmem,
        out_shape=jax.ShapeDtypeStruct(((owner_count - 1) * rank_block, far_width), bf16),
    )(*near)
    far = from_group(packed)
    steps = []
    m = 1
    while m < owner_count:
        steps.append(m)
        m *= 2
    base_far = []
    for m, n in zip(steps, (2, 3)):
        arrived = from_mirror(shrunk, m)
        base = base_part(n, shrunk, packed)
        arrived, base = lax.optimization_barrier((arrived, base))
        base_far.append(base)
        shrunk = shrunk + arrived

    halves = []
    for is_far, bases, pieces in ((False, [base_0, base_1], near), (True, base_far, [far])):
        own_keep, cross_keep, own_send, cross_send = delta_part(is_far, bases, pieces)
        cross = (cross_keep + from_tensor(cross_send, 1)).astype(bf16)
        kept = own_keep + from_tensor(own_send, 1)
        crossed = from_tensor(cross, 2)
        halves.append((kept + crossed.astype(f32)).astype(bf16))
    first = jnp.concatenate(halves, axis=1)
    second = jnp.concatenate(halves[::-1], axis=1)
    return jnp.where(g == 0, first, second)


def on_device(tokens, base_up_weight, adapter_shrink_weight, adapter_expand_weight, *index):
    pairs = lax.axis_size("groups") == 2 and lax.axis_size("tensor") == 4
    few = lax.axis_size("adapter") == 4
    columns = base_up_weight.shape[1]
    even = columns % 512 == 0 and columns >= 4096 and tokens.shape[0] % 16 == 0
    arrange = paired if pairs and few and even else general
    return arrange(
        tokens, base_up_weight, adapter_shrink_weight, adapter_expand_weight, *index
    )


def solution(mesh):
    placed = (
        P(("groups", "adapter"), "tensor"),
        P("tensor", "adapter"),
        P("adapter", "tensor", None),
        P("adapter", "tensor", None),
        P("groups", None),
        P(),
    )
    return jax.shard_map(
        on_device,
        mesh=mesh,
        in_specs=placed,
        out_specs=P(("groups", "tensor"), "adapter"),
        check_vma=False,
    )
```

```python
import functools

import jax
import jax.numpy as jnp
from jax import lax
from jax.experimental import pallas as pl
from jax.experimental.pallas import tpu as pltpu
from jax.sharding import PartitionSpec as P

adapter_scale = 0.5
lane = 128
f32 = jnp.float32
bf16 = jnp.bfloat16


def general(
    tokens,
    base_up_weight,
    adapter_shrink_weight,
    adapter_expand_weight,
    row_adapter_index,
    adapter_slot_index,
):
    owner_count = lax.axis_size("adapter")
    owner_index = lax.axis_index("adapter")
    tensor_index = lax.axis_index("tensor")
    rank_block = adapter_expand_weight.shape[1]
    columns = base_up_weight.shape[1]
    slot = jnp.take(adapter_slot_index, row_adapter_index[:, 0], axis=0)
    rows = lax.all_gather(tokens, "adapter", axis=0, tiled=True)
    expand = adapter_expand_weight[0].reshape(rank_block, owner_count, columns)
    expand = lax.all_to_all(expand, "adapter", split_axis=1, concat_axis=1, tiled=True)
    shrunk = jnp.dot(rows, adapter_shrink_weight[0], preferred_element_type=f32)
    shrunk = jnp.where((slot == owner_index)[:, None], shrunk, 0.0)
    shrunk = lax.psum(shrunk, ("adapter", "tensor"))
    shrunk = (adapter_scale * shrunk).astype(bf16)
    shrunk = lax.dynamic_slice_in_dim(shrunk, tensor_index * rank_block, rank_block, 1)
    chosen = slot[:, None] == jnp.arange(owner_count, dtype=jnp.int32)[None, :]
    spread = jnp.where(chosen[:, None, :], shrunk[:, :, None], jnp.zeros((), bf16))
    total = jnp.dot(rows, base_up_weight, preferred_element_type=f32)
    total = total + jnp.dot(
        spread.reshape(-1, rank_block * owner_count),
        expand.reshape(rank_block * owner_count, columns),
        preferred_element_type=f32,
    )
    return lax.psum_scatter(total, "tensor", scatter_dimension=0, tiled=True).astype(bf16)


vmem = pl.BlockSpec(memory_space=pltpu.VMEM)
anywhere = pl.BlockSpec(memory_space=pl.ANY)


def kernel_call(kernel, name, flops, moved, mib, **specs):
    return pl.pallas_call(
        kernel,
        cost_estimate=pl.CostEstimate(flops=flops, bytes_accessed=moved, transcendentals=0),
        compiler_params=pltpu.CompilerParams(vmem_limit_bytes=mib << 20),
        name=name,
        **specs,
    )


def cut_kernel(block, numbers, small_count, expand, weight, *refs):
    small, refs = refs[:small_count], refs[small_count:]
    whole, half, own, *loaded, held, sem, held_sem = refs
    g, a = lax.axis_index("groups"), lax.axis_index("adapter")
    columns, half_width = whole.shape[1], half.shape[1]
    firsts = (
        lax.rem(a + 3 - 2 * g, 4) * columns,
        lax.rem(a + 2, 4) * columns + g * half_width,
        a * columns,
    )
    copies = []
    for n, (first, target) in enumerate(zip(firsts, (whole, half, own))):
        span = pl.ds(pl.multiple_of(first, lane), target.shape[1])
        copies.append(pltpu.make_async_copy(expand.at[0, :, span], target, sem.at[n]))
    for n, (source, target) in enumerate(zip(small, loaded)):
        copies.append(pltpu.make_async_copy(source, target, sem.at[len(firsts) + n]))
    copies += weight_copies(block, numbers, weight, held, held_sem)
    for copy in copies:
        copy.start()
    for copy in copies:
        copy.wait()


def weight_copies(block, numbers, weight, target, sem):
    band_count = sem.shape[1]
    band = weight.shape[0] // band_count
    copies = []
    for n, number in enumerate(numbers):
        span = pl.ds(number * block, block)
        for m in range(band_count):
            rows = pl.ds(m * band, band)
            copies.append(
                pltpu.make_async_copy(weight.at[rows, span], target.at[n, rows], sem.at[n, m])
            )
    return copies


def gather_kernel(offsets, slots, index, *refs):
    owner_count = len(offsets)
    blocks = refs[:owner_count]
    shrink, rows_out, keep, send, slot_out, rows, partial = refs[owner_count:]
    a, t = lax.axis_index("adapter"), lax.axis_index("tensor")
    height, depth = blocks[0].shape
    for j, part in zip(offsets, blocks):
        where = lax.rem(a + j, owner_count)
        rows[pl.ds(pl.multiple_of(where * height, height), height), :] = part[:, :depth]
    quarter = rows.shape[0] // 4
    for i, flip in enumerate((0, 2, 1, 3)):
        start = pl.multiple_of(lax.bitwise_xor(t, flip) * quarter, quarter)
        rows_out[i * quarter : (i + 1) * quarter, :] = rows[pl.ds(start, quarter), :]
    product = lax.dot_general(
        shrink[...], rows[...], (((1,), (1,)), ((), ())), preferred_element_type=f32
    )
    named, table = index[...], slots[...]
    slot = jnp.zeros_like(named)
    for k in range(table.shape[1]):
        slot = jnp.where(named == k, table[:, k : k + 1], slot)
    slot_out[...] = slot
    partial[...] = jnp.where(slot == a, product, 0.0)
    rank_block = partial.shape[0] // 4
    for i, flip in enumerate((0, 2, 1, 3)):
        start = pl.multiple_of(lax.bitwise_xor(t, flip) * rank_block, rank_block)
        target = keep if i < 2 else send
        at = i % 2 * rank_block
        target[at : at + rank_block, :] = partial[pl.ds(start, rank_block), :]


def base_kernel(block, places, numbers, streamed, rows, weight, *refs):
    total, ahead, sem = refs[-3:]
    copies = weight_copies(block, numbers, weight, ahead, sem)
    for copy in copies:
        copy.start()

    @pl.when(lax.axis_index("tensor") >= 0)
    def _():
        for n, (which, index) in enumerate(places):
            total[:, n * block : (n + 1) * block] = jnp.dot(
                rows[...], refs[which][index], preferred_element_type=f32
            )

    bands = sem.shape[1]
    for n in range(len(numbers)):
        for copy in copies[n * bands : (n + 1) * bands]:
            copy.wait()
        if streamed:
            at = (len(places) + n) * block
            total[:, at : at + block] = jnp.dot(
                rows[...], ahead[n], preferred_element_type=f32
            )


def pack_kernel(whole, half, packed):
    columns = whole.shape[1]
    packed[:, :columns] = whole[...]
    packed[:, columns:] = half[...]


def delta_kernel(block, splits, slot, *refs):
    bases, refs = refs[: -len(splits) * 2 - 10], refs[-len(splits) * 2 - 10 :]
    own, shrunk, whole, half, packed, own_keep, own_send = refs[:7]
    cross_keep, cross_send = refs[7 : 7 + len(splits)], refs[7 + len(splits) : 7 + 2 * len(splits)]
    flat, ordered, two = refs[-3:]
    g, a, t = (lax.axis_index(name) for name in ("groups", "adapter", "tensor"))
    row_count = bases[0].shape[0]
    quarter = row_count // 4
    columns, half_width = whole.shape[1], half.shape[1]

    @pl.when(g == 0)
    def _():
        two[:, :half_width] = half[...]
        two[:, half_width:] = packed[:, columns:]

    @pl.when(g != 0)
    def _():
        two[:, :half_width] = packed[:, columns:]
        two[:, half_width:] = half[...]

    merged = shrunk[...].astype(f32)
    spread = [
        jnp.where(slot[...] == lax.rem(a + j, 4), merged, 0.0)
        for j in (0, 1 + 2 * g, 3 - 2 * g, 2)
    ]
    flat[...] = jnp.concatenate(spread, axis=0).T
    for i, turn in enumerate((0, 2, 1, 3)):
        start = pl.multiple_of(lax.bitwise_xor(t, turn) * quarter, quarter)
        ordered[i * quarter : (i + 1) * quarter, :] = flat[pl.ds(start, quarter), :].astype(bf16)
    left = ordered[...]
    at, split = 0, 0
    for base in bases:
        for column in range(0, base.shape[1], block):
            span = slice(at, at + block)
            expand = jnp.concatenate(
                [own[:, span], whole[:, span], packed[:, span], two[:, span]], axis=0
            )
            total = base[:, column : column + block] + jnp.dot(
                left, expand, preferred_element_type=f32
            )
            if at >= splits[split][1]:
                split += 1
            here = slice(at - splits[split][0], at - splits[split][0] + block)
            own_keep[:, span] = total[:quarter]
            cross_keep[split][:, here] = total[quarter : 2 * quarter]
            own_send[:, span] = total[2 * quarter : 3 * quarter]
            cross_send[split][:, here] = total[3 * quarter :]
            at += block


def column_block(width):
    for size in (512, 256, 128):
        if width % size == 0:
            return size


def paired(
    tokens,
    base_up_weight,
    adapter_shrink_weight,
    adapter_expand_weight,
    row_adapter_index,
    adapter_slot_index,
):
    owner_count = lax.axis_size("adapter")
    g = lax.axis_index("groups")
    height, depth = tokens.shape
    row_count = height * owner_count
    columns = base_up_weight.shape[1]
    rank_block = adapter_expand_weight.shape[1]
    rank = adapter_shrink_weight.shape[2]
    half_width = columns // 2
    block = column_block(columns)
    block_count = columns // block

    def from_owner(x, j):
        return lax.ppermute(x, "adapter", [(s, (s - j) % owner_count) for s in range(owner_count)])

    def from_either(x):
        pairs = []
        for group, j in ((0, 1), (1, 3)):
            for s in range(owner_count):
                pairs.append(
                    (group * owner_count + s, group * owner_count + (s - j) % owner_count)
                )
        return lax.ppermute(x, ("groups", "adapter"), pairs)

    def from_tensor(x, m):
        return lax.ppermute(x, "tensor", [(s, s ^ m) for s in range(4)])

    def from_mirror(x, m):
        return lax.ppermute(x, "adapter", [(s, s ^ m) for s in range(owner_count)])

    def from_group(x):
        return lax.ppermute(x, "groups", [(0, 1), (1, 0)])

    weight = pltpu.with_memory_space_constraint(base_up_weight, pltpu.HBM)
    expand = pltpu.with_memory_space_constraint(adapter_expand_weight, pltpu.HBM)
    offsets = (2, 1, 3)
    blocks = [from_owner(tokens, j) for j in offsets]

    cuts = [block_count * k // 14 for k in (0, 4, 8, 11, 14)]
    parts = list(zip(cuts[:-1], cuts[1:]))
    loads = [block_count * k // 14 for k in (0, 4, 8, 11, 12, 14)]
    bands = 4
    small = [
        pltpu.with_memory_space_constraint(x, pltpu.HBM)
        for x in (
            adapter_slot_index.reshape(1, owner_count),
            row_adapter_index.reshape(1, row_count),
            tokens,
            adapter_shrink_weight[0].T,
        )
    ]
    whole, half, own, slots, index, mine, shrink, held = kernel_call(
        functools.partial(cut_kernel, block, range(loads[1]), len(small)),
        "cut_expand",
        1,
        1,
        1,
        in_specs=[anywhere] * (2 + len(small)),
        out_specs=[vmem] * (4 + len(small)),
        out_shape=[pltpu.VMEM((rank_block, w), bf16) for w in (columns, half_width, columns)]
        + [pltpu.VMEM(x.shape, x.dtype) for x in small]
        + [pltpu.VMEM((loads[1], depth, block), bf16)],
        scratch_shapes=[
            pltpu.SemaphoreType.DMA((3 + len(small),)),
            pltpu.SemaphoreType.DMA((loads[1], bands)),
        ],
    )(expand, weight, *small)
    loaded = [held]
    whole, half = from_either(whole), from_owner(half, 2)

    rows, keep, send, slot = kernel_call(
        functools.partial(gather_kernel, (0, *offsets)),
        "gather_rows",
        1,
        1,
        4,
        in_specs=[vmem] * (owner_count + 3),
        out_specs=[vmem] * 4,
        out_shape=[jax.ShapeDtypeStruct((row_count, depth), bf16)]
        + [jax.ShapeDtypeStruct((rank // 2, row_count), f32)] * 2
        + [jax.ShapeDtypeStruct((1, row_count), jnp.int32)],
        scratch_shapes=[pltpu.VMEM((row_count, depth), bf16), pltpu.VMEM((rank, row_count), f32)],
    )(
        slots,
        index,
        mine,
        *blocks,
        shrink,
    )

    def base_part(n, *after):
        first, last = parts[n]
        streamed = n + 1 == len(parts)
        numbers = range(loads[n + 1], loads[n + 2])
        places, used = [], []
        for number in range(first, numbers[0] if streamed else last):
            source = max(k for k in range(len(loads) - 1) if loads[k] <= number)
            if source not in used:
                used.append(source)
            places.append((used.index(source), number - loads[source]))
        near = n < 2
        ahead = pltpu.VMEM((len(numbers), depth, block), bf16)
        out = kernel_call(
            functools.partial(base_kernel, block, places, numbers, streamed),
            "base_part",
            3 * 2 * row_count * depth * (last - first) * block if near else 1,
            3 * 2 * depth * (last - first) * block if near else 1,
            12,
            in_specs=[vmem, anywhere] + [vmem] * len(used) + [anywhere] * len(after),
            out_specs=[vmem] * (1 if streamed else 2),
            out_shape=[jax.ShapeDtypeStruct((row_count, (last - first) * block), f32)]
            + ([] if streamed else [ahead]),
            scratch_shapes=([ahead] if streamed else [])
            + [pltpu.SemaphoreType.DMA((len(numbers), bands))],
        )(rows, weight, *[loaded[k] for k in used], *after)
        loaded.append(out[-1])
        return out[0]

    arrived = from_tensor(send, 1)
    base_0 = base_part(0, send)
    arrived, base_0 = lax.optimization_barrier((arrived, base_0))
    pair = keep + arrived
    arrived = from_tensor(pair[rank_block:], 2)
    base_1 = base_part(1, pair)
    arrived, base_1, whole, half = lax.optimization_barrier((arrived, base_1, whole, half))
    shrunk = (adapter_scale * (pair[:rank_block] + arrived)).astype(bf16)
    packed = kernel_call(
        pack_kernel,
        "pack_pieces",
        1,
        1,
        2,
        in_specs=[vmem] * 2,
        out_specs=vmem,
        out_shape=jax.ShapeDtypeStruct((rank_block, columns + half_width), bf16),
    )(whole, half)
    swapped = from_group(packed)
    bases = [base_0, base_1]
    for m, n in ((1, 2), (2, 3)):
        arrived = from_mirror(shrunk, m)
        base = base_part(n, shrunk, packed)
        arrived, base = lax.optimization_barrier((arrived, base))
        bases.append(base)
        shrunk = shrunk + arrived

    middle = block_count // 2 * block
    splits = [(0, middle), (middle, columns)]
    widths = [last - first for first, last in splits]
    quarter = row_count // 4
    out = kernel_call(
        functools.partial(delta_kernel, block, splits),
        "add_delta",
        1,
        1,
        8,
        in_specs=[vmem] * (len(bases) + 6),
        out_specs=[vmem] * (2 + 2 * len(splits)),
        out_shape=[
            jax.ShapeDtypeStruct((quarter, w), f32) for w in (columns, columns, *widths, *widths)
        ],
        scratch_shapes=[
            pltpu.VMEM((row_count, rank_block * owner_count), f32),
            pltpu.VMEM((row_count, rank_block * owner_count), bf16),
            pltpu.VMEM((rank_block, columns), bf16),
        ],
    )(slot, *bases, own, shrunk, whole, half, swapped)
    own_keep, own_send = out[:2]
    crossed = []
    for keep, send in zip(out[2:4], out[4:6]):
        crossed.append(from_tensor((keep + from_tensor(send, 1)).astype(bf16), 2))
    kept = own_keep + from_tensor(own_send, 1)
    return jnp.concatenate(
        [
            (kept[:, first:last] + part.astype(f32)).astype(bf16)
            for (first, last), part in zip(splits, crossed)
        ],
        axis=1,
    )


def on_device(tokens, base_up_weight, adapter_shrink_weight, adapter_expand_weight, *index):
    pairs = lax.axis_size("groups") == 2 and lax.axis_size("tensor") == 4
    few = lax.axis_size("adapter") == 4
    columns = base_up_weight.shape[1]
    even = columns % 512 == 0 and columns >= 4096 and tokens.shape[0] % 16 == 0
    arrange = paired if pairs and few and even else general
    return arrange(
        tokens, base_up_weight, adapter_shrink_weight, adapter_expand_weight, *index
    )


def solution(mesh):
    placed = (
        P(("groups", "adapter"), "tensor"),
        P("tensor", "adapter"),
        P("adapter", "tensor", None),
        P("adapter", "tensor", None),
        P("groups", None),
        P(),
    )
    return jax.shard_map(
        on_device,
        mesh=mesh,
        in_specs=placed,
        out_specs=P(("groups", "tensor"), "adapter"),
        check_vma=False,
    )
```

```python
import functools

import jax
import jax.numpy as jnp
from jax import lax
from jax.experimental import pallas as pl
from jax.experimental.pallas import tpu as pltpu
from jax.sharding import PartitionSpec as P

adapter_scale = 0.5
lane = 128
f32 = jnp.float32
bf16 = jnp.bfloat16


def general(
    tokens,
    base_up_weight,
    adapter_shrink_weight,
    adapter_expand_weight,
    row_adapter_index,
    adapter_slot_index,
):
    owner_count = lax.axis_size("adapter")
    owner_index = lax.axis_index("adapter")
    tensor_index = lax.axis_index("tensor")
    rank_block = adapter_expand_weight.shape[1]
    columns = base_up_weight.shape[1]
    slot = jnp.take(adapter_slot_index, row_adapter_index[:, 0], axis=0)
    rows = lax.all_gather(tokens, "adapter", axis=0, tiled=True)
    expand = adapter_expand_weight[0].reshape(rank_block, owner_count, columns)
    expand = lax.all_to_all(expand, "adapter", split_axis=1, concat_axis=1, tiled=True)
    shrunk = jnp.dot(rows, adapter_shrink_weight[0], preferred_element_type=f32)
    shrunk = jnp.where((slot == owner_index)[:, None], shrunk, 0.0)
    shrunk = lax.psum(shrunk, ("adapter", "tensor"))
    shrunk = (adapter_scale * shrunk).astype(bf16)
    shrunk = lax.dynamic_slice_in_dim(shrunk, tensor_index * rank_block, rank_block, 1)
    chosen = slot[:, None] == jnp.arange(owner_count, dtype=jnp.int32)[None, :]
    spread = jnp.where(chosen[:, None, :], shrunk[:, :, None], jnp.zeros((), bf16))
    total = jnp.dot(rows, base_up_weight, preferred_element_type=f32)
    total = total + jnp.dot(
        spread.reshape(-1, rank_block * owner_count),
        expand.reshape(rank_block * owner_count, columns),
        preferred_element_type=f32,
    )
    return lax.psum_scatter(total, "tensor", scatter_dimension=0, tiled=True).astype(bf16)


vmem = pl.BlockSpec(memory_space=pltpu.VMEM)
anywhere = pl.BlockSpec(memory_space=pl.ANY)


def kernel_call(kernel, name, flops, moved, mib, **specs):
    return pl.pallas_call(
        kernel,
        cost_estimate=pl.CostEstimate(flops=flops, bytes_accessed=moved, transcendentals=0),
        compiler_params=pltpu.CompilerParams(vmem_limit_bytes=mib << 20),
        name=name,
        **specs,
    )


def cut_kernel(
    owner_count, offsets, far_width, start_of, block, numbers, small_count, expand, weight, *refs
):
    small, refs = refs[:small_count], refs[small_count:]
    *pieces, own = refs[: owner_count]
    *loaded, held, sem, held_sem = refs[owner_count:]
    g, a = lax.axis_index("groups"), lax.axis_index("adapter")
    near_width = pieces[0].shape[1]
    columns = near_width + far_width
    start = pl.multiple_of(a * columns, lane)
    copies = [
        pltpu.make_async_copy(expand.at[0, :, pl.ds(start, columns)], own, sem.at[len(pieces)])
    ]
    for n, (j, piece) in enumerate(zip(offsets, pieces)):
        to = lax.rem(a - j + owner_count, owner_count)
        start = pl.multiple_of(to * columns + g * far_width, lane)
        copies.append(
            pltpu.make_async_copy(expand.at[0, :, pl.ds(start, near_width)], piece, sem.at[n])
        )
    for n, (source, target) in enumerate(zip(small, loaded)):
        copies.append(pltpu.make_async_copy(source, target, sem.at[owner_count + n]))
    copies += weight_copies(start_of, block, numbers, weight, held, held_sem)
    for copy in copies:
        copy.start()
    for copy in copies:
        copy.wait()


def block_start(near_width, far_width, block, number):
    g, at = lax.axis_index("groups"), number * block
    return g * far_width + at if at < near_width else (1 - g) * near_width + at - near_width


def weight_copies(start_of, block, numbers, weight, target, sem):
    band_count = sem.shape[1]
    band = weight.shape[0] // band_count
    copies = []
    for n, number in enumerate(numbers):
        span = pl.ds(pl.multiple_of(start_of(number), lane), block)
        for m in range(band_count):
            rows = pl.ds(m * band, band)
            copies.append(
                pltpu.make_async_copy(weight.at[rows, span], target.at[n, rows], sem.at[n, m])
            )
    return copies


def gather_kernel(offsets, slots, index, *refs):
    owner_count = len(offsets)
    blocks = refs[:owner_count]
    shrink, rows_out, keep, send, slot_out, rows, partial = refs[owner_count:]
    a, t = lax.axis_index("adapter"), lax.axis_index("tensor")
    height, depth = blocks[0].shape
    for j, part in zip(offsets, blocks):
        where = lax.rem(a + j, owner_count)
        rows[pl.ds(pl.multiple_of(where * height, height), height), :] = part[:, :depth]
    quarter = rows.shape[0] // 4
    for i, flip in enumerate((0, 2, 1, 3)):
        start = pl.multiple_of(lax.bitwise_xor(t, flip) * quarter, quarter)
        rows_out[i * quarter : (i + 1) * quarter, :] = rows[pl.ds(start, quarter), :]
    product = lax.dot_general(
        shrink[...], rows[...], (((1,), (1,)), ((), ())), preferred_element_type=f32
    )
    named, table = index[...], slots[...]
    slot = jnp.zeros_like(named)
    for k in range(table.shape[1]):
        slot = jnp.where(named == k, table[:, k : k + 1], slot)
    slot_out[...] = slot
    partial[...] = jnp.where(slot == a, product, 0.0)
    rank_block = partial.shape[0] // 4
    for i, flip in enumerate((0, 2, 1, 3)):
        start = pl.multiple_of(lax.bitwise_xor(t, flip) * rank_block, rank_block)
        target = keep if i < 2 else send
        at = i % 2 * rank_block
        target[at : at + rank_block, :] = partial[pl.ds(start, rank_block), :]


def base_kernel(start_of, block, numbers, rows, weight, held, *refs):
    copies = []
    if numbers:
        total, ahead, sem = refs[-3:]
        copies = weight_copies(start_of, block, numbers, weight, ahead, sem)
    else:
        total = refs[-1]
    for copy in copies:
        copy.start()

    @pl.when(lax.axis_index("tensor") >= 0)
    def _():
        for n in range(held.shape[0]):
            total[:, n * block : (n + 1) * block] = jnp.dot(
                rows[...], held[n], preferred_element_type=f32
            )

    for copy in copies:
        copy.wait()


def forward_kernel(far_width, *refs):
    *near, packed = refs
    height, near_width = near[-1].shape
    start = pl.multiple_of(lax.axis_index("groups") * (near_width - far_width), lane)
    for n, piece in enumerate(near):
        skip = piece.shape[1] - near_width
        packed[n * height : (n + 1) * height, :] = piece[:, pl.ds(start + skip, far_width)]


def delta_kernel(owner_count, offsets, start_of, first, block, base_count, piece_count, slot, *refs):
    bases, refs = refs[:base_count], refs[base_count:]
    own, shrunk = refs[:2]
    pieces = refs[2 : 2 + piece_count]
    width = sum(base.shape[1] for base in bases)
    *outs, flat, ordered = refs[-6:]
    a, t = lax.axis_index("adapter"), lax.axis_index("tensor")
    row_count = bases[0].shape[0]
    quarter = row_count // 4
    slot = slot[...]
    merged = shrunk[...].astype(f32)
    spread = [
        jnp.where(slot == lax.rem(a + j, owner_count), merged, 0.0) for j in (0, *offsets)
    ]
    flat[...] = jnp.concatenate(spread, axis=0).T
    for i, turn in enumerate((0, 2, 1, 3)):
        start = pl.multiple_of(lax.bitwise_xor(t, turn) * quarter, quarter)
        ordered[i * quarter : (i + 1) * quarter, :] = flat[pl.ds(start, quarter), :].astype(bf16)
    left = ordered[...]
    at = 0
    for base in bases:
        for column in range(0, base.shape[1], block):
            source = pl.multiple_of(start_of(first + at // block), lane)
            expand = jnp.concatenate(
                [own[:, pl.ds(source, block)]]
                + [piece[:, pl.ds(piece.shape[1] - width + at, block)] for piece in pieces],
                axis=0,
            )
            total = base[:, column : column + block] + jnp.dot(
                left, expand, preferred_element_type=f32
            )
            for n, out in enumerate(outs):
                out[:, at : at + block] = total[n * quarter : (n + 1) * quarter]
            at += block


def column_block(width):
    for size in (512, 256, 128):
        if width % size == 0:
            return size


def paired(
    tokens,
    base_up_weight,
    adapter_shrink_weight,
    adapter_expand_weight,
    row_adapter_index,
    adapter_slot_index,
):
    owner_count = lax.axis_size("adapter")
    g = lax.axis_index("groups")
    height, depth = tokens.shape
    row_count = height * owner_count
    columns = base_up_weight.shape[1]
    rank_block = adapter_expand_weight.shape[1]
    rank = adapter_shrink_weight.shape[2]
    block = column_block(columns)
    block_count = columns // block
    near_count = max(1, block_count * 8 // 14)
    near_width = near_count * block
    far_width = columns - near_width

    def from_owner(x, j):
        return lax.ppermute(x, "adapter", [(s, (s - j) % owner_count) for s in range(owner_count)])

    def from_tensor(x, m):
        return lax.ppermute(x, "tensor", [(s, s ^ m) for s in range(4)])

    def from_mirror(x, m):
        return lax.ppermute(x, "adapter", [(s, s ^ m) for s in range(owner_count)])

    def from_group(x):
        return lax.ppermute(x, "groups", [(0, 1), (1, 0)])

    weight = pltpu.with_memory_space_constraint(base_up_weight, pltpu.HBM)
    expand = pltpu.with_memory_space_constraint(adapter_expand_weight, pltpu.HBM)
    offsets = (2, 1, 3)

    near_half, far_half = near_count - near_count // 2, (block_count - near_count + 1) // 2
    cuts = (0, near_half, near_count, near_count + far_half, block_count)
    parts = list(zip(cuts[:-1], cuts[1:]))
    loads = [*cuts, block_count]
    start_of = functools.partial(block_start, near_width, far_width, block)
    bands = 4

    small = [
        pltpu.with_memory_space_constraint(x, pltpu.HBM)
        for x in (
            adapter_slot_index.reshape(1, owner_count),
            row_adapter_index.reshape(1, row_count),
            tokens,
            adapter_shrink_weight[0].T,
        )
    ]
    cut = kernel_call(
        functools.partial(
            cut_kernel, owner_count, offsets, far_width, start_of, block, range(loads[1]), len(small)
        ),
        "cut_expand",
        1,
        1,
        1,
        in_specs=[anywhere] * (2 + len(small)),
        out_specs=[vmem] * (owner_count + len(small) + 1),
        out_shape=[pltpu.VMEM((rank_block, near_width), bf16)] * (owner_count - 1)
        + [pltpu.VMEM((rank_block, columns), bf16)]
        + [pltpu.VMEM(x.shape, x.dtype) for x in small]
        + [pltpu.VMEM((loads[1], depth, block), bf16)],
        scratch_shapes=[
            pltpu.SemaphoreType.DMA((owner_count + len(small),)),
            pltpu.SemaphoreType.DMA((loads[1], bands)),
        ],
    )(expand, weight, *small)
    pieces, own = cut[: owner_count - 1], cut[owner_count - 1]
    slots, index, mine, shrink, held = cut[owner_count:]
    blocks = [from_owner(tokens, j) for j in offsets]
    loaded = [held]

    rows, keep, send, slot = kernel_call(
        functools.partial(gather_kernel, (0, *offsets)),
        "gather_rows",
        1,
        1,
        4,
        in_specs=[vmem] * (owner_count + 3),
        out_specs=[vmem] * 4,
        out_shape=[jax.ShapeDtypeStruct((row_count, depth), bf16)]
        + [jax.ShapeDtypeStruct((rank // 2, row_count), f32)] * 2
        + [jax.ShapeDtypeStruct((1, row_count), jnp.int32)],
        scratch_shapes=[pltpu.VMEM((row_count, depth), bf16), pltpu.VMEM((rank, row_count), f32)],
    )(
        slots,
        index,
        mine,
        *blocks,
        shrink,
    )

    def base_part(n, *after):
        first, last = parts[n]
        numbers = range(loads[n + 1], loads[n + 2])
        out = kernel_call(
            functools.partial(base_kernel, start_of, block, numbers),
            "base_part",
            10**10,
            1,
            4,
            in_specs=[vmem, anywhere, vmem] + [anywhere] * len(after),
            out_specs=[vmem] * (2 if numbers else 1),
            out_shape=[jax.ShapeDtypeStruct((row_count, (last - first) * block), f32)]
            + ([pltpu.VMEM((len(numbers), depth, block), bf16)] if numbers else []),
            scratch_shapes=[pltpu.SemaphoreType.DMA((len(numbers), bands))] if numbers else [],
        )(rows, weight, loaded[n], *after)
        loaded.append(out[-1])
        return out[0]

    def delta_part(is_far, bases, pieces):
        first = near_count if is_far else 0
        width = sum(base.shape[1] for base in bases)
        return kernel_call(
            functools.partial(
                delta_kernel, owner_count, offsets, start_of, first, block, len(bases), len(pieces)
            ),
            "delta_part",
            1,
            1,
            8,
            in_specs=[vmem] * (3 + len(bases) + len(pieces)),
            out_specs=[vmem] * 4,
            out_shape=[jax.ShapeDtypeStruct((row_count // 4, width), f32)] * 4,
            scratch_shapes=[
                pltpu.VMEM((row_count, rank_block * owner_count), f32),
                pltpu.VMEM((row_count, rank_block * owner_count), bf16),
            ],
        )(slot, *bases, own, shrunk, *pieces)

    *pieces, own, send = lax.optimization_barrier((*pieces, own, send))
    arrived = from_tensor(send, 1)
    near = [from_owner(piece, j) for piece, j in zip(pieces, offsets)]
    pair = keep + arrived
    arrived = from_tensor(pair[rank_block:], 2)
    base_0 = base_part(0, pair)
    arrived, base_0 = lax.optimization_barrier((arrived, base_0))
    shrunk = (adapter_scale * (pair[:rank_block] + arrived)).astype(bf16)
    arrived = from_mirror(shrunk, 1)
    base_1 = base_part(1, shrunk)
    arrived, base_1, *near = lax.optimization_barrier((arrived, base_1, *near))
    shrunk = shrunk + arrived
    arrived = from_mirror(shrunk, 2)
    packed = kernel_call(
        functools.partial(forward_kernel, far_width),
        "pack_far",
        1,
        1,
        2,
        in_specs=[vmem] * (owner_count - 1),
        out_specs=vmem,
        out_shape=jax.ShapeDtypeStruct(((owner_count - 1) * rank_block, far_width), bf16),
    )(*near)
    far = from_group(packed)
    arrived, packed = lax.optimization_barrier((arrived, packed))
    shrunk = shrunk + arrived

    own_keep, cross_keep, own_send, cross_send = delta_part(False, [base_0, base_1], near)
    arrived = from_tensor(cross_send, 1)
    kept = own_keep + from_tensor(own_send, 1)
    base_2 = base_part(2, cross_send)
    arrived, base_2 = lax.optimization_barrier((arrived, base_2))
    cross = (cross_keep + arrived).astype(bf16)
    crossed = from_tensor(cross, 2)
    base_3 = base_part(3, cross)
    own_keep, cross_keep, own_send, cross_send = delta_part(True, [base_2, base_3], [far])
    own_send, cross_send, crossed = lax.optimization_barrier((own_send, cross_send, crossed))
    halves = [(kept + crossed.astype(f32)).astype(bf16)]
    cross = (cross_keep + from_tensor(cross_send, 1)).astype(bf16)
    kept = own_keep + from_tensor(own_send, 1)
    halves.append((kept + from_tensor(cross, 2).astype(f32)).astype(bf16))
    first = jnp.concatenate(halves, axis=1)
    second = jnp.concatenate(halves[::-1], axis=1)
    return jnp.where(g == 0, first, second)


def on_device(tokens, base_up_weight, adapter_shrink_weight, adapter_expand_weight, *index):
    pairs = lax.axis_size("groups") == 2 and lax.axis_size("tensor") == 4
    few = lax.axis_size("adapter") == 4
    columns = base_up_weight.shape[1]
    even = columns % 512 == 0 and columns >= 4096 and tokens.shape[0] % 16 == 0
    arrange = paired if pairs and few and even else general
    return arrange(
        tokens, base_up_weight, adapter_shrink_weight, adapter_expand_weight, *index
    )


def solution(mesh):
    placed = (
        P(("groups", "adapter"), "tensor"),
        P("tensor", "adapter"),
        P("adapter", "tensor", None),
        P("adapter", "tensor", None),
        P("groups", None),
        P(),
    )
    return jax.shard_map(
        on_device,
        mesh=mesh,
        in_specs=placed,
        out_specs=P(("groups", "tensor"), "adapter"),
        check_vma=False,
    )
```

```python
import functools

import jax
import jax.numpy as jnp
from jax import lax
from jax.experimental import pallas as pl
from jax.experimental.pallas import tpu as pltpu
from jax.sharding import PartitionSpec as P

adapter_scale = 0.5
lane = 128
f32 = jnp.float32
bf16 = jnp.bfloat16


def general(
    tokens,
    base_up_weight,
    adapter_shrink_weight,
    adapter_expand_weight,
    row_adapter_index,
    adapter_slot_index,
):
    owner_count = lax.axis_size("adapter")
    owner_index = lax.axis_index("adapter")
    tensor_index = lax.axis_index("tensor")
    rank_block = adapter_expand_weight.shape[1]
    columns = base_up_weight.shape[1]
    slot = jnp.take(adapter_slot_index, row_adapter_index[:, 0], axis=0)
    rows = lax.all_gather(tokens, "adapter", axis=0, tiled=True)
    expand = adapter_expand_weight[0].reshape(rank_block, owner_count, columns)
    expand = lax.all_to_all(expand, "adapter", split_axis=1, concat_axis=1, tiled=True)
    shrunk = jnp.dot(rows, adapter_shrink_weight[0], preferred_element_type=f32)
    shrunk = jnp.where((slot == owner_index)[:, None], shrunk, 0.0)
    shrunk = lax.psum(shrunk, ("adapter", "tensor"))
    shrunk = (adapter_scale * shrunk).astype(bf16)
    shrunk = lax.dynamic_slice_in_dim(shrunk, tensor_index * rank_block, rank_block, 1)
    chosen = slot[:, None] == jnp.arange(owner_count, dtype=jnp.int32)[None, :]
    spread = jnp.where(chosen[:, None, :], shrunk[:, :, None], jnp.zeros((), bf16))
    total = jnp.dot(rows, base_up_weight, preferred_element_type=f32)
    total = total + jnp.dot(
        spread.reshape(-1, rank_block * owner_count),
        expand.reshape(rank_block * owner_count, columns),
        preferred_element_type=f32,
    )
    return lax.psum_scatter(total, "tensor", scatter_dimension=0, tiled=True).astype(bf16)


vmem = pl.BlockSpec(memory_space=pltpu.VMEM)
anywhere = pl.BlockSpec(memory_space=pl.ANY)


def kernel_call(kernel, name, flops, moved, mib, **specs):
    return pl.pallas_call(
        kernel,
        cost_estimate=pl.CostEstimate(flops=flops, bytes_accessed=moved, transcendentals=0),
        compiler_params=pltpu.CompilerParams(vmem_limit_bytes=mib << 20),
        name=name,
        **specs,
    )


def cut_kernel(block, numbers, small_count, expand, weight, *refs):
    small, refs = refs[:small_count], refs[small_count:]
    whole, half, own, *loaded, held, sem, held_sem = refs
    g, a = lax.axis_index("groups"), lax.axis_index("adapter")
    columns, half_width = whole.shape[1], half.shape[1]
    firsts = (
        lax.rem(a + 3 - 2 * g, 4) * columns,
        lax.rem(a + 2, 4) * columns + g * half_width,
        a * columns,
    )
    copies = []
    for n, (first, target) in enumerate(zip(firsts, (whole, half, own))):
        span = pl.ds(pl.multiple_of(first, lane), target.shape[1])
        copies.append(pltpu.make_async_copy(expand.at[0, :, span], target, sem.at[n]))
    for n, (source, target) in enumerate(zip(small, loaded)):
        copies.append(pltpu.make_async_copy(source, target, sem.at[len(firsts) + n]))
    copies += weight_copies(block, numbers, weight, held, held_sem)
    for copy in copies:
        copy.start()
    for copy in copies:
        copy.wait()


def weight_copies(block, numbers, weight, target, sem):
    band_count = sem.shape[1]
    band = weight.shape[0] // band_count
    copies = []
    for n, number in enumerate(numbers):
        span = pl.ds(number * block, block)
        for m in range(band_count):
            rows = pl.ds(m * band, band)
            copies.append(
                pltpu.make_async_copy(weight.at[rows, span], target.at[n, rows], sem.at[n, m])
            )
    return copies


def gather_kernel(offsets, slots, index, *refs):
    owner_count = len(offsets)
    blocks = refs[:owner_count]
    shrink, rows_out, keep, send, slot_out, rows, partial = refs[owner_count:]
    a, t = lax.axis_index("adapter"), lax.axis_index("tensor")
    height, depth = blocks[0].shape
    for j, part in zip(offsets, blocks):
        where = lax.rem(a + j, owner_count)
        rows[pl.ds(pl.multiple_of(where * height, height), height), :] = part[:, :depth]
    quarter = rows.shape[0] // 4
    for i, flip in enumerate((0, 2, 1, 3)):
        start = pl.multiple_of(lax.bitwise_xor(t, flip) * quarter, quarter)
        rows_out[i * quarter : (i + 1) * quarter, :] = rows[pl.ds(start, quarter), :]
    product = lax.dot_general(
        shrink[...], rows[...], (((1,), (1,)), ((), ())), preferred_element_type=f32
    )
    named, table = index[...], slots[...]
    slot = jnp.zeros_like(named)
    for k in range(table.shape[1]):
        slot = jnp.where(named == k, table[:, k : k + 1], slot)
    slot_out[...] = slot
    partial[...] = jnp.where(slot == a, product, 0.0)
    rank_block = partial.shape[0] // 4
    for i, flip in enumerate((0, 2, 1, 3)):
        start = pl.multiple_of(lax.bitwise_xor(t, flip) * rank_block, rank_block)
        target = keep if i < 2 else send
        at = i % 2 * rank_block
        target[at : at + rank_block, :] = partial[pl.ds(start, rank_block), :]


def base_kernel(block, places, numbers, rows, weight, *refs):
    copies = []
    if numbers:
        total, ahead, sem = refs[-3:]
        copies = weight_copies(block, numbers, weight, ahead, sem)
    else:
        total = refs[-1]
    for copy in copies:
        copy.start()

    @pl.when(lax.axis_index("tensor") >= 0)
    def _():
        for n, (which, index) in enumerate(places):
            total[:, n * block : (n + 1) * block] = jnp.dot(
                rows[...], refs[which][index], preferred_element_type=f32
            )

    for copy in copies:
        copy.wait()


def delta_kernel(block, splits, slot, *refs):
    bases, refs = refs[: -len(splits) * 2 - 11], refs[-len(splits) * 2 - 11 :]
    own, shrunk, whole, half, far_whole, far_half, own_keep, own_send = refs[:8]
    cross_keep, cross_send = refs[8 : 8 + len(splits)], refs[8 + len(splits) : 8 + 2 * len(splits)]
    flat, ordered, two = refs[-3:]
    g, a, t = (lax.axis_index(name) for name in ("groups", "adapter", "tensor"))
    row_count = bases[0].shape[0]
    quarter = row_count // 4
    half_width = half.shape[1]

    @pl.when(g == 0)
    def _():
        two[:, :half_width] = half[...]
        two[:, half_width:] = far_half[...]

    @pl.when(g != 0)
    def _():
        two[:, :half_width] = far_half[...]
        two[:, half_width:] = half[...]

    merged = shrunk[...].astype(f32)
    spread = [
        jnp.where(slot[...] == lax.rem(a + j, 4), merged, 0.0)
        for j in (0, 1 + 2 * g, 3 - 2 * g, 2)
    ]
    flat[...] = jnp.concatenate(spread, axis=0).T
    for i, turn in enumerate((0, 2, 1, 3)):
        start = pl.multiple_of(lax.bitwise_xor(t, turn) * quarter, quarter)
        ordered[i * quarter : (i + 1) * quarter, :] = flat[pl.ds(start, quarter), :].astype(bf16)
    left = ordered[...]
    at, split = 0, 0
    for base in bases:
        for column in range(0, base.shape[1], block):
            span = slice(at, at + block)
            expand = jnp.concatenate(
                [own[:, span], whole[:, span], far_whole[:, span], two[:, span]], axis=0
            )
            total = base[:, column : column + block] + jnp.dot(
                left, expand, preferred_element_type=f32
            )
            if at >= splits[split][1]:
                split += 1
            here = slice(at - splits[split][0], at - splits[split][0] + block)
            own_keep[:, span] = total[:quarter]
            cross_keep[split][:, here] = total[quarter : 2 * quarter]
            own_send[:, span] = total[2 * quarter : 3 * quarter]
            cross_send[split][:, here] = total[3 * quarter :]
            at += block


def column_block(width):
    for size in (512, 256, 128):
        if width % size == 0:
            return size


def paired(
    tokens,
    base_up_weight,
    adapter_shrink_weight,
    adapter_expand_weight,
    row_adapter_index,
    adapter_slot_index,
):
    owner_count = lax.axis_size("adapter")
    g = lax.axis_index("groups")
    height, depth = tokens.shape
    row_count = height * owner_count
    columns = base_up_weight.shape[1]
    rank_block = adapter_expand_weight.shape[1]
    rank = adapter_shrink_weight.shape[2]
    half_width = columns // 2
    block = column_block(columns)
    block_count = columns // block

    def from_owner(x, j):
        return lax.ppermute(x, "adapter", [(s, (s - j) % owner_count) for s in range(owner_count)])

    def from_either(x):
        pairs = []
        for group, j in ((0, 1), (1, 3)):
            for s in range(owner_count):
                pairs.append(
                    (group * owner_count + s, group * owner_count + (s - j) % owner_count)
                )
        return lax.ppermute(x, ("groups", "adapter"), pairs)

    def from_tensor(x, m):
        return lax.ppermute(x, "tensor", [(s, s ^ m) for s in range(4)])

    def from_mirror(x, m):
        return lax.ppermute(x, "adapter", [(s, s ^ m) for s in range(owner_count)])

    def from_group(x):
        return lax.ppermute(x, "groups", [(0, 1), (1, 0)])

    weight = pltpu.with_memory_space_constraint(base_up_weight, pltpu.HBM)
    expand = pltpu.with_memory_space_constraint(adapter_expand_weight, pltpu.HBM)
    offsets = (2, 1, 3)
    blocks = [from_owner(tokens, j) for j in offsets]

    cuts = [block_count * k // 14 for k in (0, 4, 8, 11, 14)]
    parts = list(zip(cuts[:-1], cuts[1:]))
    loads = [block_count * k // 14 for k in (0, 5, 8, 11, 14, 14)]
    bands = 4
    small = [
        pltpu.with_memory_space_constraint(x, pltpu.HBM)
        for x in (
            adapter_slot_index.reshape(1, owner_count),
            row_adapter_index.reshape(1, row_count),
            tokens,
            adapter_shrink_weight[0].T,
        )
    ]
    whole, half, own, slots, index, mine, shrink, held = kernel_call(
        functools.partial(cut_kernel, block, range(loads[1]), len(small)),
        "cut_expand",
        1,
        1,
        1,
        in_specs=[anywhere] * (2 + len(small)),
        out_specs=[vmem] * (4 + len(small)),
        out_shape=[pltpu.VMEM((rank_block, w), bf16) for w in (columns, half_width, columns)]
        + [pltpu.VMEM(x.shape, x.dtype) for x in small]
        + [pltpu.VMEM((loads[1], depth, block), bf16)],
        scratch_shapes=[
            pltpu.SemaphoreType.DMA((3 + len(small),)),
            pltpu.SemaphoreType.DMA((loads[1], bands)),
        ],
    )(expand, weight, *small)
    loaded = [held]
    whole = from_either(whole)

    rows, keep, send, slot = kernel_call(
        functools.partial(gather_kernel, (0, *offsets)),
        "gather_rows",
        1,
        1,
        4,
        in_specs=[vmem] * (owner_count + 3),
        out_specs=[vmem] * 4,
        out_shape=[jax.ShapeDtypeStruct((row_count, depth), bf16)]
        + [jax.ShapeDtypeStruct((rank // 2, row_count), f32)] * 2
        + [jax.ShapeDtypeStruct((1, row_count), jnp.int32)],
        scratch_shapes=[pltpu.VMEM((row_count, depth), bf16), pltpu.VMEM((rank, row_count), f32)],
    )(
        slots,
        index,
        mine,
        *blocks,
        shrink,
    )

    def base_part(n, *after):
        first, last = parts[n]
        numbers = range(loads[n + 1], loads[n + 2])
        places, used = [], []
        for number in range(first, last):
            source = max(k for k in range(len(loads) - 1) if loads[k] <= number)
            if source not in used:
                used.append(source)
            places.append((used.index(source), number - loads[source]))
        out = kernel_call(
            functools.partial(base_kernel, block, places, numbers),
            "base_part",
            (2 * 10**9, 10**10, 1, 1)[n],
            1,
            4,
            in_specs=[vmem, anywhere] + [vmem] * len(used) + [anywhere] * len(after),
            out_specs=[vmem] * (2 if numbers else 1),
            out_shape=[jax.ShapeDtypeStruct((row_count, (last - first) * block), f32)]
            + ([pltpu.VMEM((len(numbers), depth, block), bf16)] if numbers else []),
            scratch_shapes=[pltpu.SemaphoreType.DMA((len(numbers), bands))] if numbers else [],
        )(rows, weight, *[loaded[k] for k in used], *after)
        loaded.append(out[-1])
        return out[0]

    half, send = lax.optimization_barrier((half, send))
    arrived = from_tensor(send, 1)
    half = from_owner(half, 2)
    pair = keep + arrived
    arrived = from_tensor(pair[rank_block:], 2)
    bases = [base_part(0, pair)]
    arrived, whole, bases[0] = lax.optimization_barrier((arrived, whole, bases[0]))
    shrunk = (adapter_scale * (pair[:rank_block] + arrived)).astype(bf16)
    arrived = from_mirror(shrunk, 1)
    far_whole = from_group(whole)
    bases.append(base_part(1, shrunk))
    arrived, half, bases[1] = lax.optimization_barrier((arrived, half, bases[1]))
    shrunk = shrunk + arrived
    arrived = from_mirror(shrunk, 2)
    far_half = from_group(half)
    bases.append(base_part(2, shrunk))
    arrived, bases[2] = lax.optimization_barrier((arrived, bases[2]))
    shrunk = shrunk + arrived
    bases.append(base_part(3, shrunk))

    middle = block_count // 2 * block
    splits = [(0, middle), (middle, columns)]
    widths = [last - first for first, last in splits]
    quarter = row_count // 4
    out = kernel_call(
        functools.partial(delta_kernel, block, splits),
        "add_delta",
        1,
        1,
        8,
        in_specs=[vmem] * (len(bases) + 7),
        out_specs=[vmem] * (2 + 2 * len(splits)),
        out_shape=[
            jax.ShapeDtypeStruct((quarter, w), f32) for w in (columns, columns, *widths, *widths)
        ],
        scratch_shapes=[
            pltpu.VMEM((row_count, rank_block * owner_count), f32),
            pltpu.VMEM((row_count, rank_block * owner_count), bf16),
            pltpu.VMEM((rank_block, columns), bf16),
        ],
    )(slot, *bases, own, shrunk, whole, half, far_whole, far_half)
    own_keep, own_send = out[:2]
    crossed = []
    for keep, send in zip(out[2:4], out[4:6]):
        crossed.append(from_tensor((keep + from_tensor(send, 1)).astype(bf16), 2))
    kept = own_keep + from_tensor(own_send, 1)
    return jnp.concatenate(
        [
            (kept[:, first:last] + part.astype(f32)).astype(bf16)
            for (first, last), part in zip(splits, crossed)
        ],
        axis=1,
    )


def on_device(tokens, base_up_weight, adapter_shrink_weight, adapter_expand_weight, *index):
    pairs = lax.axis_size("groups") == 2 and lax.axis_size("tensor") == 4
    few = lax.axis_size("adapter") == 4
    columns = base_up_weight.shape[1]
    even = columns % 512 == 0 and columns >= 4096 and tokens.shape[0] % 16 == 0
    arrange = paired if pairs and few and even else general
    return arrange(
        tokens, base_up_weight, adapter_shrink_weight, adapter_expand_weight, *index
    )


def solution(mesh):
    placed = (
        P(("groups", "adapter"), "tensor"),
        P("tensor", "adapter"),
        P("adapter", "tensor", None),
        P("adapter", "tensor", None),
        P("groups", None),
        P(),
    )
    return jax.shard_map(
        on_device,
        mesh=mesh,
        in_specs=placed,
        out_specs=P(("groups", "tensor"), "adapter"),
        check_vma=False,
    )
```

```python
import functools

import jax
import jax.numpy as jnp
from jax import lax
from jax.experimental import pallas as pl
from jax.experimental.pallas import tpu as pltpu
from jax.sharding import PartitionSpec as P

adapter_scale = 0.5
lane = 128
f32 = jnp.float32
bf16 = jnp.bfloat16


def general(
    tokens,
    base_up_weight,
    adapter_shrink_weight,
    adapter_expand_weight,
    row_adapter_index,
    adapter_slot_index,
):
    owner_count = lax.axis_size("adapter")
    owner_index = lax.axis_index("adapter")
    tensor_index = lax.axis_index("tensor")
    rank_block = adapter_expand_weight.shape[1]
    columns = base_up_weight.shape[1]
    slot = jnp.take(adapter_slot_index, row_adapter_index[:, 0], axis=0)
    rows = lax.all_gather(tokens, "adapter", axis=0, tiled=True)
    expand = adapter_expand_weight[0].reshape(rank_block, owner_count, columns)
    expand = lax.all_to_all(expand, "adapter", split_axis=1, concat_axis=1, tiled=True)
    shrunk = jnp.dot(rows, adapter_shrink_weight[0], preferred_element_type=f32)
    shrunk = jnp.where((slot == owner_index)[:, None], shrunk, 0.0)
    shrunk = lax.psum(shrunk, ("adapter", "tensor"))
    shrunk = (adapter_scale * shrunk).astype(bf16)
    shrunk = lax.dynamic_slice_in_dim(shrunk, tensor_index * rank_block, rank_block, 1)
    chosen = slot[:, None] == jnp.arange(owner_count, dtype=jnp.int32)[None, :]
    spread = jnp.where(chosen[:, None, :], shrunk[:, :, None], jnp.zeros((), bf16))
    total = jnp.dot(rows, base_up_weight, preferred_element_type=f32)
    total = total + jnp.dot(
        spread.reshape(-1, rank_block * owner_count),
        expand.reshape(rank_block * owner_count, columns),
        preferred_element_type=f32,
    )
    return lax.psum_scatter(total, "tensor", scatter_dimension=0, tiled=True).astype(bf16)


vmem = pl.BlockSpec(memory_space=pltpu.VMEM)
anywhere = pl.BlockSpec(memory_space=pl.ANY)


def kernel_call(kernel, name, flops, moved, mib, **specs):
    return pl.pallas_call(
        kernel,
        cost_estimate=pl.CostEstimate(flops=flops, bytes_accessed=moved, transcendentals=0),
        compiler_params=pltpu.CompilerParams(vmem_limit_bytes=mib << 20),
        name=name,
        **specs,
    )


def cut_kernel(block, numbers, small_count, expand, weight, *refs):
    small, refs = refs[:small_count], refs[small_count:]
    whole, half, own, *loaded, held, sem, held_sem = refs
    g, a = lax.axis_index("groups"), lax.axis_index("adapter")
    columns, half_width = whole.shape[1], half.shape[1]
    firsts = (
        lax.bitwise_xor(a, 2 + g) * columns,
        lax.bitwise_xor(a, 1) * columns + g * half_width,
        a * columns,
    )
    copies = []
    for n, (first, target) in enumerate(zip(firsts, (whole, half, own))):
        span = pl.ds(pl.multiple_of(first, lane), target.shape[1])
        copies.append(pltpu.make_async_copy(expand.at[0, :, span], target, sem.at[n]))
    for n, (source, target) in enumerate(zip(small, loaded)):
        copies.append(pltpu.make_async_copy(source, target, sem.at[len(firsts) + n]))
    copies += weight_copies(block, numbers, weight, held, held_sem)
    for copy in copies:
        copy.start()
    for copy in copies:
        copy.wait()


def weight_copies(block, numbers, weight, target, sem):
    band_count = sem.shape[1]
    band = weight.shape[0] // band_count
    copies = []
    for n, number in enumerate(numbers):
        span = pl.ds(number * block, block)
        for m in range(band_count):
            rows = pl.ds(m * band, band)
            copies.append(
                pltpu.make_async_copy(weight.at[rows, span], target.at[n, rows], sem.at[n, m])
            )
    return copies


def gather_kernel(offsets, slots, index, *refs):
    owner_count = len(offsets)
    blocks = refs[:owner_count]
    shrink, rows_out, keep, send, slot_out, rows, partial = refs[owner_count:]
    a, t = lax.axis_index("adapter"), lax.axis_index("tensor")
    height, depth = blocks[0].shape
    for j, part in zip(offsets, blocks):
        where = lax.bitwise_xor(a, j)
        rows[pl.ds(pl.multiple_of(where * height, height), height), :] = part[:, :depth]
    quarter = rows.shape[0] // 4
    for i, flip in enumerate((0, 2, 1, 3)):
        start = pl.multiple_of(lax.bitwise_xor(t, flip) * quarter, quarter)
        rows_out[i * quarter : (i + 1) * quarter, :] = rows[pl.ds(start, quarter), :]
    product = lax.dot_general(
        shrink[...], rows[...], (((1,), (1,)), ((), ())), preferred_element_type=f32
    )
    named, table = index[...], slots[...]
    slot = jnp.zeros_like(named)
    for k in range(table.shape[1]):
        slot = jnp.where(named == k, table[:, k : k + 1], slot)
    slot_out[...] = slot
    partial[...] = jnp.where(slot == a, product, 0.0)
    rank_block = partial.shape[0] // 4
    for i, flip in enumerate((0, 2, 1, 3)):
        start = pl.multiple_of(lax.bitwise_xor(t, flip) * rank_block, rank_block)
        target = keep if i < 2 else send
        at = i % 2 * rank_block
        target[at : at + rank_block, :] = partial[pl.ds(start, rank_block), :]


def base_kernel(block, places, numbers, streamed, rows, weight, *refs):
    total, ahead, sem = refs[-3:]
    copies = weight_copies(block, numbers, weight, ahead, sem)
    for copy in copies:
        copy.start()

    @pl.when(lax.axis_index("tensor") >= 0)
    def _():
        for n, (which, index) in enumerate(places):
            total[:, n * block : (n + 1) * block] = jnp.dot(
                rows[...], refs[which][index], preferred_element_type=f32
            )

    bands = sem.shape[1]
    for n in range(len(numbers)):
        for copy in copies[n * bands : (n + 1) * bands]:
            copy.wait()
        if streamed:
            at = (len(places) + n) * block
            total[:, at : at + block] = jnp.dot(
                rows[...], ahead[n], preferred_element_type=f32
            )


def delta_kernel(block, splits, slot, *refs):
    bases, refs = refs[: -len(splits) * 2 - 11], refs[-len(splits) * 2 - 11 :]
    own, shrunk, whole, half, far_whole, far_half, own_keep, own_send = refs[:8]
    cross_keep, cross_send = refs[8 : 8 + len(splits)], refs[8 + len(splits) : 8 + 2 * len(splits)]
    flat, ordered, two = refs[-3:]
    g, a, t = (lax.axis_index(name) for name in ("groups", "adapter", "tensor"))
    row_count = bases[0].shape[0]
    quarter = row_count // 4
    half_width = half.shape[1]

    @pl.when(g == 0)
    def _():
        two[:, :half_width] = half[...]
        two[:, half_width:] = far_half[...]

    @pl.when(g != 0)
    def _():
        two[:, :half_width] = far_half[...]
        two[:, half_width:] = half[...]

    merged = shrunk[...].astype(f32)
    spread = [
        jnp.where(slot[...] == lax.bitwise_xor(a, j), merged, 0.0)
        for j in (0, 2 + g, 3 - g, 1)
    ]
    flat[...] = jnp.concatenate(spread, axis=0).T
    for i, turn in enumerate((0, 2, 1, 3)):
        start = pl.multiple_of(lax.bitwise_xor(t, turn) * quarter, quarter)
        ordered[i * quarter : (i + 1) * quarter, :] = flat[pl.ds(start, quarter), :].astype(bf16)
    left = ordered[...]
    at, split = 0, 0
    for base in bases:
        for column in range(0, base.shape[1], block):
            span = slice(at, at + block)
            expand = jnp.concatenate(
                [own[:, span], whole[:, span], far_whole[:, span], two[:, span]], axis=0
            )
            total = base[:, column : column + block] + jnp.dot(
                left, expand, preferred_element_type=f32
            )
            if at >= splits[split][1]:
                split += 1
            here = slice(at - splits[split][0], at - splits[split][0] + block)
            own_keep[:, span] = total[:quarter]
            cross_keep[split][:, here] = total[quarter : 2 * quarter]
            own_send[:, span] = total[2 * quarter : 3 * quarter]
            cross_send[split][:, here] = total[3 * quarter :]
            at += block


def column_block(width):
    for size in (512, 256, 128):
        if width % size == 0:
            return size


def paired(
    tokens,
    base_up_weight,
    adapter_shrink_weight,
    adapter_expand_weight,
    row_adapter_index,
    adapter_slot_index,
):
    owner_count = lax.axis_size("adapter")
    g = lax.axis_index("groups")
    height, depth = tokens.shape
    row_count = height * owner_count
    columns = base_up_weight.shape[1]
    rank_block = adapter_expand_weight.shape[1]
    rank = adapter_shrink_weight.shape[2]
    half_width = columns // 2
    block = column_block(columns)
    block_count = columns // block

    def from_owner(x, first, second):
        pairs = []
        for group, m in ((0, first), (1, second)):
            for s in range(owner_count):
                pairs.append((group * owner_count + s, group * owner_count + (s ^ m)))
        return lax.ppermute(x, ("groups", "adapter"), pairs)

    def from_tensor(x, m):
        return lax.ppermute(x, "tensor", [(s, s ^ m) for s in range(4)])

    def from_group(x):
        return lax.ppermute(x, "groups", [(0, 1), (1, 0)])

    weight = pltpu.with_memory_space_constraint(base_up_weight, pltpu.HBM)
    expand = pltpu.with_memory_space_constraint(adapter_expand_weight, pltpu.HBM)
    offsets = (2, 3, 1)
    blocks = [from_owner(tokens, j, j) for j in offsets]

    cuts = [block_count * k // 14 for k in (0, 4, 8, 11, 14)]
    parts = list(zip(cuts[:-1], cuts[1:]))
    loads = [block_count * k // 14 for k in (0, 4, 8, 11, 12, 14)]
    bands = 4
    small = [
        pltpu.with_memory_space_constraint(x, pltpu.HBM)
        for x in (
            adapter_slot_index.reshape(1, owner_count),
            row_adapter_index.reshape(1, row_count),
            tokens,
            adapter_shrink_weight[0].T,
        )
    ]
    whole, half, own, slots, index, mine, shrink, held = kernel_call(
        functools.partial(cut_kernel, block, range(loads[1]), len(small)),
        "cut_expand",
        1,
        1,
        1,
        in_specs=[anywhere] * (2 + len(small)),
        out_specs=[vmem] * (4 + len(small)),
        out_shape=[pltpu.VMEM((rank_block, w), bf16) for w in (columns, half_width, columns)]
        + [pltpu.VMEM(x.shape, x.dtype) for x in small]
        + [pltpu.VMEM((loads[1], depth, block), bf16)],
        scratch_shapes=[
            pltpu.SemaphoreType.DMA((3 + len(small),)),
            pltpu.SemaphoreType.DMA((loads[1], bands)),
        ],
    )(expand, weight, *small)
    loaded = [held]
    whole, half = from_owner(whole, 2, 3), from_owner(half, 1, 1)

    rows, keep, send, slot = kernel_call(
        functools.partial(gather_kernel, (0, *offsets)),
        "gather_rows",
        1,
        1,
        4,
        in_specs=[vmem] * (owner_count + 3),
        out_specs=[vmem] * 4,
        out_shape=[jax.ShapeDtypeStruct((row_count, depth), bf16)]
        + [jax.ShapeDtypeStruct((rank // 2, row_count), f32)] * 2
        + [jax.ShapeDtypeStruct((1, row_count), jnp.int32)],
        scratch_shapes=[pltpu.VMEM((row_count, depth), bf16), pltpu.VMEM((rank, row_count), f32)],
    )(
        slots,
        index,
        mine,
        *blocks,
        shrink,
    )

    def base_part(n, *after):
        first, last = parts[n]
        streamed = n + 1 == len(parts)
        numbers = range(loads[n + 1], loads[n + 2])
        places, used = [], []
        for number in range(first, numbers[0] if streamed else last):
            source = max(k for k in range(len(loads) - 1) if loads[k] <= number)
            if source not in used:
                used.append(source)
            places.append((used.index(source), number - loads[source]))
        near = n < 2
        ahead = pltpu.VMEM((len(numbers), depth, block), bf16)
        out = kernel_call(
            functools.partial(base_kernel, block, places, numbers, streamed),
            "base_part",
            3 * 2 * row_count * depth * (last - first) * block if near else 1,
            3 * 2 * depth * (last - first) * block if near else 1,
            12,
            in_specs=[vmem, anywhere] + [vmem] * len(used) + [anywhere] * len(after),
            out_specs=[vmem] * (1 if streamed else 2),
            out_shape=[jax.ShapeDtypeStruct((row_count, (last - first) * block), f32)]
            + ([] if streamed else [ahead]),
            scratch_shapes=([ahead] if streamed else [])
            + [pltpu.SemaphoreType.DMA((len(numbers), bands))],
        )(rows, weight, *[loaded[k] for k in used], *after)
        loaded.append(out[-1])
        return out[0]

    arrived = from_tensor(send, 1)
    base_0 = base_part(0, send)
    arrived, base_0 = lax.optimization_barrier((arrived, base_0))
    pair = keep + arrived
    arrived = from_tensor(pair[rank_block:], 2)
    base_1 = base_part(1, pair)
    arrived, base_1, whole, half = lax.optimization_barrier((arrived, base_1, whole, half))
    shrunk = (adapter_scale * (pair[:rank_block] + arrived)).astype(bf16)
    far_whole, far_half = from_group(whole), from_group(half)
    bases = [base_0, base_1]
    for m, n in ((1, 2), (2, 3)):
        arrived = from_owner(shrunk, m, m)
        base = base_part(n, shrunk, whole, half)
        arrived, base = lax.optimization_barrier((arrived, base))
        bases.append(base)
        shrunk = shrunk + arrived

    middle = block_count // 2 * block
    splits = [(0, middle), (middle, columns)]
    widths = [last - first for first, last in splits]
    quarter = row_count // 4
    out = kernel_call(
        functools.partial(delta_kernel, block, splits),
        "add_delta",
        1,
        1,
        8,
        in_specs=[vmem] * (len(bases) + 7),
        out_specs=[vmem] * (2 + 2 * len(splits)),
        out_shape=[
            jax.ShapeDtypeStruct((quarter, w), f32) for w in (columns, columns, *widths, *widths)
        ],
        scratch_shapes=[
            pltpu.VMEM((row_count, rank_block * owner_count), f32),
            pltpu.VMEM((row_count, rank_block * owner_count), bf16),
            pltpu.VMEM((rank_block, columns), bf16),
        ],
    )(slot, *bases, own, shrunk, whole, half, far_whole, far_half)
    own_keep, own_send = out[:2]
    crossed = []
    for keep, send in zip(out[2:4], out[4:6]):
        crossed.append(from_tensor((keep + from_tensor(send, 1)).astype(bf16), 2))
    kept = own_keep + from_tensor(own_send, 1)
    return jnp.concatenate(
        [
            (kept[:, first:last] + part.astype(f32)).astype(bf16)
            for (first, last), part in zip(splits, crossed)
        ],
        axis=1,
    )


def on_device(tokens, base_up_weight, adapter_shrink_weight, adapter_expand_weight, *index):
    pairs = lax.axis_size("groups") == 2 and lax.axis_size("tensor") == 4
    few = lax.axis_size("adapter") == 4
    columns = base_up_weight.shape[1]
    even = columns % 512 == 0 and columns >= 4096 and tokens.shape[0] % 16 == 0
    arrange = paired if pairs and few and even else general
    return arrange(
        tokens, base_up_weight, adapter_shrink_weight, adapter_expand_weight, *index
    )


def solution(mesh):
    placed = (
        P(("groups", "adapter"), "tensor"),
        P("tensor", "adapter"),
        P("adapter", "tensor", None),
        P("adapter", "tensor", None),
        P("groups", None),
        P(),
    )
    return jax.shard_map(
        on_device,
        mesh=mesh,
        in_specs=placed,
        out_specs=P(("groups", "tensor"), "adapter"),
        check_vma=False,
    )
```

```python
import functools

import jax
import jax.numpy as jnp
from jax import lax
from jax.experimental import pallas as pl
from jax.experimental.pallas import tpu as pltpu
from jax.sharding import PartitionSpec as P

adapter_scale = 0.5
lane = 128
f32 = jnp.float32
bf16 = jnp.bfloat16


def general(
    tokens,
    base_up_weight,
    adapter_shrink_weight,
    adapter_expand_weight,
    row_adapter_index,
    adapter_slot_index,
):
    owner_count = lax.axis_size("adapter")
    owner_index = lax.axis_index("adapter")
    tensor_index = lax.axis_index("tensor")
    rank_block = adapter_expand_weight.shape[1]
    columns = base_up_weight.shape[1]
    slot = jnp.take(adapter_slot_index, row_adapter_index[:, 0], axis=0)
    rows = lax.all_gather(tokens, "adapter", axis=0, tiled=True)
    expand = adapter_expand_weight[0].reshape(rank_block, owner_count, columns)
    expand = lax.all_to_all(expand, "adapter", split_axis=1, concat_axis=1, tiled=True)
    shrunk = jnp.dot(rows, adapter_shrink_weight[0], preferred_element_type=f32)
    shrunk = jnp.where((slot == owner_index)[:, None], shrunk, 0.0)
    shrunk = lax.psum(shrunk, ("adapter", "tensor"))
    shrunk = (adapter_scale * shrunk).astype(bf16)
    shrunk = lax.dynamic_slice_in_dim(shrunk, tensor_index * rank_block, rank_block, 1)
    chosen = slot[:, None] == jnp.arange(owner_count, dtype=jnp.int32)[None, :]
    spread = jnp.where(chosen[:, None, :], shrunk[:, :, None], jnp.zeros((), bf16))
    total = jnp.dot(rows, base_up_weight, preferred_element_type=f32)
    total = total + jnp.dot(
        spread.reshape(-1, rank_block * owner_count),
        expand.reshape(rank_block * owner_count, columns),
        preferred_element_type=f32,
    )
    return lax.psum_scatter(total, "tensor", scatter_dimension=0, tiled=True).astype(bf16)


vmem = pl.BlockSpec(memory_space=pltpu.VMEM)
anywhere = pl.BlockSpec(memory_space=pl.ANY)


def kernel_call(kernel, name, flops, moved, mib, **specs):
    return pl.pallas_call(
        kernel,
        cost_estimate=pl.CostEstimate(flops=flops, bytes_accessed=moved, transcendentals=0),
        compiler_params=pltpu.CompilerParams(vmem_limit_bytes=mib << 20),
        name=name,
        **specs,
    )


def cut_kernel(block, numbers, small_count, expand, weight, *refs):
    small, refs = refs[:small_count], refs[small_count:]
    across, beside, own, *loaded, held, sem, held_sem = refs
    g, a = lax.axis_index("groups"), lax.axis_index("adapter")
    columns = own.shape[1]
    firsts = (
        lax.bitwise_xor(a, 2 + g) * columns,
        lax.bitwise_xor(a, 1) * columns,
        a * columns,
    )
    copies = []
    for n, (first, target) in enumerate(zip(firsts, (across, beside, own))):
        span = pl.ds(pl.multiple_of(first, lane), columns)
        copies.append(pltpu.make_async_copy(expand.at[0, :, span], target, sem.at[n]))
    for n, (source, target) in enumerate(zip(small, loaded)):
        copies.append(pltpu.make_async_copy(source, target, sem.at[len(firsts) + n]))
    copies += weight_copies(block, numbers, weight, held, held_sem)
    for copy in copies:
        copy.start()
    for copy in copies:
        copy.wait()


def weight_copies(block, numbers, weight, target, sem):
    band_count = sem.shape[1]
    band = weight.shape[0] // band_count
    copies = []
    for n, number in enumerate(numbers):
        span = pl.ds(number * block, block)
        for m in range(band_count):
            rows = pl.ds(m * band, band)
            copies.append(
                pltpu.make_async_copy(weight.at[rows, span], target.at[n, rows], sem.at[n, m])
            )
    return copies


def gather_kernel(offsets, slots, index, *refs):
    owner_count = len(offsets)
    blocks = refs[:owner_count]
    shrink, rows_out, keep, send, slot_out, rows, partial = refs[owner_count:]
    a, t = lax.axis_index("adapter"), lax.axis_index("tensor")
    height, depth = blocks[0].shape
    for j, part in zip(offsets, blocks):
        where = lax.bitwise_xor(a, j)
        rows[pl.ds(pl.multiple_of(where * height, height), height), :] = part[:, :depth]
    quarter = rows.shape[0] // 4
    for i, flip in enumerate((0, 2, 1, 3)):
        start = pl.multiple_of(lax.bitwise_xor(t, flip) * quarter, quarter)
        rows_out[i * quarter : (i + 1) * quarter, :] = rows[pl.ds(start, quarter), :]
    product = lax.dot_general(
        shrink[...], rows[...], (((1,), (1,)), ((), ())), preferred_element_type=f32
    )
    named, table = index[...], slots[...]
    slot = jnp.zeros_like(named)
    for k in range(table.shape[1]):
        slot = jnp.where(named == k, table[:, k : k + 1], slot)
    slot_out[...] = slot
    partial[...] = jnp.where(slot == a, product, 0.0)
    rank_block = partial.shape[0] // 4
    for i, flip in enumerate((0, 2, 1, 3)):
        start = pl.multiple_of(lax.bitwise_xor(t, flip) * rank_block, rank_block)
        target = keep if i < 2 else send
        at = i % 2 * rank_block
        target[at : at + rank_block, :] = partial[pl.ds(start, rank_block), :]


def base_kernel(block, places, numbers, streamed, rows, weight, *refs):
    total, ahead, sem = refs[-3:]
    copies = weight_copies(block, numbers, weight, ahead, sem)
    for copy in copies:
        copy.start()

    @pl.when(lax.axis_index("tensor") >= 0)
    def _():
        for n, (which, index) in enumerate(places):
            total[:, n * block : (n + 1) * block] = jnp.dot(
                rows[...], refs[which][index], preferred_element_type=f32
            )

    bands = sem.shape[1]
    for n in range(len(numbers)):
        for copy in copies[n * bands : (n + 1) * bands]:
            copy.wait()
        if streamed:
            at = (len(places) + n) * block
            total[:, at : at + block] = jnp.dot(
                rows[...], ahead[n], preferred_element_type=f32
            )


def delta_kernel(block, splits, slot, *refs):
    bases, refs = refs[: -len(splits) * 2 - 9], refs[-len(splits) * 2 - 9 :]
    own, shrunk, across, beside, swapped, own_keep, own_send = refs[:7]
    cross_keep, cross_send = refs[7 : 7 + len(splits)], refs[7 + len(splits) : 7 + 2 * len(splits)]
    flat, ordered = refs[-2:]
    g, a, t = (lax.axis_index(name) for name in ("groups", "adapter", "tensor"))
    row_count = bases[0].shape[0]
    quarter = row_count // 4
    merged = shrunk[...].astype(f32)
    spread = [
        jnp.where(slot[...] == lax.bitwise_xor(a, j), merged, 0.0)
        for j in (0, 2 + g, 1, 3 - g)
    ]
    flat[...] = jnp.concatenate(spread, axis=0).T
    for i, turn in enumerate((0, 2, 1, 3)):
        start = pl.multiple_of(lax.bitwise_xor(t, turn) * quarter, quarter)
        ordered[i * quarter : (i + 1) * quarter, :] = flat[pl.ds(start, quarter), :].astype(bf16)
    left = ordered[...]
    at, split = 0, 0
    for base in bases:
        for column in range(0, base.shape[1], block):
            span = slice(at, at + block)
            expand = jnp.concatenate(
                [own[:, span], across[:, span], beside[:, span], swapped[:, span]], axis=0
            )
            total = base[:, column : column + block] + jnp.dot(
                left, expand, preferred_element_type=f32
            )
            if at >= splits[split][1]:
                split += 1
            here = slice(at - splits[split][0], at - splits[split][0] + block)
            own_keep[:, span] = total[:quarter]
            cross_keep[split][:, here] = total[quarter : 2 * quarter]
            own_send[:, span] = total[2 * quarter : 3 * quarter]
            cross_send[split][:, here] = total[3 * quarter :]
            at += block


def column_block(width):
    for size in (512, 256, 128):
        if width % size == 0:
            return size


def paired(
    tokens,
    base_up_weight,
    adapter_shrink_weight,
    adapter_expand_weight,
    row_adapter_index,
    adapter_slot_index,
):
    owner_count = lax.axis_size("adapter")
    g = lax.axis_index("groups")
    height, depth = tokens.shape
    row_count = height * owner_count
    columns = base_up_weight.shape[1]
    rank_block = adapter_expand_weight.shape[1]
    rank = adapter_shrink_weight.shape[2]
    block = column_block(columns)
    block_count = columns // block

    def from_owner(x, first, second):
        pairs = []
        for group, m in ((0, first), (1, second)):
            for s in range(owner_count):
                pairs.append((group * owner_count + s, group * owner_count + (s ^ m)))
        return lax.ppermute(x, ("groups", "adapter"), pairs)

    def from_tensor(x, m):
        return lax.ppermute(x, "tensor", [(s, s ^ m) for s in range(4)])

    def from_group(x):
        return lax.ppermute(x, "groups", [(0, 1), (1, 0)])

    weight = pltpu.with_memory_space_constraint(base_up_weight, pltpu.HBM)
    expand = pltpu.with_memory_space_constraint(adapter_expand_weight, pltpu.HBM)
    offsets = (2, 3, 1)
    blocks = [from_owner(tokens, j, j) for j in offsets]

    cuts = [block_count * k // 14 for k in (0, 4, 8, 11, 14)]
    parts = list(zip(cuts[:-1], cuts[1:]))
    loads = [block_count * k // 14 for k in (0, 4, 8, 11, 12, 14)]
    bands = 4
    small = [
        pltpu.with_memory_space_constraint(x, pltpu.HBM)
        for x in (
            adapter_slot_index.reshape(1, owner_count),
            row_adapter_index.reshape(1, row_count),
            tokens,
            adapter_shrink_weight[0].T,
        )
    ]
    across, beside, own, slots, index, mine, shrink, held = kernel_call(
        functools.partial(cut_kernel, block, range(loads[1]), len(small)),
        "cut_expand",
        1,
        1,
        1,
        in_specs=[anywhere] * (2 + len(small)),
        out_specs=[vmem] * (4 + len(small)),
        out_shape=[pltpu.VMEM((rank_block, w), bf16) for w in (columns,) * 3]
        + [pltpu.VMEM(x.shape, x.dtype) for x in small]
        + [pltpu.VMEM((loads[1], depth, block), bf16)],
        scratch_shapes=[
            pltpu.SemaphoreType.DMA((3 + len(small),)),
            pltpu.SemaphoreType.DMA((loads[1], bands)),
        ],
    )(expand, weight, *small)
    loaded = [held]
    across = from_owner(across, 2, 3)

    rows, keep, send, slot = kernel_call(
        functools.partial(gather_kernel, (0, *offsets)),
        "gather_rows",
        1,
        1,
        4,
        in_specs=[vmem] * (owner_count + 3),
        out_specs=[vmem] * 4,
        out_shape=[jax.ShapeDtypeStruct((row_count, depth), bf16)]
        + [jax.ShapeDtypeStruct((rank // 2, row_count), f32)] * 2
        + [jax.ShapeDtypeStruct((1, row_count), jnp.int32)],
        scratch_shapes=[pltpu.VMEM((row_count, depth), bf16), pltpu.VMEM((rank, row_count), f32)],
    )(
        slots,
        index,
        mine,
        *blocks,
        shrink,
    )

    def base_part(n, *after):
        first, last = parts[n]
        streamed = n + 1 == len(parts)
        numbers = range(loads[n + 1], loads[n + 2])
        places, used = [], []
        for number in range(first, numbers[0] if streamed else last):
            source = max(k for k in range(len(loads) - 1) if loads[k] <= number)
            if source not in used:
                used.append(source)
            places.append((used.index(source), number - loads[source]))
        near = n < 2
        ahead = pltpu.VMEM((len(numbers), depth, block), bf16)
        out = kernel_call(
            functools.partial(base_kernel, block, places, numbers, streamed),
            "base_part",
            3 * 2 * row_count * depth * (last - first) * block if near else 1,
            3 * 2 * depth * (last - first) * block if near else 1,
            12,
            in_specs=[vmem, anywhere] + [vmem] * len(used) + [anywhere] * len(after),
            out_specs=[vmem] * (1 if streamed else 2),
            out_shape=[jax.ShapeDtypeStruct((row_count, (last - first) * block), f32)]
            + ([] if streamed else [ahead]),
            scratch_shapes=([ahead] if streamed else [])
            + [pltpu.SemaphoreType.DMA((len(numbers), bands))],
        )(rows, weight, *[loaded[k] for k in used], *after)
        loaded.append(out[-1])
        return out[0]

    arrived = from_tensor(send, 1)
    base_0 = base_part(0, send)
    arrived, base_0 = lax.optimization_barrier((arrived, base_0))
    pair = keep + arrived
    arrived = from_tensor(pair[rank_block:], 2)
    base_1 = base_part(1, pair)
    arrived, base_1, across = lax.optimization_barrier((arrived, base_1, across))
    shrunk = (adapter_scale * (pair[:rank_block] + arrived)).astype(bf16)
    swapped = from_group(across)
    beside, shrunk = lax.optimization_barrier((beside, shrunk))
    beside = from_owner(beside, 1, 1)
    bases = [base_0, base_1]
    for m, n in ((1, 2), (2, 3)):
        arrived = from_owner(shrunk, m, m)
        base = base_part(n, shrunk, across)
        arrived, base = lax.optimization_barrier((arrived, base))
        bases.append(base)
        shrunk = shrunk + arrived

    middle = block_count // 2 * block
    splits = [(0, middle), (middle, columns)]
    widths = [last - first for first, last in splits]
    quarter = row_count // 4
    out = kernel_call(
        functools.partial(delta_kernel, block, splits),
        "add_delta",
        1,
        1,
        8,
        in_specs=[vmem] * (len(bases) + 6),
        out_specs=[vmem] * (2 + 2 * len(splits)),
        out_shape=[
            jax.ShapeDtypeStruct((quarter, w), f32) for w in (columns, columns, *widths, *widths)
        ],
        scratch_shapes=[
            pltpu.VMEM((row_count, rank_block * owner_count), f32),
            pltpu.VMEM((row_count, rank_block * owner_count), bf16),
        ],
    )(slot, *bases, own, shrunk, across, beside, swapped)
    own_keep, own_send = out[:2]
    crossed = []
    for keep, send in zip(out[2:4], out[4:6]):
        crossed.append(from_tensor((keep + from_tensor(send, 1)).astype(bf16), 2))
    kept = own_keep + from_tensor(own_send, 1)
    return jnp.concatenate(
        [
            (kept[:, first:last] + part.astype(f32)).astype(bf16)
            for (first, last), part in zip(splits, crossed)
        ],
        axis=1,
    )


def on_device(tokens, base_up_weight, adapter_shrink_weight, adapter_expand_weight, *index):
    pairs = lax.axis_size("groups") == 2 and lax.axis_size("tensor") == 4
    few = lax.axis_size("adapter") == 4
    columns = base_up_weight.shape[1]
    even = columns % 512 == 0 and columns >= 4096 and tokens.shape[0] % 16 == 0
    arrange = paired if pairs and few and even else general
    return arrange(
        tokens, base_up_weight, adapter_shrink_weight, adapter_expand_weight, *index
    )


def solution(mesh):
    placed = (
        P(("groups", "adapter"), "tensor"),
        P("tensor", "adapter"),
        P("adapter", "tensor", None),
        P("adapter", "tensor", None),
        P("groups", None),
        P(),
    )
    return jax.shard_map(
        on_device,
        mesh=mesh,
        in_specs=placed,
        out_specs=P(("groups", "tensor"), "adapter"),
        check_vma=False,
    )
```

```python
import functools

import jax
import jax.numpy as jnp
from jax import lax
from jax.experimental import pallas as pl
from jax.experimental.pallas import tpu as pltpu
from jax.sharding import PartitionSpec as P

adapter_scale = 0.5
lane = 128
f32 = jnp.float32
bf16 = jnp.bfloat16


def general(
    tokens,
    base_up_weight,
    adapter_shrink_weight,
    adapter_expand_weight,
    row_adapter_index,
    adapter_slot_index,
):
    owner_count = lax.axis_size("adapter")
    owner_index = lax.axis_index("adapter")
    tensor_index = lax.axis_index("tensor")
    rank_block = adapter_expand_weight.shape[1]
    columns = base_up_weight.shape[1]
    slot = jnp.take(adapter_slot_index, row_adapter_index[:, 0], axis=0)
    rows = lax.all_gather(tokens, "adapter", axis=0, tiled=True)
    expand = adapter_expand_weight[0].reshape(rank_block, owner_count, columns)
    expand = lax.all_to_all(expand, "adapter", split_axis=1, concat_axis=1, tiled=True)
    shrunk = jnp.dot(rows, adapter_shrink_weight[0], preferred_element_type=f32)
    shrunk = jnp.where((slot == owner_index)[:, None], shrunk, 0.0)
    shrunk = lax.psum(shrunk, ("adapter", "tensor"))
    shrunk = (adapter_scale * shrunk).astype(bf16)
    shrunk = lax.dynamic_slice_in_dim(shrunk, tensor_index * rank_block, rank_block, 1)
    chosen = slot[:, None] == jnp.arange(owner_count, dtype=jnp.int32)[None, :]
    spread = jnp.where(chosen[:, None, :], shrunk[:, :, None], jnp.zeros((), bf16))
    total = jnp.dot(rows, base_up_weight, preferred_element_type=f32)
    total = total + jnp.dot(
        spread.reshape(-1, rank_block * owner_count),
        expand.reshape(rank_block * owner_count, columns),
        preferred_element_type=f32,
    )
    return lax.psum_scatter(total, "tensor", scatter_dimension=0, tiled=True).astype(bf16)


vmem = pl.BlockSpec(memory_space=pltpu.VMEM)
anywhere = pl.BlockSpec(memory_space=pl.ANY)


def kernel_call(kernel, name, flops, moved, mib, **specs):
    return pl.pallas_call(
        kernel,
        cost_estimate=pl.CostEstimate(flops=flops, bytes_accessed=moved, transcendentals=0),
        compiler_params=pltpu.CompilerParams(vmem_limit_bytes=mib << 20),
        name=name,
        **specs,
    )


def cut_kernel(block, numbers, small_count, expand, weight, *refs):
    small, refs = refs[:small_count], refs[small_count:]
    across, beside, own, *loaded, held, sem, held_sem = refs
    g, a = lax.axis_index("groups"), lax.axis_index("adapter")
    columns = own.shape[1]
    firsts = (
        lax.bitwise_xor(a, 2 + g) * columns,
        lax.bitwise_xor(a, 1) * columns,
        a * columns,
    )
    copies = []
    for n, (first, target) in enumerate(zip(firsts, (across, beside, own))):
        span = pl.ds(pl.multiple_of(first, lane), columns)
        copies.append(pltpu.make_async_copy(expand.at[0, :, span], target, sem.at[n]))
    for n, (source, target) in enumerate(zip(small, loaded)):
        copies.append(pltpu.make_async_copy(source, target, sem.at[len(firsts) + n]))
    copies += weight_copies(block, numbers, weight, held, held_sem)
    for copy in copies:
        copy.start()
    for copy in copies:
        copy.wait()


def weight_copies(block, numbers, weight, target, sem):
    band_count = sem.shape[1]
    band = weight.shape[0] // band_count
    copies = []
    for n, number in enumerate(numbers):
        span = pl.ds(number * block, block)
        for m in range(band_count):
            rows = pl.ds(m * band, band)
            copies.append(
                pltpu.make_async_copy(weight.at[rows, span], target.at[n, rows], sem.at[n, m])
            )
    return copies


def gather_kernel(offsets, slots, index, *refs):
    owner_count = len(offsets)
    blocks = refs[:owner_count]
    shrink, rows_out, keep, send, slot_out, rows, partial = refs[owner_count:]
    a, t = lax.axis_index("adapter"), lax.axis_index("tensor")
    height, depth = blocks[0].shape
    for j, part in zip(offsets, blocks):
        where = lax.bitwise_xor(a, j)
        rows[pl.ds(pl.multiple_of(where * height, height), height), :] = part[:, :depth]
    quarter = rows.shape[0] // 4
    for i, flip in enumerate((0, 2, 1, 3)):
        start = pl.multiple_of(lax.bitwise_xor(t, flip) * quarter, quarter)
        rows_out[i * quarter : (i + 1) * quarter, :] = rows[pl.ds(start, quarter), :]
    product = lax.dot_general(
        shrink[...], rows[...], (((1,), (1,)), ((), ())), preferred_element_type=f32
    )
    named, table = index[...], slots[...]
    slot = jnp.zeros_like(named)
    for k in range(table.shape[1]):
        slot = jnp.where(named == k, table[:, k : k + 1], slot)
    slot_out[...] = slot
    partial[...] = jnp.where(slot == a, product, 0.0)
    rank_block = partial.shape[0] // 4
    for i, flip in enumerate((0, 2, 1, 3)):
        start = pl.multiple_of(lax.bitwise_xor(t, flip) * rank_block, rank_block)
        target = keep if i < 2 else send
        at = i % 2 * rank_block
        target[at : at + rank_block, :] = partial[pl.ds(start, rank_block), :]


def base_kernel(block, places, numbers, streamed, rows, weight, *refs):
    total, ahead, sem = refs[-3:]
    copies = weight_copies(block, numbers, weight, ahead, sem)
    for copy in copies:
        copy.start()

    @pl.when(lax.axis_index("tensor") >= 0)
    def _():
        for n, (which, index) in enumerate(places):
            total[:, n * block : (n + 1) * block] = jnp.dot(
                rows[...], refs[which][index], preferred_element_type=f32
            )

    bands = sem.shape[1]
    for n in range(len(numbers)):
        for copy in copies[n * bands : (n + 1) * bands]:
            copy.wait()
        if streamed:
            at = (len(places) + n) * block
            total[:, at : at + block] = jnp.dot(
                rows[...], ahead[n], preferred_element_type=f32
            )


def delta_kernel(block, splits, slot, *refs):
    bases, refs = refs[: -len(splits) * 2 - 9], refs[-len(splits) * 2 - 9 :]
    own, shrunk, across, beside, swapped, own_keep, own_send = refs[:7]
    cross_keep, cross_send = refs[7 : 7 + len(splits)], refs[7 + len(splits) : 7 + 2 * len(splits)]
    flat, ordered = refs[-2:]
    g, a, t = (lax.axis_index(name) for name in ("groups", "adapter", "tensor"))
    row_count = bases[0].shape[0]
    quarter = row_count // 4
    merged = shrunk[...].astype(f32)
    spread = [
        jnp.where(slot[...] == lax.bitwise_xor(a, j), merged, 0.0)
        for j in (0, 2 + g, 1, 3 - g)
    ]
    flat[...] = jnp.concatenate(spread, axis=0).T
    for i, turn in enumerate((0, 2, 1, 3)):
        start = pl.multiple_of(lax.bitwise_xor(t, turn) * quarter, quarter)
        ordered[i * quarter : (i + 1) * quarter, :] = flat[pl.ds(start, quarter), :].astype(bf16)
    left = ordered[...]
    at, split = 0, 0
    for base in bases:
        for column in range(0, base.shape[1], block):
            span = slice(at, at + block)
            expand = jnp.concatenate(
                [own[:, span], across[:, span], beside[:, span], swapped[:, span]], axis=0
            )
            total = base[:, column : column + block] + jnp.dot(
                left, expand, preferred_element_type=f32
            )
            if at >= splits[split][1]:
                split += 1
            here = slice(at - splits[split][0], at - splits[split][0] + block)
            own_keep[:, span] = total[:quarter]
            cross_keep[split][:, here] = total[quarter : 2 * quarter]
            own_send[:, span] = total[2 * quarter : 3 * quarter]
            cross_send[split][:, here] = total[3 * quarter :]
            at += block


def column_block(width):
    for size in (512, 256, 128):
        if width % size == 0:
            return size


def paired(
    tokens,
    base_up_weight,
    adapter_shrink_weight,
    adapter_expand_weight,
    row_adapter_index,
    adapter_slot_index,
):
    owner_count = lax.axis_size("adapter")
    g = lax.axis_index("groups")
    height, depth = tokens.shape
    row_count = height * owner_count
    columns = base_up_weight.shape[1]
    rank_block = adapter_expand_weight.shape[1]
    rank = adapter_shrink_weight.shape[2]
    block = column_block(columns)
    block_count = columns // block

    def from_owner(x, first, second):
        pairs = []
        for group, m in ((0, first), (1, second)):
            for s in range(owner_count):
                pairs.append((group * owner_count + s, group * owner_count + (s ^ m)))
        return lax.ppermute(x, ("groups", "adapter"), pairs)

    def from_tensor(x, m):
        return lax.ppermute(x, "tensor", [(s, s ^ m) for s in range(4)])

    def from_group(x):
        return lax.ppermute(x, "groups", [(0, 1), (1, 0)])

    weight = pltpu.with_memory_space_constraint(base_up_weight, pltpu.HBM)
    expand = pltpu.with_memory_space_constraint(adapter_expand_weight, pltpu.HBM)
    offsets = (2, 3, 1)
    blocks = [from_owner(tokens, j, j) for j in offsets]

    cuts = [block_count * k // 14 for k in (0, 4, 8, 11, 14)]
    parts = list(zip(cuts[:-1], cuts[1:]))
    loads = [block_count * k // 14 for k in (0, 4, 8, 11, 13, 14)]
    bands = 4
    small = [
        pltpu.with_memory_space_constraint(x, pltpu.HBM)
        for x in (
            adapter_slot_index.reshape(1, owner_count),
            row_adapter_index.reshape(1, row_count),
            tokens,
            adapter_shrink_weight[0].T,
        )
    ]
    across, beside, own, slots, index, mine, shrink, held = kernel_call(
        functools.partial(cut_kernel, block, range(loads[1]), len(small)),
        "cut_expand",
        1,
        1,
        1,
        in_specs=[anywhere] * (2 + len(small)),
        out_specs=[vmem] * (4 + len(small)),
        out_shape=[pltpu.VMEM((rank_block, w), bf16) for w in (columns,) * 3]
        + [pltpu.VMEM(x.shape, x.dtype) for x in small]
        + [pltpu.VMEM((loads[1], depth, block), bf16)],
        scratch_shapes=[
            pltpu.SemaphoreType.DMA((3 + len(small),)),
            pltpu.SemaphoreType.DMA((loads[1], bands)),
        ],
    )(expand, weight, *small)
    loaded = [held]
    across, beside = from_owner(across, 2, 3), from_owner(beside, 1, 1)

    rows, keep, send, slot = kernel_call(
        functools.partial(gather_kernel, (0, *offsets)),
        "gather_rows",
        1,
        1,
        4,
        in_specs=[vmem] * (owner_count + 3),
        out_specs=[vmem] * 4,
        out_shape=[jax.ShapeDtypeStruct((row_count, depth), bf16)]
        + [jax.ShapeDtypeStruct((rank // 2, row_count), f32)] * 2
        + [jax.ShapeDtypeStruct((1, row_count), jnp.int32)],
        scratch_shapes=[pltpu.VMEM((row_count, depth), bf16), pltpu.VMEM((rank, row_count), f32)],
    )(
        slots,
        index,
        mine,
        *blocks,
        shrink,
    )

    def base_part(n, *after):
        first, last = parts[n]
        streamed = n + 1 == len(parts)
        numbers = range(loads[n + 1], loads[n + 2])
        places, used = [], []
        for number in range(first, numbers[0] if streamed else last):
            source = max(k for k in range(len(loads) - 1) if loads[k] <= number)
            if source not in used:
                used.append(source)
            places.append((used.index(source), number - loads[source]))
        near = n < 2
        ahead = pltpu.VMEM((len(numbers), depth, block), bf16)
        out = kernel_call(
            functools.partial(base_kernel, block, places, numbers, streamed),
            "base_part",
            3 * 2 * row_count * depth * (last - first) * block if near else 1,
            3 * 2 * depth * (last - first) * block if near else 1,
            12,
            in_specs=[vmem, anywhere] + [vmem] * len(used) + [anywhere] * len(after),
            out_specs=[vmem] * (1 if streamed else 2),
            out_shape=[jax.ShapeDtypeStruct((row_count, (last - first) * block), f32)]
            + ([] if streamed else [ahead]),
            scratch_shapes=([ahead] if streamed else [])
            + [pltpu.SemaphoreType.DMA((len(numbers), bands))],
        )(rows, weight, *[loaded[k] for k in used], *after)
        loaded.append(out[-1])
        return out[0]

    arrived = from_tensor(send, 1)
    base_0 = base_part(0, send)
    arrived, base_0 = lax.optimization_barrier((arrived, base_0))
    pair = keep + arrived
    arrived = from_tensor(pair[rank_block:], 2)
    base_1 = base_part(1, pair)
    arrived, base_1, across = lax.optimization_barrier((arrived, base_1, across))
    shrunk = (adapter_scale * (pair[:rank_block] + arrived)).astype(bf16)
    swapped = from_group(across)
    bases = [base_0, base_1]
    for m, n in ((1, 2), (2, 3)):
        arrived = from_owner(shrunk, m, m)
        base = base_part(n, shrunk, across)
        arrived, base = lax.optimization_barrier((arrived, base))
        bases.append(base)
        shrunk = shrunk + arrived

    middle = block_count // 2 * block
    splits = [(0, middle), (middle, columns)]
    widths = [last - first for first, last in splits]
    quarter = row_count // 4
    out = kernel_call(
        functools.partial(delta_kernel, block, splits),
        "add_delta",
        1,
        1,
        8,
        in_specs=[vmem] * (len(bases) + 6),
        out_specs=[vmem] * (2 + 2 * len(splits)),
        out_shape=[
            jax.ShapeDtypeStruct((quarter, w), f32) for w in (columns, columns, *widths, *widths)
        ],
        scratch_shapes=[
            pltpu.VMEM((row_count, rank_block * owner_count), f32),
            pltpu.VMEM((row_count, rank_block * owner_count), bf16),
        ],
    )(slot, *bases, own, shrunk, across, beside, swapped)
    own_keep, own_send = out[:2]
    crossed = []
    for keep, send in zip(out[2:4], out[4:6]):
        crossed.append(from_tensor((keep + from_tensor(send, 1)).astype(bf16), 2))
    kept = own_keep + from_tensor(own_send, 1)
    return jnp.concatenate(
        [
            (kept[:, first:last] + part.astype(f32)).astype(bf16)
            for (first, last), part in zip(splits, crossed)
        ],
        axis=1,
    )


def on_device(tokens, base_up_weight, adapter_shrink_weight, adapter_expand_weight, *index):
    pairs = lax.axis_size("groups") == 2 and lax.axis_size("tensor") == 4
    few = lax.axis_size("adapter") == 4
    columns = base_up_weight.shape[1]
    even = columns % 512 == 0 and columns >= 4096 and tokens.shape[0] % 16 == 0
    arrange = paired if pairs and few and even else general
    return arrange(
        tokens, base_up_weight, adapter_shrink_weight, adapter_expand_weight, *index
    )


def solution(mesh):
    placed = (
        P(("groups", "adapter"), "tensor"),
        P("tensor", "adapter"),
        P("adapter", "tensor", None),
        P("adapter", "tensor", None),
        P("groups", None),
        P(),
    )
    return jax.shard_map(
        on_device,
        mesh=mesh,
        in_specs=placed,
        out_specs=P(("groups", "tensor"), "adapter"),
        check_vma=False,
    )
```

```python
import functools

import jax
import jax.numpy as jnp
from jax import lax
from jax.experimental import pallas as pl
from jax.experimental.pallas import tpu as pltpu
from jax.sharding import PartitionSpec as P

adapter_scale = 0.5
lane = 128
f32 = jnp.float32
bf16 = jnp.bfloat16


def general(
    tokens,
    base_up_weight,
    adapter_shrink_weight,
    adapter_expand_weight,
    row_adapter_index,
    adapter_slot_index,
):
    owner_count = lax.axis_size("adapter")
    owner_index = lax.axis_index("adapter")
    tensor_index = lax.axis_index("tensor")
    rank_block = adapter_expand_weight.shape[1]
    columns = base_up_weight.shape[1]
    slot = jnp.take(adapter_slot_index, row_adapter_index[:, 0], axis=0)
    rows = lax.all_gather(tokens, "adapter", axis=0, tiled=True)
    expand = adapter_expand_weight[0].reshape(rank_block, owner_count, columns)
    expand = lax.all_to_all(expand, "adapter", split_axis=1, concat_axis=1, tiled=True)
    shrunk = jnp.dot(rows, adapter_shrink_weight[0], preferred_element_type=f32)
    shrunk = jnp.where((slot == owner_index)[:, None], shrunk, 0.0)
    shrunk = lax.psum(shrunk, ("adapter", "tensor"))
    shrunk = (adapter_scale * shrunk).astype(bf16)
    shrunk = lax.dynamic_slice_in_dim(shrunk, tensor_index * rank_block, rank_block, 1)
    chosen = slot[:, None] == jnp.arange(owner_count, dtype=jnp.int32)[None, :]
    spread = jnp.where(chosen[:, None, :], shrunk[:, :, None], jnp.zeros((), bf16))
    total = jnp.dot(rows, base_up_weight, preferred_element_type=f32)
    total = total + jnp.dot(
        spread.reshape(-1, rank_block * owner_count),
        expand.reshape(rank_block * owner_count, columns),
        preferred_element_type=f32,
    )
    return lax.psum_scatter(total, "tensor", scatter_dimension=0, tiled=True).astype(bf16)


vmem = pl.BlockSpec(memory_space=pltpu.VMEM)
anywhere = pl.BlockSpec(memory_space=pl.ANY)


def kernel_call(kernel, name, flops, moved, mib, **specs):
    return pl.pallas_call(
        kernel,
        cost_estimate=pl.CostEstimate(flops=flops, bytes_accessed=moved, transcendentals=0),
        compiler_params=pltpu.CompilerParams(vmem_limit_bytes=mib << 20),
        name=name,
        **specs,
    )


def cut_kernel(block, numbers, small_count, expand, weight, *refs):
    small, refs = refs[:small_count], refs[small_count:]
    across, beside, own, *loaded, held, sem, held_sem = refs
    g, a = lax.axis_index("groups"), lax.axis_index("adapter")
    columns = own.shape[1]
    firsts = (
        lax.bitwise_xor(a, 2 + g) * columns,
        lax.bitwise_xor(a, 1) * columns,
        a * columns,
    )
    copies = []
    for n, (first, target) in enumerate(zip(firsts, (across, beside, own))):
        span = pl.ds(pl.multiple_of(first, lane), columns)
        copies.append(pltpu.make_async_copy(expand.at[0, :, span], target, sem.at[n]))
    for n, (source, target) in enumerate(zip(small, loaded)):
        copies.append(pltpu.make_async_copy(source, target, sem.at[len(firsts) + n]))
    copies += weight_copies(block, numbers, weight, held, held_sem)
    for copy in copies:
        copy.start()
    for copy in copies:
        copy.wait()


def weight_copies(block, numbers, weight, target, sem):
    band_count = sem.shape[1]
    band = weight.shape[0] // band_count
    copies = []
    for n, number in enumerate(numbers):
        span = pl.ds(number * block, block)
        for m in range(band_count):
            rows = pl.ds(m * band, band)
            copies.append(
                pltpu.make_async_copy(weight.at[rows, span], target.at[n, rows], sem.at[n, m])
            )
    return copies


def gather_kernel(offsets, slots, index, *refs):
    owner_count = len(offsets)
    blocks = refs[:owner_count]
    shrink, rows_out, keep, send, slot_out, rows, partial = refs[owner_count:]
    a, t = lax.axis_index("adapter"), lax.axis_index("tensor")
    height, depth = blocks[0].shape
    for j, part in zip(offsets, blocks):
        where = lax.bitwise_xor(a, j)
        rows[pl.ds(pl.multiple_of(where * height, height), height), :] = part[:, :depth]
    quarter = rows.shape[0] // 4
    for i, flip in enumerate((0, 2, 1, 3)):
        start = pl.multiple_of(lax.bitwise_xor(t, flip) * quarter, quarter)
        rows_out[i * quarter : (i + 1) * quarter, :] = rows[pl.ds(start, quarter), :]
    product = lax.dot_general(
        shrink[...], rows[...], (((1,), (1,)), ((), ())), preferred_element_type=f32
    )
    named, table = index[...], slots[...]
    slot = jnp.zeros_like(named)
    for k in range(table.shape[1]):
        slot = jnp.where(named == k, table[:, k : k + 1], slot)
    slot_out[...] = slot
    partial[...] = jnp.where(slot == a, product, 0.0)
    rank_block = partial.shape[0] // 4
    for i, flip in enumerate((0, 2, 1, 3)):
        start = pl.multiple_of(lax.bitwise_xor(t, flip) * rank_block, rank_block)
        target = keep if i < 2 else send
        at = i % 2 * rank_block
        target[at : at + rank_block, :] = partial[pl.ds(start, rank_block), :]


def base_kernel(block, places, numbers, rows, weight, *refs):
    copies = []
    if numbers:
        total, ahead, sem = refs[-3:]
        copies = weight_copies(block, numbers, weight, ahead, sem)
    else:
        total = refs[-1]
    for copy in copies:
        copy.start()

    @pl.when(lax.axis_index("tensor") >= 0)
    def _():
        for n, (which, index) in enumerate(places):
            total[:, n * block : (n + 1) * block] = jnp.dot(
                rows[...], refs[which][index], preferred_element_type=f32
            )

    for copy in copies:
        copy.wait()


def delta_kernel(block, first, splits, slot, *refs):
    bases, refs = refs[: -len(splits) * 2 - 9], refs[-len(splits) * 2 - 9 :]
    own, shrunk, across, beside, swapped, own_keep, own_send = refs[:7]
    cross_keep, cross_send = refs[7 : 7 + len(splits)], refs[7 + len(splits) : 7 + 2 * len(splits)]
    flat, ordered = refs[-2:]
    g, a, t = (lax.axis_index(name) for name in ("groups", "adapter", "tensor"))
    row_count = bases[0].shape[0]
    quarter = row_count // 4
    merged = shrunk[...].astype(f32)
    spread = [
        jnp.where(slot[...] == lax.bitwise_xor(a, j), merged, 0.0)
        for j in (0, 2 + g, 1, 3 - g)
    ]
    flat[...] = jnp.concatenate(spread, axis=0).T
    for i, turn in enumerate((0, 2, 1, 3)):
        start = pl.multiple_of(lax.bitwise_xor(t, turn) * quarter, quarter)
        ordered[i * quarter : (i + 1) * quarter, :] = flat[pl.ds(start, quarter), :].astype(bf16)
    left = ordered[...]
    at, split = 0, 0
    for base in bases:
        for column in range(0, base.shape[1], block):
            span, there = slice(at, at + block), slice(first + at, first + at + block)
            expand = jnp.concatenate(
                [piece[:, there] for piece in (own, across, beside, swapped)], axis=0
            )
            total = base[:, column : column + block] + jnp.dot(
                left, expand, preferred_element_type=f32
            )
            if at >= splits[split][1]:
                split += 1
            here = slice(at - splits[split][0], at - splits[split][0] + block)
            own_keep[:, span] = total[:quarter]
            cross_keep[split][:, here] = total[quarter : 2 * quarter]
            own_send[:, span] = total[2 * quarter : 3 * quarter]
            cross_send[split][:, here] = total[3 * quarter :]
            at += block


def column_block(width):
    for size in (512, 256, 128):
        if width % size == 0:
            return size


def paired(
    tokens,
    base_up_weight,
    adapter_shrink_weight,
    adapter_expand_weight,
    row_adapter_index,
    adapter_slot_index,
):
    owner_count = lax.axis_size("adapter")
    g = lax.axis_index("groups")
    height, depth = tokens.shape
    row_count = height * owner_count
    columns = base_up_weight.shape[1]
    rank_block = adapter_expand_weight.shape[1]
    rank = adapter_shrink_weight.shape[2]
    block = column_block(columns)
    block_count = columns // block

    def from_owner(x, first, second):
        pairs = []
        for group, m in ((0, first), (1, second)):
            for s in range(owner_count):
                pairs.append((group * owner_count + s, group * owner_count + (s ^ m)))
        return lax.ppermute(x, ("groups", "adapter"), pairs)

    def from_tensor(x, m):
        return lax.ppermute(x, "tensor", [(s, s ^ m) for s in range(4)])

    def from_group(x):
        return lax.ppermute(x, "groups", [(0, 1), (1, 0)])

    weight = pltpu.with_memory_space_constraint(base_up_weight, pltpu.HBM)
    expand = pltpu.with_memory_space_constraint(adapter_expand_weight, pltpu.HBM)
    offsets = (2, 3, 1)
    blocks = [from_owner(tokens, j, j) for j in offsets]

    cuts = [block_count * k // 14 for k in (0, 4, 8, 11, 12, 14)]
    parts = list(zip(cuts[:-1], cuts[1:]))
    loads = [block_count * k // 14 for k in (0, 4, 8, 11, 13, 14, 14)]
    bands = 4
    costs = (15 * 10**8, 15 * 10**8, 1, 1, 1)
    small = [
        pltpu.with_memory_space_constraint(x, pltpu.HBM)
        for x in (
            adapter_slot_index.reshape(1, owner_count),
            row_adapter_index.reshape(1, row_count),
            tokens,
            adapter_shrink_weight[0].T,
        )
    ]
    across, beside, own, slots, index, mine, shrink, held = kernel_call(
        functools.partial(cut_kernel, block, range(loads[1]), len(small)),
        "cut_expand",
        1,
        1,
        1,
        in_specs=[anywhere] * (2 + len(small)),
        out_specs=[vmem] * (4 + len(small)),
        out_shape=[pltpu.VMEM((rank_block, w), bf16) for w in (columns,) * 3]
        + [pltpu.VMEM(x.shape, x.dtype) for x in small]
        + [pltpu.VMEM((loads[1], depth, block), bf16)],
        scratch_shapes=[
            pltpu.SemaphoreType.DMA((3 + len(small),)),
            pltpu.SemaphoreType.DMA((loads[1], bands)),
        ],
    )(expand, weight, *small)
    loaded = [held]
    across, beside = from_owner(across, 2, 3), from_owner(beside, 1, 1)

    rows, keep, send, slot = kernel_call(
        functools.partial(gather_kernel, (0, *offsets)),
        "gather_rows",
        1,
        1,
        4,
        in_specs=[vmem] * (owner_count + 3),
        out_specs=[vmem] * 4,
        out_shape=[jax.ShapeDtypeStruct((row_count, depth), bf16)]
        + [jax.ShapeDtypeStruct((rank // 2, row_count), f32)] * 2
        + [jax.ShapeDtypeStruct((1, row_count), jnp.int32)],
        scratch_shapes=[pltpu.VMEM((row_count, depth), bf16), pltpu.VMEM((rank, row_count), f32)],
    )(
        slots,
        index,
        mine,
        *blocks,
        shrink,
    )

    def base_part(n, *after):
        first, last = parts[n]
        numbers = range(loads[n + 1], loads[n + 2])
        places, used = [], []
        for number in range(first, last):
            source = max(k for k in range(len(loads) - 1) if loads[k] <= number)
            if source not in used:
                used.append(source)
            places.append((used.index(source), number - loads[source]))
        out = kernel_call(
            functools.partial(base_kernel, block, places, numbers),
            "base_part",
            costs[n],
            1,
            4,
            in_specs=[vmem, anywhere] + [vmem] * len(used) + [anywhere] * len(after),
            out_specs=[vmem] * (2 if numbers else 1),
            out_shape=[jax.ShapeDtypeStruct((row_count, (last - first) * block), f32)]
            + ([pltpu.VMEM((len(numbers), depth, block), bf16)] if numbers else []),
            scratch_shapes=[pltpu.SemaphoreType.DMA((len(numbers), bands))] if numbers else [],
        )(rows, weight, *[loaded[k] for k in used], *after)
        loaded.append(out[-1])
        return out[0]

    arrived = from_tensor(send, 1)
    base_0 = base_part(0, send)
    arrived, base_0 = lax.optimization_barrier((arrived, base_0))
    pair = keep + arrived
    arrived = from_tensor(pair[rank_block:], 2)
    base_1 = base_part(1, pair)
    arrived, base_1, across = lax.optimization_barrier((arrived, base_1, across))
    shrunk = (adapter_scale * (pair[:rank_block] + arrived)).astype(bf16)
    swapped = from_group(across)
    bases = [base_0, base_1]
    for m, n in ((1, 2), (2, 3)):
        arrived = from_owner(shrunk, m, m)
        base = base_part(n, shrunk, across)
        arrived, base = lax.optimization_barrier((arrived, base))
        bases.append(base)
        shrunk = shrunk + arrived

    quarter = row_count // 4

    def delta_part(first, bases, splits):
        width = splits[-1][1]
        widths = [last - begin for begin, last in splits]
        out = kernel_call(
            functools.partial(delta_kernel, block, first * block, splits),
            "add_delta",
            1,
            1,
            8,
            in_specs=[vmem] * (len(bases) + 6),
            out_specs=[vmem] * (2 + 2 * len(splits)),
            out_shape=[
                jax.ShapeDtypeStruct((quarter, w), f32) for w in (width, width, *widths, *widths)
            ],
            scratch_shapes=[
                pltpu.VMEM((row_count, rank_block * owner_count), f32),
                pltpu.VMEM((row_count, rank_block * owner_count), bf16),
            ],
        )(slot, *bases, own, shrunk, across, beside, swapped)
        return out[0], out[1], out[2 : 2 + len(splits)], out[2 + len(splits) :]

    def finish(own_keep, own_send, cross_keep, arrived, splits, before=()):
        crossed = [
            from_tensor((keep + other).astype(bf16), 2) for keep, other in zip(cross_keep, arrived)
        ]
        *before, crossed[0] = lax.optimization_barrier((*before, crossed[0]))
        kept = own_keep + from_tensor(own_send, 1)
        return before + [
            (kept[:, begin:last] + part.astype(f32)).astype(bf16)
            for (begin, last), part in zip(splits, crossed)
        ]

    most = parts[-1][0]
    middle = most // 2 * block
    splits = [(0, middle), (middle, most * block)]
    own_keep, own_send, cross_keep, cross_send = delta_part(0, bases, splits)
    arrived = [from_tensor(x, 1) for x in cross_send]
    last_base = base_part(4, cross_send[0])
    *arrived, last_base = lax.optimization_barrier((*arrived, last_base))
    pieces = finish(own_keep, own_send, cross_keep, arrived, splits)
    splits = [(0, (block_count - most) * block)]
    own_keep, own_send, cross_keep, cross_send = delta_part(most, [last_base], splits)
    arrived = [from_tensor(x, 1) for x in cross_send]
    pieces = finish(own_keep, own_send, cross_keep, arrived, splits, pieces)
    return jnp.concatenate(pieces, axis=1)


def on_device(tokens, base_up_weight, adapter_shrink_weight, adapter_expand_weight, *index):
    pairs = lax.axis_size("groups") == 2 and lax.axis_size("tensor") == 4
    few = lax.axis_size("adapter") == 4
    columns = base_up_weight.shape[1]
    even = columns % 512 == 0 and columns >= 4096 and tokens.shape[0] % 16 == 0
    arrange = paired if pairs and few and even else general
    return arrange(
        tokens, base_up_weight, adapter_shrink_weight, adapter_expand_weight, *index
    )


def solution(mesh):
    placed = (
        P(("groups", "adapter"), "tensor"),
        P("tensor", "adapter"),
        P("adapter", "tensor", None),
        P("adapter", "tensor", None),
        P("groups", None),
        P(),
    )
    return jax.shard_map(
        on_device,
        mesh=mesh,
        in_specs=placed,
        out_specs=P(("groups", "tensor"), "adapter"),
        check_vma=False,
    )
```

```python
import functools

import jax
import jax.numpy as jnp
from jax import lax
from jax.experimental import pallas as pl
from jax.experimental.pallas import tpu as pltpu
from jax.sharding import PartitionSpec as P

adapter_scale = 0.5
lane = 128
f32 = jnp.float32
bf16 = jnp.bfloat16


def general(
    tokens,
    base_up_weight,
    adapter_shrink_weight,
    adapter_expand_weight,
    row_adapter_index,
    adapter_slot_index,
):
    owner_count = lax.axis_size("adapter")
    owner_index = lax.axis_index("adapter")
    tensor_index = lax.axis_index("tensor")
    rank_block = adapter_expand_weight.shape[1]
    columns = base_up_weight.shape[1]
    slot = jnp.take(adapter_slot_index, row_adapter_index[:, 0], axis=0)
    rows = lax.all_gather(tokens, "adapter", axis=0, tiled=True)
    expand = adapter_expand_weight[0].reshape(rank_block, owner_count, columns)
    expand = lax.all_to_all(expand, "adapter", split_axis=1, concat_axis=1, tiled=True)
    shrunk = jnp.dot(rows, adapter_shrink_weight[0], preferred_element_type=f32)
    shrunk = jnp.where((slot == owner_index)[:, None], shrunk, 0.0)
    shrunk = lax.psum(shrunk, ("adapter", "tensor"))
    shrunk = (adapter_scale * shrunk).astype(bf16)
    shrunk = lax.dynamic_slice_in_dim(shrunk, tensor_index * rank_block, rank_block, 1)
    chosen = slot[:, None] == jnp.arange(owner_count, dtype=jnp.int32)[None, :]
    spread = jnp.where(chosen[:, None, :], shrunk[:, :, None], jnp.zeros((), bf16))
    total = jnp.dot(rows, base_up_weight, preferred_element_type=f32)
    total = total + jnp.dot(
        spread.reshape(-1, rank_block * owner_count),
        expand.reshape(rank_block * owner_count, columns),
        preferred_element_type=f32,
    )
    return lax.psum_scatter(total, "tensor", scatter_dimension=0, tiled=True).astype(bf16)


vmem = pl.BlockSpec(memory_space=pltpu.VMEM)
anywhere = pl.BlockSpec(memory_space=pl.ANY)


def kernel_call(kernel, name, flops, moved, mib, **specs):
    return pl.pallas_call(
        kernel,
        cost_estimate=pl.CostEstimate(flops=flops, bytes_accessed=moved, transcendentals=0),
        compiler_params=pltpu.CompilerParams(vmem_limit_bytes=mib << 20),
        name=name,
        **specs,
    )


def cut_kernel(block, numbers, small_count, expand, weight, *refs):
    small, refs = refs[:small_count], refs[small_count:]
    across, beside, own, *loaded, held, sem, held_sem = refs
    g, a = lax.axis_index("groups"), lax.axis_index("adapter")
    columns = own.shape[1]
    firsts = (
        lax.bitwise_xor(a, 2 + g) * columns,
        lax.bitwise_xor(a, 1) * columns,
        a * columns,
    )
    copies = []
    for n, (first, target) in enumerate(zip(firsts, (across, beside, own))):
        span = pl.ds(pl.multiple_of(first, lane), columns)
        copies.append(pltpu.make_async_copy(expand.at[0, :, span], target, sem.at[n]))
    for n, (source, target) in enumerate(zip(small, loaded)):
        copies.append(pltpu.make_async_copy(source, target, sem.at[len(firsts) + n]))
    copies += weight_copies(block, numbers, weight, held, held_sem)
    for copy in copies:
        copy.start()
    for copy in copies:
        copy.wait()


def weight_copies(block, numbers, weight, target, sem):
    band_count = sem.shape[1]
    band = weight.shape[0] // band_count
    copies = []
    for n, number in enumerate(numbers):
        span = pl.ds(number * block, block)
        for m in range(band_count):
            rows = pl.ds(m * band, band)
            copies.append(
                pltpu.make_async_copy(weight.at[rows, span], target.at[n, rows], sem.at[n, m])
            )
    return copies


def gather_kernel(offsets, slots, index, *refs):
    owner_count = len(offsets)
    blocks = refs[:owner_count]
    shrink, rows_out, *parts_out, slot_out, rows, partial = refs[owner_count:]
    a, t = lax.axis_index("adapter"), lax.axis_index("tensor")
    height, depth = blocks[0].shape
    for j, part in zip(offsets, blocks):
        where = lax.bitwise_xor(a, j)
        rows[pl.ds(pl.multiple_of(where * height, height), height), :] = part[:, :depth]
    quarter = rows.shape[0] // 4
    for i, flip in enumerate((0, 2, 1, 3)):
        start = pl.multiple_of(lax.bitwise_xor(t, flip) * quarter, quarter)
        rows_out[i * quarter : (i + 1) * quarter, :] = rows[pl.ds(start, quarter), :]
    product = lax.dot_general(
        shrink[...], rows[...], (((1,), (1,)), ((), ())), preferred_element_type=f32
    )
    named, table = index[...], slots[...]
    slot = jnp.zeros_like(named)
    for k in range(table.shape[1]):
        slot = jnp.where(named == k, table[:, k : k + 1], slot)
    slot_out[...] = slot
    partial[...] = jnp.where(slot == a, product, 0.0)
    rank_block = partial.shape[0] // 4
    for flip, part in enumerate(parts_out):
        start = pl.multiple_of(lax.bitwise_xor(t, flip) * rank_block, rank_block)
        part[...] = partial[pl.ds(start, rank_block), :]


def base_kernel(block, places, numbers, streamed, rows, weight, *refs):
    total, ahead, sem = refs[-3:]
    copies = weight_copies(block, numbers, weight, ahead, sem)
    for copy in copies:
        copy.start()

    @pl.when(lax.axis_index("tensor") >= 0)
    def _():
        for n, (which, index) in enumerate(places):
            total[:, n * block : (n + 1) * block] = jnp.dot(
                rows[...], refs[which][index], preferred_element_type=f32
            )

    bands = sem.shape[1]
    for n in range(len(numbers)):
        for copy in copies[n * bands : (n + 1) * bands]:
            copy.wait()
        if streamed:
            at = (len(places) + n) * block
            total[:, at : at + block] = jnp.dot(
                rows[...], ahead[n], preferred_element_type=f32
            )


def delta_kernel(block, splits, slot, *refs):
    bases, refs = refs[: -len(splits) * 2 - 9], refs[-len(splits) * 2 - 9 :]
    own, shrunk, across, beside, swapped, own_keep, own_send = refs[:7]
    cross_keep, cross_send = refs[7 : 7 + len(splits)], refs[7 + len(splits) : 7 + 2 * len(splits)]
    flat, ordered = refs[-2:]
    g, a, t = (lax.axis_index(name) for name in ("groups", "adapter", "tensor"))
    row_count = bases[0].shape[0]
    quarter = row_count // 4
    merged = shrunk[...].astype(f32)
    spread = [
        jnp.where(slot[...] == lax.bitwise_xor(a, j), merged, 0.0)
        for j in (0, 2 + g, 1, 3 - g)
    ]
    flat[...] = jnp.concatenate(spread, axis=0).T
    for i, turn in enumerate((0, 2, 1, 3)):
        start = pl.multiple_of(lax.bitwise_xor(t, turn) * quarter, quarter)
        ordered[i * quarter : (i + 1) * quarter, :] = flat[pl.ds(start, quarter), :].astype(bf16)
    left = ordered[...]
    at, split = 0, 0
    for base in bases:
        for column in range(0, base.shape[1], block):
            span = slice(at, at + block)
            expand = jnp.concatenate(
                [own[:, span], across[:, span], beside[:, span], swapped[:, span]], axis=0
            )
            total = base[:, column : column + block] + jnp.dot(
                left, expand, preferred_element_type=f32
            )
            if at >= splits[split][1]:
                split += 1
            here = slice(at - splits[split][0], at - splits[split][0] + block)
            own_keep[:, span] = total[:quarter]
            cross_keep[split][:, here] = total[quarter : 2 * quarter]
            own_send[:, span] = total[2 * quarter : 3 * quarter]
            cross_send[split][:, here] = total[3 * quarter :]
            at += block


def column_block(width):
    for size in (512, 256, 128):
        if width % size == 0:
            return size


def paired(
    tokens,
    base_up_weight,
    adapter_shrink_weight,
    adapter_expand_weight,
    row_adapter_index,
    adapter_slot_index,
):
    owner_count = lax.axis_size("adapter")
    g = lax.axis_index("groups")
    height, depth = tokens.shape
    row_count = height * owner_count
    columns = base_up_weight.shape[1]
    rank_block = adapter_expand_weight.shape[1]
    rank = adapter_shrink_weight.shape[2]
    block = column_block(columns)
    block_count = columns // block

    def from_owner(x, first, second):
        pairs = []
        for group, m in ((0, first), (1, second)):
            for s in range(owner_count):
                pairs.append((group * owner_count + s, group * owner_count + (s ^ m)))
        return lax.ppermute(x, ("groups", "adapter"), pairs)

    def from_tensor(x, m):
        return lax.ppermute(x, "tensor", [(s, s ^ m) for s in range(4)])

    def from_group(x):
        return lax.ppermute(x, "groups", [(0, 1), (1, 0)])

    weight = pltpu.with_memory_space_constraint(base_up_weight, pltpu.HBM)
    expand = pltpu.with_memory_space_constraint(adapter_expand_weight, pltpu.HBM)
    offsets = (2, 3, 1)
    blocks = [from_owner(tokens, j, j) for j in offsets]

    cuts = [block_count * k // 14 for k in (0, 4, 8, 11, 14)]
    parts = list(zip(cuts[:-1], cuts[1:]))
    loads = [block_count * k // 14 for k in (0, 4, 8, 11, 13, 14)]
    bands = 4
    small = [
        pltpu.with_memory_space_constraint(x, pltpu.HBM)
        for x in (
            adapter_slot_index.reshape(1, owner_count),
            row_adapter_index.reshape(1, row_count),
            tokens,
            adapter_shrink_weight[0].T,
        )
    ]
    across, beside, own, slots, index, mine, shrink, held = kernel_call(
        functools.partial(cut_kernel, block, range(loads[1]), len(small)),
        "cut_expand",
        1,
        1,
        1,
        in_specs=[anywhere] * (2 + len(small)),
        out_specs=[vmem] * (4 + len(small)),
        out_shape=[pltpu.VMEM((rank_block, w), bf16) for w in (columns,) * 3]
        + [pltpu.VMEM(x.shape, x.dtype) for x in small]
        + [pltpu.VMEM((loads[1], depth, block), bf16)],
        scratch_shapes=[
            pltpu.SemaphoreType.DMA((3 + len(small),)),
            pltpu.SemaphoreType.DMA((loads[1], bands)),
        ],
    )(expand, weight, *small)
    loaded = [held]
    across, beside = from_owner(across, 2, 3), from_owner(beside, 1, 1)

    rows, *mine_parts, slot = kernel_call(
        functools.partial(gather_kernel, (0, *offsets)),
        "gather_rows",
        1,
        1,
        4,
        in_specs=[vmem] * (owner_count + 3),
        out_specs=[vmem] * 6,
        out_shape=[jax.ShapeDtypeStruct((row_count, depth), bf16)]
        + [jax.ShapeDtypeStruct((rank_block, row_count), f32)] * 4
        + [jax.ShapeDtypeStruct((1, row_count), jnp.int32)],
        scratch_shapes=[pltpu.VMEM((row_count, depth), bf16), pltpu.VMEM((rank, row_count), f32)],
    )(
        slots,
        index,
        mine,
        *blocks,
        shrink,
    )

    def base_part(n, *after):
        first, last = parts[n]
        streamed = n + 1 == len(parts)
        numbers = range(loads[n + 1], loads[n + 2])
        places, used = [], []
        for number in range(first, numbers[0] if streamed else last):
            source = max(k for k in range(len(loads) - 1) if loads[k] <= number)
            if source not in used:
                used.append(source)
            places.append((used.index(source), number - loads[source]))
        near = n < 2
        ahead = pltpu.VMEM((len(numbers), depth, block), bf16)
        out = kernel_call(
            functools.partial(base_kernel, block, places, numbers, streamed),
            "base_part",
            3 * 2 * row_count * depth * (last - first) * block if near else 1,
            3 * 2 * depth * (last - first) * block if near else 1,
            12,
            in_specs=[vmem, anywhere] + [vmem] * len(used) + [anywhere] * len(after),
            out_specs=[vmem] * (1 if streamed else 2),
            out_shape=[jax.ShapeDtypeStruct((row_count, (last - first) * block), f32)]
            + ([] if streamed else [ahead]),
            scratch_shapes=([ahead] if streamed else [])
            + [pltpu.SemaphoreType.DMA((len(numbers), bands))],
        )(rows, weight, *[loaded[k] for k in used], *after)
        loaded.append(out[-1])
        return out[0]

    arrived = [from_tensor(mine_parts[m], m) for m in (1, 2, 3)]
    bases = [base_part(0, *mine_parts[1:])]
    bases.append(base_part(1, bases[0]))
    *arrived, across, bases[1] = lax.optimization_barrier((*arrived, across, bases[1]))
    swapped = from_group(across)
    shrunk = adapter_scale * (mine_parts[0] + arrived[0] + arrived[1] + arrived[2])
    shrunk = shrunk.astype(bf16)
    arrived = [from_owner(shrunk, m, m) for m in (1, 2, 3)]
    bases.append(base_part(2, shrunk, across))
    bases.append(base_part(3, bases[2]))
    *arrived, bases[3] = lax.optimization_barrier((*arrived, bases[3]))
    shrunk = shrunk + arrived[0] + arrived[1] + arrived[2]

    middle = block_count // 2 * block
    splits = [(0, middle), (middle, columns)]
    widths = [last - first for first, last in splits]
    quarter = row_count // 4
    out = kernel_call(
        functools.partial(delta_kernel, block, splits),
        "add_delta",
        1,
        1,
        8,
        in_specs=[vmem] * (len(bases) + 6),
        out_specs=[vmem] * (2 + 2 * len(splits)),
        out_shape=[
            jax.ShapeDtypeStruct((quarter, w), f32) for w in (columns, columns, *widths, *widths)
        ],
        scratch_shapes=[
            pltpu.VMEM((row_count, rank_block * owner_count), f32),
            pltpu.VMEM((row_count, rank_block * owner_count), bf16),
        ],
    )(slot, *bases, own, shrunk, across, beside, swapped)
    own_keep, own_send = out[:2]
    crossed = []
    for keep, send in zip(out[2:4], out[4:6]):
        crossed.append(from_tensor((keep + from_tensor(send, 1)).astype(bf16), 2))
    kept = own_keep + from_tensor(own_send, 1)
    return jnp.concatenate(
        [
            (kept[:, first:last] + part.astype(f32)).astype(bf16)
            for (first, last), part in zip(splits, crossed)
        ],
        axis=1,
    )


def on_device(tokens, base_up_weight, adapter_shrink_weight, adapter_expand_weight, *index):
    pairs = lax.axis_size("groups") == 2 and lax.axis_size("tensor") == 4
    few = lax.axis_size("adapter") == 4
    columns = base_up_weight.shape[1]
    even = columns % 512 == 0 and columns >= 4096 and tokens.shape[0] % 16 == 0
    arrange = paired if pairs and few and even else general
    return arrange(
        tokens, base_up_weight, adapter_shrink_weight, adapter_expand_weight, *index
    )


def solution(mesh):
    placed = (
        P(("groups", "adapter"), "tensor"),
        P("tensor", "adapter"),
        P("adapter", "tensor", None),
        P("adapter", "tensor", None),
        P("groups", None),
        P(),
    )
    return jax.shard_map(
        on_device,
        mesh=mesh,
        in_specs=placed,
        out_specs=P(("groups", "tensor"), "adapter"),
        check_vma=False,
    )
```

```python
import functools

import jax
import jax.numpy as jnp
from jax import lax
from jax.experimental import pallas as pl
from jax.experimental.pallas import tpu as pltpu
from jax.sharding import PartitionSpec as P

adapter_scale = 0.5
lane = 128
f32 = jnp.float32
bf16 = jnp.bfloat16


def general(
    tokens,
    base_up_weight,
    adapter_shrink_weight,
    adapter_expand_weight,
    row_adapter_index,
    adapter_slot_index,
):
    owner_count = lax.axis_size("adapter")
    owner_index = lax.axis_index("adapter")
    tensor_index = lax.axis_index("tensor")
    rank_block = adapter_expand_weight.shape[1]
    columns = base_up_weight.shape[1]
    slot = jnp.take(adapter_slot_index, row_adapter_index[:, 0], axis=0)
    rows = lax.all_gather(tokens, "adapter", axis=0, tiled=True)
    expand = adapter_expand_weight[0].reshape(rank_block, owner_count, columns)
    expand = lax.all_to_all(expand, "adapter", split_axis=1, concat_axis=1, tiled=True)
    shrunk = jnp.dot(rows, adapter_shrink_weight[0], preferred_element_type=f32)
    shrunk = jnp.where((slot == owner_index)[:, None], shrunk, 0.0)
    shrunk = lax.psum(shrunk, ("adapter", "tensor"))
    shrunk = (adapter_scale * shrunk).astype(bf16)
    shrunk = lax.dynamic_slice_in_dim(shrunk, tensor_index * rank_block, rank_block, 1)
    chosen = slot[:, None] == jnp.arange(owner_count, dtype=jnp.int32)[None, :]
    spread = jnp.where(chosen[:, None, :], shrunk[:, :, None], jnp.zeros((), bf16))
    total = jnp.dot(rows, base_up_weight, preferred_element_type=f32)
    total = total + jnp.dot(
        spread.reshape(-1, rank_block * owner_count),
        expand.reshape(rank_block * owner_count, columns),
        preferred_element_type=f32,
    )
    return lax.psum_scatter(total, "tensor", scatter_dimension=0, tiled=True).astype(bf16)


vmem = pl.BlockSpec(memory_space=pltpu.VMEM)
anywhere = pl.BlockSpec(memory_space=pl.ANY)


def kernel_call(kernel, name, flops, moved, mib, **specs):
    return pl.pallas_call(
        kernel,
        cost_estimate=pl.CostEstimate(flops=flops, bytes_accessed=moved, transcendentals=0),
        compiler_params=pltpu.CompilerParams(vmem_limit_bytes=mib << 20),
        name=name,
        **specs,
    )


def cut_kernel(block, numbers, small_count, expand, weight, *refs):
    small, refs = refs[:small_count], refs[small_count:]
    across, beside, own, *loaded, held, sem, held_sem = refs
    g, a = lax.axis_index("groups"), lax.axis_index("adapter")
    columns = own.shape[1]
    firsts = (
        lax.bitwise_xor(a, 2 + g) * columns,
        lax.bitwise_xor(a, 1) * columns,
        a * columns,
    )
    copies = []
    for n, (first, target) in enumerate(zip(firsts, (across, beside, own))):
        span = pl.ds(pl.multiple_of(first, lane), columns)
        copies.append(pltpu.make_async_copy(expand.at[0, :, span], target, sem.at[n]))
    for n, (source, target) in enumerate(zip(small, loaded)):
        copies.append(pltpu.make_async_copy(source, target, sem.at[len(firsts) + n]))
    copies += weight_copies(block, numbers, weight, held, held_sem)
    for copy in copies:
        copy.start()
    for copy in copies:
        copy.wait()


def weight_copies(block, numbers, weight, target, sem):
    band_count = sem.shape[1]
    band = weight.shape[0] // band_count
    copies = []
    for n, number in enumerate(numbers):
        span = pl.ds(number * block, block)
        for m in range(band_count):
            rows = pl.ds(m * band, band)
            copies.append(
                pltpu.make_async_copy(weight.at[rows, span], target.at[n, rows], sem.at[n, m])
            )
    return copies


def gather_kernel(offsets, slots, index, *refs):
    owner_count = len(offsets)
    blocks = refs[:owner_count]
    shrink, rows_out, keep, send, slot_out, rows, partial = refs[owner_count:]
    a, t = lax.axis_index("adapter"), lax.axis_index("tensor")
    height, depth = blocks[0].shape
    for j, part in zip(offsets, blocks):
        where = lax.bitwise_xor(a, j)
        rows[pl.ds(pl.multiple_of(where * height, height), height), :] = part[:, :depth]
    quarter = rows.shape[0] // 4
    for i, flip in enumerate((0, 2, 1, 3)):
        start = pl.multiple_of(lax.bitwise_xor(t, flip) * quarter, quarter)
        rows_out[i * quarter : (i + 1) * quarter, :] = rows[pl.ds(start, quarter), :]
    product = lax.dot_general(
        shrink[...], rows[...], (((1,), (1,)), ((), ())), preferred_element_type=f32
    )
    named, table = index[...], slots[...]
    slot = jnp.zeros_like(named)
    for k in range(table.shape[1]):
        slot = jnp.where(named == k, table[:, k : k + 1], slot)
    slot_out[...] = slot
    partial[...] = jnp.where(slot == a, product, 0.0)
    rank_block = partial.shape[0] // 4
    for i, flip in enumerate((0, 2, 1, 3)):
        start = pl.multiple_of(lax.bitwise_xor(t, flip) * rank_block, rank_block)
        target = keep if i < 2 else send
        at = i % 2 * rank_block
        target[at : at + rank_block, :] = partial[pl.ds(start, rank_block), :]


def base_kernel(block, stream, ahead, rows, weight, held, *refs):
    refs = list(refs)
    copies, streamed, later = [], None, []
    if ahead:
        sem = refs.pop()
    if stream:
        streamed, stream_sem = refs[-2:]
        refs = refs[:-2]
        copies = weight_copies(block, stream, weight, streamed, stream_sem)
    if ahead:
        later = weight_copies(block, ahead, weight, refs.pop(), sem)
    total = refs[-1]
    for copy in copies + later:
        copy.start()

    @pl.when(lax.axis_index("tensor") >= 0)
    def _():
        for n in range(held.shape[0]):
            total[:, n * block : (n + 1) * block] = jnp.dot(
                rows[...], held[n], preferred_element_type=f32
            )

    for n in range(len(stream)):
        bands = len(copies) // len(stream)
        for copy in copies[n * bands : (n + 1) * bands]:
            copy.wait()
        at = (held.shape[0] + n) * block
        total[:, at : at + block] = jnp.dot(
            rows[...], streamed[n], preferred_element_type=f32
        )
    for copy in later:
        copy.wait()


def delta_kernel(block, splits, slot, *refs):
    bases, refs = refs[: -len(splits) * 2 - 9], refs[-len(splits) * 2 - 9 :]
    own, shrunk, across, beside, swapped, own_keep, own_send = refs[:7]
    cross_keep, cross_send = refs[7 : 7 + len(splits)], refs[7 + len(splits) : 7 + 2 * len(splits)]
    flat, ordered = refs[-2:]
    g, a, t = (lax.axis_index(name) for name in ("groups", "adapter", "tensor"))
    row_count = bases[0].shape[0]
    quarter = row_count // 4
    merged = shrunk[...].astype(f32)
    spread = [
        jnp.where(slot[...] == lax.bitwise_xor(a, j), merged, 0.0)
        for j in (0, 2 + g, 1, 3 - g)
    ]
    flat[...] = jnp.concatenate(spread, axis=0).T
    for i, turn in enumerate((0, 2, 1, 3)):
        start = pl.multiple_of(lax.bitwise_xor(t, turn) * quarter, quarter)
        ordered[i * quarter : (i + 1) * quarter, :] = flat[pl.ds(start, quarter), :].astype(bf16)
    left = ordered[...]
    at, split = 0, 0
    for base in bases:
        for column in range(0, base.shape[1], block):
            span = slice(at, at + block)
            expand = jnp.concatenate(
                [own[:, span], across[:, span], beside[:, span], swapped[:, span]], axis=0
            )
            total = base[:, column : column + block] + jnp.dot(
                left, expand, preferred_element_type=f32
            )
            if at >= splits[split][1]:
                split += 1
            here = slice(at - splits[split][0], at - splits[split][0] + block)
            own_keep[:, span] = total[:quarter]
            cross_keep[split][:, here] = total[quarter : 2 * quarter]
            own_send[:, span] = total[2 * quarter : 3 * quarter]
            cross_send[split][:, here] = total[3 * quarter :]
            at += block


def column_block(width):
    for size in (512, 256, 128):
        if width % size == 0:
            return size


def paired(
    tokens,
    base_up_weight,
    adapter_shrink_weight,
    adapter_expand_weight,
    row_adapter_index,
    adapter_slot_index,
):
    owner_count = lax.axis_size("adapter")
    g = lax.axis_index("groups")
    height, depth = tokens.shape
    row_count = height * owner_count
    columns = base_up_weight.shape[1]
    rank_block = adapter_expand_weight.shape[1]
    rank = adapter_shrink_weight.shape[2]
    block = column_block(columns)
    block_count = columns // block

    def from_owner(x, first, second):
        pairs = []
        for group, m in ((0, first), (1, second)):
            for s in range(owner_count):
                pairs.append((group * owner_count + s, group * owner_count + (s ^ m)))
        return lax.ppermute(x, ("groups", "adapter"), pairs)

    def from_tensor(x, m):
        return lax.ppermute(x, "tensor", [(s, s ^ m) for s in range(4)])

    def from_group(x):
        return lax.ppermute(x, "groups", [(0, 1), (1, 0)])

    weight = pltpu.with_memory_space_constraint(base_up_weight, pltpu.HBM)
    expand = pltpu.with_memory_space_constraint(adapter_expand_weight, pltpu.HBM)
    offsets = (2, 3, 1)
    blocks = [from_owner(tokens, j, j) for j in offsets]

    loads = [block_count * k // 14 for k in (0, 4, 8, 11, 14)]
    streams = [range(loads[1], loads[2]), range(0), range(0)]
    aheads = [range(loads[2], loads[3]), range(loads[3], loads[4]), range(0)]
    bands = 4
    small = [
        pltpu.with_memory_space_constraint(x, pltpu.HBM)
        for x in (
            adapter_slot_index.reshape(1, owner_count),
            row_adapter_index.reshape(1, row_count),
            tokens,
            adapter_shrink_weight[0].T,
        )
    ]
    across, beside, own, slots, index, mine, shrink, held = kernel_call(
        functools.partial(cut_kernel, block, range(loads[1]), len(small)),
        "cut_expand",
        1,
        1,
        1,
        in_specs=[anywhere] * (2 + len(small)),
        out_specs=[vmem] * (4 + len(small)),
        out_shape=[pltpu.VMEM((rank_block, w), bf16) for w in (columns,) * 3]
        + [pltpu.VMEM(x.shape, x.dtype) for x in small]
        + [pltpu.VMEM((loads[1], depth, block), bf16)],
        scratch_shapes=[
            pltpu.SemaphoreType.DMA((3 + len(small),)),
            pltpu.SemaphoreType.DMA((loads[1], bands)),
        ],
    )(expand, weight, *small)
    across = from_owner(across, 2, 3)

    rows, keep, send, slot = kernel_call(
        functools.partial(gather_kernel, (0, *offsets)),
        "gather_rows",
        1,
        1,
        4,
        in_specs=[vmem] * (owner_count + 3),
        out_specs=[vmem] * 4,
        out_shape=[jax.ShapeDtypeStruct((row_count, depth), bf16)]
        + [jax.ShapeDtypeStruct((rank // 2, row_count), f32)] * 2
        + [jax.ShapeDtypeStruct((1, row_count), jnp.int32)],
        scratch_shapes=[pltpu.VMEM((row_count, depth), bf16), pltpu.VMEM((rank, row_count), f32)],
    )(
        slots,
        index,
        mine,
        *blocks,
        shrink,
    )

    def base_part(n, held, *after):
        stream, ahead = streams[n], aheads[n]
        width = (held.shape[0] + len(stream)) * block
        extra, scratch = [], []
        if ahead:
            extra = [pltpu.VMEM((len(ahead), depth, block), bf16)]
        if stream:
            scratch += [
                pltpu.VMEM((len(stream), depth, block), bf16),
                pltpu.SemaphoreType.DMA((len(stream), bands)),
            ]
        if ahead:
            scratch += [pltpu.SemaphoreType.DMA((len(ahead), bands))]
        return kernel_call(
            functools.partial(base_kernel, block, stream, ahead),
            "base_part",
            (2 * 10**9, 1, 1)[n],
            1,
            12,
            in_specs=[vmem, anywhere, vmem] + [anywhere] * len(after),
            out_specs=[vmem] * (1 + len(extra)),
            out_shape=[jax.ShapeDtypeStruct((row_count, width), f32)] + extra,
            scratch_shapes=scratch,
        )(rows, weight, held, *after)

    beside, send = lax.optimization_barrier((beside, send))
    arrived = from_tensor(send, 1)
    beside = from_owner(beside, 1, 1)
    pair = keep + arrived
    arrived = from_tensor(pair[rank_block:], 2)
    base, held = base_part(0, held, pair)
    arrived, across, base = lax.optimization_barrier((arrived, across, base))
    bases = [base]
    shrunk = (adapter_scale * (pair[:rank_block] + arrived)).astype(bf16)
    arrived = from_owner(shrunk, 1, 1)
    swapped = from_group(across)
    base, held = base_part(1, held, shrunk, across)
    bases.append(base)
    arrived, base = lax.optimization_barrier((arrived, base))
    shrunk = shrunk + arrived
    arrived = from_owner(shrunk, 2, 2)
    bases += base_part(2, held, shrunk)
    arrived, base = lax.optimization_barrier((arrived, bases[-1]))
    shrunk = shrunk + arrived

    middle = block_count // 2 * block
    splits = [(0, middle), (middle, columns)]
    widths = [last - first for first, last in splits]
    quarter = row_count // 4
    out = kernel_call(
        functools.partial(delta_kernel, block, splits),
        "add_delta",
        1,
        1,
        8,
        in_specs=[vmem] * (len(bases) + 6),
        out_specs=[vmem] * (2 + 2 * len(splits)),
        out_shape=[
            jax.ShapeDtypeStruct((quarter, w), f32) for w in (columns, columns, *widths, *widths)
        ],
        scratch_shapes=[
            pltpu.VMEM((row_count, rank_block * owner_count), f32),
            pltpu.VMEM((row_count, rank_block * owner_count), bf16),
        ],
    )(slot, *bases, own, shrunk, across, beside, swapped)
    own_keep, own_send = out[:2]
    crossed = []
    for keep, send in zip(out[2:4], out[4:6]):
        crossed.append(from_tensor((keep + from_tensor(send, 1)).astype(bf16), 2))
    kept = own_keep + from_tensor(own_send, 1)
    return jnp.concatenate(
        [
            (kept[:, first:last] + part.astype(f32)).astype(bf16)
            for (first, last), part in zip(splits, crossed)
        ],
        axis=1,
    )


def on_device(tokens, base_up_weight, adapter_shrink_weight, adapter_expand_weight, *index):
    pairs = lax.axis_size("groups") == 2 and lax.axis_size("tensor") == 4
    few = lax.axis_size("adapter") == 4
    columns = base_up_weight.shape[1]
    even = columns % 512 == 0 and columns >= 4096 and tokens.shape[0] % 16 == 0
    arrange = paired if pairs and few and even else general
    return arrange(
        tokens, base_up_weight, adapter_shrink_weight, adapter_expand_weight, *index
    )


def solution(mesh):
    placed = (
        P(("groups", "adapter"), "tensor"),
        P("tensor", "adapter"),
        P("adapter", "tensor", None),
        P("adapter", "tensor", None),
        P("groups", None),
        P(),
    )
    return jax.shard_map(
        on_device,
        mesh=mesh,
        in_specs=placed,
        out_specs=P(("groups", "tensor"), "adapter"),
        check_vma=False,
    )
```

```python
import functools

import jax
import jax.numpy as jnp
from jax import lax
from jax.experimental import pallas as pl
from jax.experimental.pallas import tpu as pltpu
from jax.sharding import PartitionSpec as P

adapter_scale = 0.5
lane = 128
f32 = jnp.float32
bf16 = jnp.bfloat16


def general(
    tokens,
    base_up_weight,
    adapter_shrink_weight,
    adapter_expand_weight,
    row_adapter_index,
    adapter_slot_index,
):
    owner_count = lax.axis_size("adapter")
    owner_index = lax.axis_index("adapter")
    tensor_index = lax.axis_index("tensor")
    rank_block = adapter_expand_weight.shape[1]
    columns = base_up_weight.shape[1]
    slot = jnp.take(adapter_slot_index, row_adapter_index[:, 0], axis=0)
    rows = lax.all_gather(tokens, "adapter", axis=0, tiled=True)
    expand = adapter_expand_weight[0].reshape(rank_block, owner_count, columns)
    expand = lax.all_to_all(expand, "adapter", split_axis=1, concat_axis=1, tiled=True)
    shrunk = jnp.dot(rows, adapter_shrink_weight[0], preferred_element_type=f32)
    shrunk = jnp.where((slot == owner_index)[:, None], shrunk, 0.0)
    shrunk = lax.psum(shrunk, ("adapter", "tensor"))
    shrunk = (adapter_scale * shrunk).astype(bf16)
    shrunk = lax.dynamic_slice_in_dim(shrunk, tensor_index * rank_block, rank_block, 1)
    chosen = slot[:, None] == jnp.arange(owner_count, dtype=jnp.int32)[None, :]
    spread = jnp.where(chosen[:, None, :], shrunk[:, :, None], jnp.zeros((), bf16))
    total = jnp.dot(rows, base_up_weight, preferred_element_type=f32)
    total = total + jnp.dot(
        spread.reshape(-1, rank_block * owner_count),
        expand.reshape(rank_block * owner_count, columns),
        preferred_element_type=f32,
    )
    return lax.psum_scatter(total, "tensor", scatter_dimension=0, tiled=True).astype(bf16)


vmem = pl.BlockSpec(memory_space=pltpu.VMEM)
anywhere = pl.BlockSpec(memory_space=pl.ANY)


def kernel_call(kernel, name, flops, moved, mib, **specs):
    return pl.pallas_call(
        kernel,
        cost_estimate=pl.CostEstimate(flops=flops, bytes_accessed=moved, transcendentals=0),
        compiler_params=pltpu.CompilerParams(vmem_limit_bytes=mib << 20),
        name=name,
        **specs,
    )


def cut_kernel(block, numbers, small_count, expand, weight, *refs):
    small, refs = refs[:small_count], refs[small_count:]
    across, beside, own, *loaded, held, sem, held_sem = refs
    g, a = lax.axis_index("groups"), lax.axis_index("adapter")
    columns = own.shape[1]
    firsts = (
        lax.bitwise_xor(a, 2 + g) * columns,
        lax.bitwise_xor(a, 1) * columns,
        a * columns,
    )
    copies = []
    for n, (first, target) in enumerate(zip(firsts, (across, beside, own))):
        span = pl.ds(pl.multiple_of(first, lane), columns)
        copies.append(pltpu.make_async_copy(expand.at[0, :, span], target, sem.at[n]))
    for n, (source, target) in enumerate(zip(small, loaded)):
        copies.append(pltpu.make_async_copy(source, target, sem.at[len(firsts) + n]))
    copies += weight_copies(block, numbers, weight, held, held_sem)
    for copy in copies:
        copy.start()
    for copy in copies:
        copy.wait()


def weight_copies(block, numbers, weight, target, sem):
    band_count = sem.shape[1]
    band = weight.shape[0] // band_count
    copies = []
    for n, number in enumerate(numbers):
        span = pl.ds(number * block, block)
        for m in range(band_count):
            rows = pl.ds(m * band, band)
            copies.append(
                pltpu.make_async_copy(weight.at[rows, span], target.at[n, rows], sem.at[n, m])
            )
    return copies


def gather_kernel(offsets, slots, index, *refs):
    owner_count = len(offsets)
    blocks = refs[:owner_count]
    shrink, rows_out, keep, send, slot_out, rows, partial = refs[owner_count:]
    a, t = lax.axis_index("adapter"), lax.axis_index("tensor")
    height, depth = blocks[0].shape
    for j, part in zip(offsets, blocks):
        where = lax.bitwise_xor(a, j)
        rows[pl.ds(pl.multiple_of(where * height, height), height), :] = part[:, :depth]
    quarter = rows.shape[0] // 4
    for i, flip in enumerate((0, 2, 1, 3)):
        start = pl.multiple_of(lax.bitwise_xor(t, flip) * quarter, quarter)
        rows_out[i * quarter : (i + 1) * quarter, :] = rows[pl.ds(start, quarter), :]
    product = lax.dot_general(
        shrink[...], rows[...], (((1,), (1,)), ((), ())), preferred_element_type=f32
    )
    named, table = index[...], slots[...]
    slot = jnp.zeros_like(named)
    for k in range(table.shape[1]):
        slot = jnp.where(named == k, table[:, k : k + 1], slot)
    slot_out[...] = slot
    partial[...] = jnp.where(slot == a, product, 0.0)
    rank_block = partial.shape[0] // 4
    for i, flip in enumerate((0, 2, 1, 3)):
        start = pl.multiple_of(lax.bitwise_xor(t, flip) * rank_block, rank_block)
        target = keep if i < 2 else send
        at = i % 2 * rank_block
        target[at : at + rank_block, :] = partial[pl.ds(start, rank_block), :]


def base_kernel(block, places, numbers, streamed, rows, weight, *refs):
    total, ahead, sem = refs[-3:]
    copies = weight_copies(block, numbers, weight, ahead, sem)
    for copy in copies:
        copy.start()

    @pl.when(lax.axis_index("tensor") >= 0)
    def _():
        for n, (which, index) in enumerate(places):
            total[:, n * block : (n + 1) * block] = jnp.dot(
                rows[...], refs[which][index], preferred_element_type=f32
            )

    bands = sem.shape[1]
    for n in range(len(numbers)):
        for copy in copies[n * bands : (n + 1) * bands]:
            copy.wait()
        if streamed:
            at = (len(places) + n) * block
            total[:, at : at + block] = jnp.dot(
                rows[...], ahead[n], preferred_element_type=f32
            )


def delta_kernel(block, splits, slot, *refs):
    bases, refs = refs[: -len(splits) * 2 - 9], refs[-len(splits) * 2 - 9 :]
    own, shrunk, across, beside, swapped, own_keep, own_send = refs[:7]
    cross_keep, cross_send = refs[7 : 7 + len(splits)], refs[7 + len(splits) : 7 + 2 * len(splits)]
    flat, ordered = refs[-2:]
    g, a, t = (lax.axis_index(name) for name in ("groups", "adapter", "tensor"))
    row_count = bases[0].shape[0]
    quarter = row_count // 4
    merged = shrunk[...].astype(f32)
    spread = [
        jnp.where(slot[...] == lax.bitwise_xor(a, j), merged, 0.0)
        for j in (0, 2 + g, 1, 3 - g)
    ]
    flat[...] = jnp.concatenate(spread, axis=0).T
    for i, turn in enumerate((0, 2, 1, 3)):
        start = pl.multiple_of(lax.bitwise_xor(t, turn) * quarter, quarter)
        ordered[i * quarter : (i + 1) * quarter, :] = flat[pl.ds(start, quarter), :].astype(bf16)
    left = ordered[...]
    at, split = 0, 0
    for base in bases:
        for column in range(0, base.shape[1], block):
            span = slice(at, at + block)
            expand = jnp.concatenate(
                [own[:, span], across[:, span], beside[:, span], swapped[:, span]], axis=0
            )
            total = base[:, column : column + block] + jnp.dot(
                left, expand, preferred_element_type=f32
            )
            if at >= splits[split][1]:
                split += 1
            here = slice(at - splits[split][0], at - splits[split][0] + block)
            own_keep[:, span] = total[:quarter]
            cross_keep[split][:, here] = total[quarter : 2 * quarter]
            own_send[:, span] = total[2 * quarter : 3 * quarter]
            cross_send[split][:, here] = total[3 * quarter :]
            at += block


def column_block(width):
    for size in (512, 256, 128):
        if width % size == 0:
            return size


def paired(
    tokens,
    base_up_weight,
    adapter_shrink_weight,
    adapter_expand_weight,
    row_adapter_index,
    adapter_slot_index,
):
    owner_count = lax.axis_size("adapter")
    g = lax.axis_index("groups")
    height, depth = tokens.shape
    row_count = height * owner_count
    columns = base_up_weight.shape[1]
    rank_block = adapter_expand_weight.shape[1]
    rank = adapter_shrink_weight.shape[2]
    block = column_block(columns)
    block_count = columns // block

    def from_owner(x, first, second):
        pairs = []
        for group, m in ((0, first), (1, second)):
            for s in range(owner_count):
                pairs.append((group * owner_count + s, group * owner_count + (s ^ m)))
        return lax.ppermute(x, ("groups", "adapter"), pairs)

    def from_tensor(x, m):
        return lax.ppermute(x, "tensor", [(s, s ^ m) for s in range(4)])

    def from_group(x):
        return lax.ppermute(x, "groups", [(0, 1), (1, 0)])

    weight = pltpu.with_memory_space_constraint(base_up_weight, pltpu.HBM)
    expand = pltpu.with_memory_space_constraint(adapter_expand_weight, pltpu.HBM)
    offsets = (2, 3, 1)
    blocks = [from_owner(tokens, j, j) for j in offsets]

    cuts = [block_count * k // 14 for k in (0, 4, 8, 11, 14)]
    parts = list(zip(cuts[:-1], cuts[1:]))
    loads = [block_count * k // 14 for k in (0, 4, 8, 11, 13, 14)]
    bands = 4
    small = [
        pltpu.with_memory_space_constraint(x, pltpu.HBM)
        for x in (
            adapter_slot_index.reshape(1, owner_count),
            row_adapter_index.reshape(1, row_count),
            tokens,
            adapter_shrink_weight[0].T,
        )
    ]
    across, beside, own, slots, index, mine, shrink, held = kernel_call(
        functools.partial(cut_kernel, block, range(loads[1]), len(small)),
        "cut_expand",
        1,
        1,
        1,
        in_specs=[anywhere] * (2 + len(small)),
        out_specs=[vmem] * (4 + len(small)),
        out_shape=[pltpu.VMEM((rank_block, w), bf16) for w in (columns,) * 3]
        + [pltpu.VMEM(x.shape, x.dtype) for x in small]
        + [pltpu.VMEM((loads[1], depth, block), bf16)],
        scratch_shapes=[
            pltpu.SemaphoreType.DMA((3 + len(small),)),
            pltpu.SemaphoreType.DMA((loads[1], bands)),
        ],
    )(expand, weight, *small)
    loaded = [held]
    across, beside = from_owner(across, 2, 3), from_owner(beside, 1, 1)

    rows, keep, send, slot = kernel_call(
        functools.partial(gather_kernel, (0, *offsets)),
        "gather_rows",
        1,
        1,
        4,
        in_specs=[vmem] * (owner_count + 3),
        out_specs=[vmem] * 4,
        out_shape=[jax.ShapeDtypeStruct((row_count, depth), bf16)]
        + [jax.ShapeDtypeStruct((rank // 2, row_count), f32)] * 2
        + [jax.ShapeDtypeStruct((1, row_count), jnp.int32)],
        scratch_shapes=[pltpu.VMEM((row_count, depth), bf16), pltpu.VMEM((rank, row_count), f32)],
    )(
        slots,
        index,
        mine,
        *blocks,
        shrink,
    )

    def base_part(n, *after):
        first, last = parts[n]
        streamed = n + 1 == len(parts)
        numbers = range(loads[n + 1], loads[n + 2])
        places, used = [], []
        for number in range(first, numbers[0] if streamed else last):
            source = max(k for k in range(len(loads) - 1) if loads[k] <= number)
            if source not in used:
                used.append(source)
            places.append((used.index(source), number - loads[source]))
        ahead = pltpu.VMEM((len(numbers), depth, block), bf16)
        out = kernel_call(
            functools.partial(base_kernel, block, places, numbers, streamed),
            "base_part",
            (15 * 10**8, 15 * 10**8, 10**10, 1)[n],
            1,
            12,
            in_specs=[vmem, anywhere] + [vmem] * len(used) + [anywhere] * len(after),
            out_specs=[vmem] * (1 if streamed else 2),
            out_shape=[jax.ShapeDtypeStruct((row_count, (last - first) * block), f32)]
            + ([] if streamed else [ahead]),
            scratch_shapes=([ahead] if streamed else [])
            + [pltpu.SemaphoreType.DMA((len(numbers), bands))],
        )(rows, weight, *[loaded[k] for k in used], *after)
        loaded.append(out[-1])
        return out[0]

    arrived = from_tensor(send, 1)
    base_0 = base_part(0, send)
    arrived, base_0 = lax.optimization_barrier((arrived, base_0))
    pair = keep + arrived
    arrived = from_tensor(pair[rank_block:], 2)
    base_1 = base_part(1, pair)
    arrived, base_1 = lax.optimization_barrier((arrived, base_1))
    shrunk = (adapter_scale * (pair[:rank_block] + arrived)).astype(bf16)
    across, _ = lax.optimization_barrier((across, shrunk))
    swapped = from_group(across)
    bases = [base_0, base_1]
    for m, n in ((2, 2), (1, 3)):
        arrived = from_owner(shrunk, m, m)
        base = base_part(n, shrunk, across)
        arrived, base = lax.optimization_barrier((arrived, base))
        bases.append(base)
        shrunk = shrunk + arrived

    middle = block_count * 5 // 14 * block
    splits = [(0, middle), (middle, columns)]
    widths = [last - first for first, last in splits]
    quarter = row_count // 4
    out = kernel_call(
        functools.partial(delta_kernel, block, splits),
        "add_delta",
        1,
        1,
        8,
        in_specs=[vmem] * (len(bases) + 6),
        out_specs=[vmem] * (2 + 2 * len(splits)),
        out_shape=[
            jax.ShapeDtypeStruct((quarter, w), f32) for w in (columns, columns, *widths, *widths)
        ],
        scratch_shapes=[
            pltpu.VMEM((row_count, rank_block * owner_count), f32),
            pltpu.VMEM((row_count, rank_block * owner_count), bf16),
        ],
    )(slot, *bases, own, shrunk, across, beside, swapped)
    own_keep, own_send = out[:2]
    arrived = [from_tensor(x, 1) for x in out[4:6]]
    arrived[1], own_send = lax.optimization_barrier((arrived[1], own_send))
    crossed = [
        from_tensor((keep + other).astype(bf16), 2) for keep, other in zip(out[2:4], arrived)
    ]
    kept = own_keep + from_tensor(own_send, 1)
    return jnp.concatenate(
        [
            (kept[:, first:last] + part.astype(f32)).astype(bf16)
            for (first, last), part in zip(splits, crossed)
        ],
        axis=1,
    )


def on_device(tokens, base_up_weight, adapter_shrink_weight, adapter_expand_weight, *index):
    pairs = lax.axis_size("groups") == 2 and lax.axis_size("tensor") == 4
    few = lax.axis_size("adapter") == 4
    columns = base_up_weight.shape[1]
    even = columns % 512 == 0 and columns >= 4096 and tokens.shape[0] % 16 == 0
    arrange = paired if pairs and few and even else general
    return arrange(
        tokens, base_up_weight, adapter_shrink_weight, adapter_expand_weight, *index
    )


def solution(mesh):
    placed = (
        P(("groups", "adapter"), "tensor"),
        P("tensor", "adapter"),
        P("adapter", "tensor", None),
        P("adapter", "tensor", None),
        P("groups", None),
        P(),
    )
    return jax.shard_map(
        on_device,
        mesh=mesh,
        in_specs=placed,
        out_specs=P(("groups", "tensor"), "adapter"),
        check_vma=False,
    )
```

```python
import functools

import jax
import jax.numpy as jnp
from jax import lax
from jax.experimental import pallas as pl
from jax.experimental.pallas import tpu as pltpu
from jax.sharding import PartitionSpec as P

adapter_scale = 0.5
lane = 128
f32 = jnp.float32
bf16 = jnp.bfloat16


def general(
    tokens,
    base_up_weight,
    adapter_shrink_weight,
    adapter_expand_weight,
    row_adapter_index,
    adapter_slot_index,
):
    owner_count = lax.axis_size("adapter")
    owner_index = lax.axis_index("adapter")
    tensor_index = lax.axis_index("tensor")
    rank_block = adapter_expand_weight.shape[1]
    columns = base_up_weight.shape[1]
    slot = jnp.take(adapter_slot_index, row_adapter_index[:, 0], axis=0)
    rows = lax.all_gather(tokens, "adapter", axis=0, tiled=True)
    expand = adapter_expand_weight[0].reshape(rank_block, owner_count, columns)
    expand = lax.all_to_all(expand, "adapter", split_axis=1, concat_axis=1, tiled=True)
    shrunk = jnp.dot(rows, adapter_shrink_weight[0], preferred_element_type=f32)
    shrunk = jnp.where((slot == owner_index)[:, None], shrunk, 0.0)
    shrunk = lax.psum(shrunk, ("adapter", "tensor"))
    shrunk = (adapter_scale * shrunk).astype(bf16)
    shrunk = lax.dynamic_slice_in_dim(shrunk, tensor_index * rank_block, rank_block, 1)
    chosen = slot[:, None] == jnp.arange(owner_count, dtype=jnp.int32)[None, :]
    spread = jnp.where(chosen[:, None, :], shrunk[:, :, None], jnp.zeros((), bf16))
    total = jnp.dot(rows, base_up_weight, preferred_element_type=f32)
    total = total + jnp.dot(
        spread.reshape(-1, rank_block * owner_count),
        expand.reshape(rank_block * owner_count, columns),
        preferred_element_type=f32,
    )
    return lax.psum_scatter(total, "tensor", scatter_dimension=0, tiled=True).astype(bf16)


vmem = pl.BlockSpec(memory_space=pltpu.VMEM)
anywhere = pl.BlockSpec(memory_space=pl.ANY)


def kernel_call(kernel, name, flops, moved, mib, **specs):
    return pl.pallas_call(
        kernel,
        cost_estimate=pl.CostEstimate(flops=flops, bytes_accessed=moved, transcendentals=0),
        compiler_params=pltpu.CompilerParams(vmem_limit_bytes=mib << 20),
        name=name,
        **specs,
    )


def cut_kernel(block, numbers, small_count, expand, weight, *refs):
    small, refs = refs[:small_count], refs[small_count:]
    across, beside, own, *loaded, held, sem, held_sem = refs
    g, a = lax.axis_index("groups"), lax.axis_index("adapter")
    columns = own.shape[1]
    firsts = (
        lax.bitwise_xor(a, 2 + g) * columns,
        lax.bitwise_xor(a, 1) * columns,
        a * columns,
    )
    copies = []
    for n, (first, target) in enumerate(zip(firsts, (across, beside, own))):
        span = pl.ds(pl.multiple_of(first, lane), columns)
        copies.append(pltpu.make_async_copy(expand.at[0, :, span], target, sem.at[n]))
    for n, (source, target) in enumerate(zip(small, loaded)):
        copies.append(pltpu.make_async_copy(source, target, sem.at[len(firsts) + n]))
    copies += weight_copies(block, numbers, weight, held, held_sem)
    for copy in copies:
        copy.start()
    for copy in copies:
        copy.wait()


def weight_copies(block, numbers, weight, target, sem):
    band_count = sem.shape[1]
    band = weight.shape[0] // band_count
    copies = []
    for n, number in enumerate(numbers):
        span = pl.ds(number * block, block)
        for m in range(band_count):
            rows = pl.ds(m * band, band)
            copies.append(
                pltpu.make_async_copy(weight.at[rows, span], target.at[n, rows], sem.at[n, m])
            )
    return copies


def gather_kernel(offsets, slots, index, *refs):
    owner_count = len(offsets)
    blocks = refs[:owner_count]
    shrink, rows_out, keep, send, slot_out, rows, partial = refs[owner_count:]
    a, t = lax.axis_index("adapter"), lax.axis_index("tensor")
    height, depth = blocks[0].shape
    for j, part in zip(offsets, blocks):
        where = lax.bitwise_xor(a, j)
        rows[pl.ds(pl.multiple_of(where * height, height), height), :] = part[:, :depth]
    quarter = rows.shape[0] // 4
    for i, flip in enumerate((0, 2, 1, 3)):
        start = pl.multiple_of(lax.bitwise_xor(t, flip) * quarter, quarter)
        rows_out[i * quarter : (i + 1) * quarter, :] = rows[pl.ds(start, quarter), :]
    product = lax.dot_general(
        shrink[...], rows[...], (((1,), (1,)), ((), ())), preferred_element_type=f32
    )
    named, table = index[...], slots[...]
    slot = jnp.zeros_like(named)
    for k in range(table.shape[1]):
        slot = jnp.where(named == k, table[:, k : k + 1], slot)
    slot_out[...] = slot
    partial[...] = jnp.where(slot == a, product, 0.0)
    rank_block = partial.shape[0] // 4
    for i, flip in enumerate((0, 2, 1, 3)):
        start = pl.multiple_of(lax.bitwise_xor(t, flip) * rank_block, rank_block)
        target = keep if i < 2 else send
        at = i % 2 * rank_block
        target[at : at + rank_block, :] = partial[pl.ds(start, rank_block), :]


def base_kernel(block, places, numbers, streamed, rows, weight, *refs):
    total, ahead, sem = refs[-3:]
    copies = weight_copies(block, numbers, weight, ahead, sem)
    for copy in copies:
        copy.start()

    @pl.when(lax.axis_index("tensor") >= 0)
    def _():
        for n, (which, index) in enumerate(places):
            total[:, n * block : (n + 1) * block] = jnp.dot(
                rows[...], refs[which][index], preferred_element_type=f32
            )

    bands = sem.shape[1]
    for n in range(len(numbers)):
        for copy in copies[n * bands : (n + 1) * bands]:
            copy.wait()
        if streamed:
            at = (len(places) + n) * block
            total[:, at : at + block] = jnp.dot(
                rows[...], ahead[n], preferred_element_type=f32
            )


def delta_kernel(block, splits, slot, *refs):
    bases, refs = refs[: -len(splits) * 2 - 9], refs[-len(splits) * 2 - 9 :]
    own, shrunk, across, beside, swapped, own_keep, own_send = refs[:7]
    cross_keep, cross_send = refs[7 : 7 + len(splits)], refs[7 + len(splits) : 7 + 2 * len(splits)]
    flat, ordered = refs[-2:]
    g, a, t = (lax.axis_index(name) for name in ("groups", "adapter", "tensor"))
    row_count = bases[0].shape[0]
    quarter = row_count // 4
    merged = shrunk[...].astype(f32)
    spread = [
        jnp.where(slot[...] == lax.bitwise_xor(a, j), merged, 0.0)
        for j in (0, 2 + g, 1, 3 - g)
    ]
    flat[...] = jnp.concatenate(spread, axis=0).T
    for i, turn in enumerate((0, 2, 1, 3)):
        start = pl.multiple_of(lax.bitwise_xor(t, turn) * quarter, quarter)
        ordered[i * quarter : (i + 1) * quarter, :] = flat[pl.ds(start, quarter), :].astype(bf16)
    left = ordered[...]
    at, split = 0, 0
    for base in bases:
        for column in range(0, base.shape[1], block):
            span = slice(at, at + block)
            expand = jnp.concatenate(
                [own[:, span], across[:, span], beside[:, span], swapped[:, span]], axis=0
            )
            total = base[:, column : column + block] + jnp.dot(
                left, expand, preferred_element_type=f32
            )
            if at >= splits[split][1]:
                split += 1
            here = slice(at - splits[split][0], at - splits[split][0] + block)
            own_keep[:, span] = total[:quarter]
            cross_keep[split][:, here] = total[quarter : 2 * quarter]
            own_send[:, span] = total[2 * quarter : 3 * quarter]
            cross_send[split][:, here] = total[3 * quarter :]
            at += block


def column_block(width):
    for size in (512, 256, 128):
        if width % size == 0:
            return size


def paired(
    tokens,
    base_up_weight,
    adapter_shrink_weight,
    adapter_expand_weight,
    row_adapter_index,
    adapter_slot_index,
):
    owner_count = lax.axis_size("adapter")
    g = lax.axis_index("groups")
    height, depth = tokens.shape
    row_count = height * owner_count
    columns = base_up_weight.shape[1]
    rank_block = adapter_expand_weight.shape[1]
    rank = adapter_shrink_weight.shape[2]
    block = column_block(columns)
    block_count = columns // block

    def from_owner(x, first, second):
        pairs = []
        for group, m in ((0, first), (1, second)):
            for s in range(owner_count):
                pairs.append((group * owner_count + s, group * owner_count + (s ^ m)))
        return lax.ppermute(x, ("groups", "adapter"), pairs)

    def from_tensor(x, m):
        return lax.ppermute(x, "tensor", [(s, s ^ m) for s in range(4)])

    def from_group(x):
        return lax.ppermute(x, "groups", [(0, 1), (1, 0)])

    weight = pltpu.with_memory_space_constraint(base_up_weight, pltpu.HBM)
    expand = pltpu.with_memory_space_constraint(adapter_expand_weight, pltpu.HBM)
    offsets = (2, 3, 1)
    blocks = [from_owner(tokens, j, j) for j in offsets]

    cuts = [block_count * k // 14 for k in (0, 4, 8, 11, 14)]
    parts = list(zip(cuts[:-1], cuts[1:]))
    loads = [block_count * k // 14 for k in (0, 4, 8, 11, 13, 14)]
    bands = 4
    small = [
        pltpu.with_memory_space_constraint(x, pltpu.HBM)
        for x in (
            adapter_slot_index.reshape(1, owner_count),
            row_adapter_index.reshape(1, row_count),
            tokens,
            adapter_shrink_weight[0].T,
        )
    ]
    across, beside, own, slots, index, mine, shrink, held = kernel_call(
        functools.partial(cut_kernel, block, range(loads[1]), len(small)),
        "cut_expand",
        1,
        1,
        1,
        in_specs=[anywhere] * (2 + len(small)),
        out_specs=[vmem] * (4 + len(small)),
        out_shape=[pltpu.VMEM((rank_block, w), bf16) for w in (columns,) * 3]
        + [pltpu.VMEM(x.shape, x.dtype) for x in small]
        + [pltpu.VMEM((loads[1], depth, block), bf16)],
        scratch_shapes=[
            pltpu.SemaphoreType.DMA((3 + len(small),)),
            pltpu.SemaphoreType.DMA((loads[1], bands)),
        ],
    )(expand, weight, *small)
    loaded = [held]
    across, beside = from_owner(across, 2, 3), from_owner(beside, 1, 1)

    rows, keep, send, slot = kernel_call(
        functools.partial(gather_kernel, (0, *offsets)),
        "gather_rows",
        1,
        1,
        4,
        in_specs=[vmem] * (owner_count + 3),
        out_specs=[vmem] * 4,
        out_shape=[jax.ShapeDtypeStruct((row_count, depth), bf16)]
        + [jax.ShapeDtypeStruct((rank // 2, row_count), f32)] * 2
        + [jax.ShapeDtypeStruct((1, row_count), jnp.int32)],
        scratch_shapes=[pltpu.VMEM((row_count, depth), bf16), pltpu.VMEM((rank, row_count), f32)],
    )(
        slots,
        index,
        mine,
        *blocks,
        shrink,
    )

    def base_part(n, *after):
        first, last = parts[n]
        streamed = n + 1 == len(parts)
        numbers = range(loads[n + 1], loads[n + 2])
        places, used = [], []
        for number in range(first, numbers[0] if streamed else last):
            source = max(k for k in range(len(loads) - 1) if loads[k] <= number)
            if source not in used:
                used.append(source)
            places.append((used.index(source), number - loads[source]))
        ahead = pltpu.VMEM((len(numbers), depth, block), bf16)
        out = kernel_call(
            functools.partial(base_kernel, block, places, numbers, streamed),
            "base_part",
            (15 * 10**8, 15 * 10**8, 10**10, 1)[n],
            1,
            12,
            in_specs=[vmem, anywhere] + [vmem] * len(used) + [anywhere] * len(after),
            out_specs=[vmem] * (1 if streamed else 2),
            out_shape=[jax.ShapeDtypeStruct((row_count, (last - first) * block), f32)]
            + ([] if streamed else [ahead]),
            scratch_shapes=([ahead] if streamed else [])
            + [pltpu.SemaphoreType.DMA((len(numbers), bands))],
        )(rows, weight, *[loaded[k] for k in used], *after)
        loaded.append(out[-1])
        return out[0]

    arrived = from_tensor(send, 1)
    base_0 = base_part(0, send)
    arrived, base_0 = lax.optimization_barrier((arrived, base_0))
    pair = keep + arrived
    arrived = from_tensor(pair[rank_block:], 2)
    base_1 = base_part(1, pair)
    arrived, base_1 = lax.optimization_barrier((arrived, base_1))
    shrunk = (adapter_scale * (pair[:rank_block] + arrived)).astype(bf16)
    across, _ = lax.optimization_barrier((across, shrunk))
    swapped = from_group(across)
    bases = [base_0, base_1]
    for m, n in ((2, 2), (1, 3)):
        arrived = from_owner(shrunk, m, m)
        base = base_part(n, shrunk, across)
        arrived, base = lax.optimization_barrier((arrived, base))
        bases.append(base)
        shrunk = shrunk + arrived

    edges = [block_count * k // 14 * block for k in (0, 4, 9, 14)]
    splits = list(zip(edges[:-1], edges[1:]))
    widths = [last - first for first, last in splits]
    quarter = row_count // 4
    out = kernel_call(
        functools.partial(delta_kernel, block, splits),
        "add_delta",
        1,
        1,
        8,
        in_specs=[vmem] * (len(bases) + 6),
        out_specs=[vmem] * (2 + 2 * len(splits)),
        out_shape=[
            jax.ShapeDtypeStruct((quarter, w), f32) for w in (columns, columns, *widths, *widths)
        ],
        scratch_shapes=[
            pltpu.VMEM((row_count, rank_block * owner_count), f32),
            pltpu.VMEM((row_count, rank_block * owner_count), bf16),
        ],
    )(slot, *bases, own, shrunk, across, beside, swapped)
    own_keep, own_send = out[:2]
    cross_keep, cross_send = out[2 : 2 + len(splits)], out[2 + len(splits) :]
    arrived = [from_tensor(x, 1) for x in cross_send]
    arrived[-1], own_send = lax.optimization_barrier((arrived[-1], own_send))
    crossed = [
        from_tensor((keep + other).astype(bf16), 2) for keep, other in zip(cross_keep, arrived)
    ]
    kept = own_keep + from_tensor(own_send, 1)
    return jnp.concatenate(
        [
            (kept[:, first:last] + part.astype(f32)).astype(bf16)
            for (first, last), part in zip(splits, crossed)
        ],
        axis=1,
    )


def on_device(tokens, base_up_weight, adapter_shrink_weight, adapter_expand_weight, *index):
    pairs = lax.axis_size("groups") == 2 and lax.axis_size("tensor") == 4
    few = lax.axis_size("adapter") == 4
    columns = base_up_weight.shape[1]
    even = columns % 512 == 0 and columns >= 4096 and tokens.shape[0] % 16 == 0
    arrange = paired if pairs and few and even else general
    return arrange(
        tokens, base_up_weight, adapter_shrink_weight, adapter_expand_weight, *index
    )


def solution(mesh):
    placed = (
        P(("groups", "adapter"), "tensor"),
        P("tensor", "adapter"),
        P("adapter", "tensor", None),
        P("adapter", "tensor", None),
        P("groups", None),
        P(),
    )
    return jax.shard_map(
        on_device,
        mesh=mesh,
        in_specs=placed,
        out_specs=P(("groups", "tensor"), "adapter"),
        check_vma=False,
    )
```

```python
import functools

import jax
import jax.numpy as jnp
from jax import lax
from jax.experimental import pallas as pl
from jax.experimental.pallas import tpu as pltpu
from jax.sharding import PartitionSpec as P

adapter_scale = 0.5
lane = 128
f32 = jnp.float32
bf16 = jnp.bfloat16


def general(
    tokens,
    base_up_weight,
    adapter_shrink_weight,
    adapter_expand_weight,
    row_adapter_index,
    adapter_slot_index,
):
    owner_count = lax.axis_size("adapter")
    owner_index = lax.axis_index("adapter")
    tensor_index = lax.axis_index("tensor")
    rank_block = adapter_expand_weight.shape[1]
    columns = base_up_weight.shape[1]
    slot = jnp.take(adapter_slot_index, row_adapter_index[:, 0], axis=0)
    rows = lax.all_gather(tokens, "adapter", axis=0, tiled=True)
    expand = adapter_expand_weight[0].reshape(rank_block, owner_count, columns)
    expand = lax.all_to_all(expand, "adapter", split_axis=1, concat_axis=1, tiled=True)
    shrunk = jnp.dot(rows, adapter_shrink_weight[0], preferred_element_type=f32)
    shrunk = jnp.where((slot == owner_index)[:, None], shrunk, 0.0)
    shrunk = lax.psum(shrunk, ("adapter", "tensor"))
    shrunk = (adapter_scale * shrunk).astype(bf16)
    shrunk = lax.dynamic_slice_in_dim(shrunk, tensor_index * rank_block, rank_block, 1)
    chosen = slot[:, None] == jnp.arange(owner_count, dtype=jnp.int32)[None, :]
    spread = jnp.where(chosen[:, None, :], shrunk[:, :, None], jnp.zeros((), bf16))
    total = jnp.dot(rows, base_up_weight, preferred_element_type=f32)
    total = total + jnp.dot(
        spread.reshape(-1, rank_block * owner_count),
        expand.reshape(rank_block * owner_count, columns),
        preferred_element_type=f32,
    )
    return lax.psum_scatter(total, "tensor", scatter_dimension=0, tiled=True).astype(bf16)


vmem = pl.BlockSpec(memory_space=pltpu.VMEM)
anywhere = pl.BlockSpec(memory_space=pl.ANY)


def kernel_call(kernel, name, flops, moved, mib, **specs):
    return pl.pallas_call(
        kernel,
        cost_estimate=pl.CostEstimate(flops=flops, bytes_accessed=moved, transcendentals=0),
        compiler_params=pltpu.CompilerParams(vmem_limit_bytes=mib << 20),
        name=name,
        **specs,
    )


def cut_kernel(block, numbers, small_count, expand, weight, *refs):
    small, refs = refs[:small_count], refs[small_count:]
    across, beside, own, *loaded, held, sem, held_sem = refs
    g, a = lax.axis_index("groups"), lax.axis_index("adapter")
    columns = own.shape[1]
    firsts = (
        lax.bitwise_xor(a, 2 + g) * columns,
        lax.bitwise_xor(a, 1) * columns,
        a * columns,
    )
    copies = []
    for n, (first, target) in enumerate(zip(firsts, (across, beside, own))):
        span = pl.ds(pl.multiple_of(first, lane), columns)
        copies.append(pltpu.make_async_copy(expand.at[0, :, span], target, sem.at[n]))
    for n, (source, target) in enumerate(zip(small, loaded)):
        copies.append(pltpu.make_async_copy(source, target, sem.at[len(firsts) + n]))
    copies += weight_copies(block, numbers, weight, held, held_sem)
    for copy in copies:
        copy.start()
    for copy in copies:
        copy.wait()


def weight_copies(block, numbers, weight, target, sem):
    band_count = sem.shape[1]
    band = weight.shape[0] // band_count
    copies = []
    for n, number in enumerate(numbers):
        span = pl.ds(number * block, block)
        for m in range(band_count):
            rows = pl.ds(m * band, band)
            copies.append(
                pltpu.make_async_copy(weight.at[rows, span], target.at[n, rows], sem.at[n, m])
            )
    return copies


def gather_kernel(offsets, slots, index, *refs):
    owner_count = len(offsets)
    blocks = refs[:owner_count]
    shrink, rows_out, keep, send, slot_out, rows, partial = refs[owner_count:]
    a, t = lax.axis_index("adapter"), lax.axis_index("tensor")
    height, depth = blocks[0].shape
    for j, part in zip(offsets, blocks):
        where = lax.bitwise_xor(a, j)
        rows[pl.ds(pl.multiple_of(where * height, height), height), :] = part[:, :depth]
    quarter = rows.shape[0] // 4
    for i, flip in enumerate((0, 2, 1, 3)):
        start = pl.multiple_of(lax.bitwise_xor(t, flip) * quarter, quarter)
        rows_out[i * quarter : (i + 1) * quarter, :] = rows[pl.ds(start, quarter), :]
    product = lax.dot_general(
        shrink[...], rows[...], (((1,), (1,)), ((), ())), preferred_element_type=f32
    )
    named, table = index[...], slots[...]
    slot = jnp.zeros_like(named)
    for k in range(table.shape[1]):
        slot = jnp.where(named == k, table[:, k : k + 1], slot)
    slot_out[...] = slot
    partial[...] = jnp.where(slot == a, product, 0.0)
    rank_block = partial.shape[0] // 4
    for i, flip in enumerate((0, 2, 1, 3)):
        start = pl.multiple_of(lax.bitwise_xor(t, flip) * rank_block, rank_block)
        target = keep if i < 2 else send
        at = i % 2 * rank_block
        target[at : at + rank_block, :] = partial[pl.ds(start, rank_block), :]


def base_kernel(block, places, numbers, streamed, rows, weight, *refs):
    total, ahead, sem = refs[-3:]
    copies = weight_copies(block, numbers, weight, ahead, sem)
    for copy in copies:
        copy.start()

    @pl.when(lax.axis_index("tensor") >= 0)
    def _():
        for n, (which, index) in enumerate(places):
            total[:, n * block : (n + 1) * block] = jnp.dot(
                rows[...], refs[which][index], preferred_element_type=f32
            )

    bands = sem.shape[1]
    for n in range(len(numbers)):
        for copy in copies[n * bands : (n + 1) * bands]:
            copy.wait()
        if streamed:
            at = (len(places) + n) * block
            total[:, at : at + block] = jnp.dot(
                rows[...], ahead[n], preferred_element_type=f32
            )


def delta_kernel(block, splits, slot, *refs):
    bases, refs = refs[: -len(splits) * 2 - 9], refs[-len(splits) * 2 - 9 :]
    own, shrunk, across, beside, swapped, own_keep, own_send = refs[:7]
    cross_keep, cross_send = refs[7 : 7 + len(splits)], refs[7 + len(splits) : 7 + 2 * len(splits)]
    flat, ordered = refs[-2:]
    g, a, t = (lax.axis_index(name) for name in ("groups", "adapter", "tensor"))
    row_count = bases[0].shape[0]
    quarter = row_count // 4
    merged = shrunk[...].astype(f32)
    spread = [
        jnp.where(slot[...] == lax.bitwise_xor(a, j), merged, 0.0)
        for j in (0, 2 + g, 1, 3 - g)
    ]
    flat[...] = jnp.concatenate(spread, axis=0).T
    for i, turn in enumerate((0, 2, 1, 3)):
        start = pl.multiple_of(lax.bitwise_xor(t, turn) * quarter, quarter)
        ordered[i * quarter : (i + 1) * quarter, :] = flat[pl.ds(start, quarter), :].astype(bf16)
    left = ordered[...]
    at, split = 0, 0
    for base in bases:
        for column in range(0, base.shape[1], block):
            span = slice(at, at + block)
            expand = jnp.concatenate(
                [own[:, span], across[:, span], beside[:, span], swapped[:, span]], axis=0
            )
            total = base[:, column : column + block] + jnp.dot(
                left, expand, preferred_element_type=f32
            )
            if at >= splits[split][1]:
                split += 1
            here = slice(at - splits[split][0], at - splits[split][0] + block)
            own_keep[:, span] = total[:quarter]
            cross_keep[split][:, here] = total[quarter : 2 * quarter]
            own_send[:, span] = total[2 * quarter : 3 * quarter]
            cross_send[split][:, here] = total[3 * quarter :]
            at += block


def column_block(width):
    for size in (512, 256, 128):
        if width % size == 0:
            return size


def paired(
    tokens,
    base_up_weight,
    adapter_shrink_weight,
    adapter_expand_weight,
    row_adapter_index,
    adapter_slot_index,
):
    owner_count = lax.axis_size("adapter")
    g = lax.axis_index("groups")
    height, depth = tokens.shape
    row_count = height * owner_count
    columns = base_up_weight.shape[1]
    rank_block = adapter_expand_weight.shape[1]
    rank = adapter_shrink_weight.shape[2]
    block = column_block(columns)
    block_count = columns // block

    def from_owner(x, first, second):
        pairs = []
        for group, m in ((0, first), (1, second)):
            for s in range(owner_count):
                pairs.append((group * owner_count + s, group * owner_count + (s ^ m)))
        return lax.ppermute(x, ("groups", "adapter"), pairs)

    def from_tensor(x, m):
        return lax.ppermute(x, "tensor", [(s, s ^ m) for s in range(4)])

    def from_group(x):
        return lax.ppermute(x, "groups", [(0, 1), (1, 0)])

    weight = pltpu.with_memory_space_constraint(base_up_weight, pltpu.HBM)
    expand = pltpu.with_memory_space_constraint(adapter_expand_weight, pltpu.HBM)
    offsets = (2, 3, 1)
    blocks = [from_owner(tokens, j, j) for j in offsets]

    cuts = [block_count * k // 14 for k in (0, 4, 8, 11, 14)]
    parts = list(zip(cuts[:-1], cuts[1:]))
    loads = [block_count * k // 14 for k in (0, 5, 8, 11, 13, 14)]
    bands = 4
    small = [
        pltpu.with_memory_space_constraint(x, pltpu.HBM)
        for x in (
            adapter_slot_index.reshape(1, owner_count),
            row_adapter_index.reshape(1, row_count),
            tokens,
            adapter_shrink_weight[0].T,
        )
    ]
    across, beside, own, slots, index, mine, shrink, held = kernel_call(
        functools.partial(cut_kernel, block, range(loads[1]), len(small)),
        "cut_expand",
        1,
        1,
        1,
        in_specs=[anywhere] * (2 + len(small)),
        out_specs=[vmem] * (4 + len(small)),
        out_shape=[pltpu.VMEM((rank_block, w), bf16) for w in (columns,) * 3]
        + [pltpu.VMEM(x.shape, x.dtype) for x in small]
        + [pltpu.VMEM((loads[1], depth, block), bf16)],
        scratch_shapes=[
            pltpu.SemaphoreType.DMA((3 + len(small),)),
            pltpu.SemaphoreType.DMA((loads[1], bands)),
        ],
    )(expand, weight, *small)
    loaded = [held]
    across, beside = from_owner(across, 2, 3), from_owner(beside, 1, 1)

    rows, keep, send, slot = kernel_call(
        functools.partial(gather_kernel, (0, *offsets)),
        "gather_rows",
        1,
        1,
        4,
        in_specs=[vmem] * (owner_count + 3),
        out_specs=[vmem] * 4,
        out_shape=[jax.ShapeDtypeStruct((row_count, depth), bf16)]
        + [jax.ShapeDtypeStruct((rank // 2, row_count), f32)] * 2
        + [jax.ShapeDtypeStruct((1, row_count), jnp.int32)],
        scratch_shapes=[pltpu.VMEM((row_count, depth), bf16), pltpu.VMEM((rank, row_count), f32)],
    )(
        slots,
        index,
        mine,
        *blocks,
        shrink,
    )

    def base_part(n, *after):
        first, last = parts[n]
        streamed = n + 1 == len(parts)
        numbers = range(loads[n + 1], loads[n + 2])
        places, used = [], []
        for number in range(first, numbers[0] if streamed else last):
            source = max(k for k in range(len(loads) - 1) if loads[k] <= number)
            if source not in used:
                used.append(source)
            places.append((used.index(source), number - loads[source]))
        ahead = pltpu.VMEM((len(numbers), depth, block), bf16)
        out = kernel_call(
            functools.partial(base_kernel, block, places, numbers, streamed),
            "base_part",
            (15 * 10**8, 15 * 10**8, 10**10, 1)[n],
            1,
            12,
            in_specs=[vmem, anywhere] + [vmem] * len(used) + [anywhere] * len(after),
            out_specs=[vmem] * (1 if streamed else 2),
            out_shape=[jax.ShapeDtypeStruct((row_count, (last - first) * block), f32)]
            + ([] if streamed else [ahead]),
            scratch_shapes=([ahead] if streamed else [])
            + [pltpu.SemaphoreType.DMA((len(numbers), bands))],
        )(rows, weight, *[loaded[k] for k in used], *after)
        loaded.append(out[-1])
        return out[0]

    arrived = from_tensor(send, 1)
    base_0 = base_part(0, send)
    arrived, base_0 = lax.optimization_barrier((arrived, base_0))
    pair = keep + arrived
    arrived = from_tensor(pair[rank_block:], 2)
    base_1 = base_part(1, pair)
    arrived, base_1 = lax.optimization_barrier((arrived, base_1))
    shrunk = (adapter_scale * (pair[:rank_block] + arrived)).astype(bf16)
    across, _ = lax.optimization_barrier((across, shrunk))
    swapped = from_group(across)
    bases = [base_0, base_1]
    for m, n in ((2, 2), (1, 3)):
        arrived = from_owner(shrunk, m, m)
        base = base_part(n, shrunk, across)
        arrived, base = lax.optimization_barrier((arrived, base))
        bases.append(base)
        shrunk = shrunk + arrived

    middle = block_count * 5 // 14 * block
    splits = [(0, middle), (middle, columns)]
    widths = [last - first for first, last in splits]
    quarter = row_count // 4
    out = kernel_call(
        functools.partial(delta_kernel, block, splits),
        "add_delta",
        1,
        1,
        8,
        in_specs=[vmem] * (len(bases) + 6),
        out_specs=[vmem] * (2 + 2 * len(splits)),
        out_shape=[
            jax.ShapeDtypeStruct((quarter, w), f32) for w in (columns, columns, *widths, *widths)
        ],
        scratch_shapes=[
            pltpu.VMEM((row_count, rank_block * owner_count), f32),
            pltpu.VMEM((row_count, rank_block * owner_count), bf16),
        ],
    )(slot, *bases, own, shrunk, across, beside, swapped)
    own_keep, own_send = out[:2]
    arrived = [from_tensor(x, 1) for x in out[4:6]]
    arrived[1], own_send = lax.optimization_barrier((arrived[1], own_send))
    crossed = [
        from_tensor((keep + other).astype(bf16), 2) for keep, other in zip(out[2:4], arrived)
    ]
    kept = own_keep + from_tensor(own_send, 1)
    return jnp.concatenate(
        [
            (kept[:, first:last] + part.astype(f32)).astype(bf16)
            for (first, last), part in zip(splits, crossed)
        ],
        axis=1,
    )


def on_device(tokens, base_up_weight, adapter_shrink_weight, adapter_expand_weight, *index):
    pairs = lax.axis_size("groups") == 2 and lax.axis_size("tensor") == 4
    few = lax.axis_size("adapter") == 4
    columns = base_up_weight.shape[1]
    even = columns % 512 == 0 and columns >= 4096 and tokens.shape[0] % 16 == 0
    arrange = paired if pairs and few and even else general
    return arrange(
        tokens, base_up_weight, adapter_shrink_weight, adapter_expand_weight, *index
    )


def solution(mesh):
    placed = (
        P(("groups", "adapter"), "tensor"),
        P("tensor", "adapter"),
        P("adapter", "tensor", None),
        P("adapter", "tensor", None),
        P("groups", None),
        P(),
    )
    return jax.shard_map(
        on_device,
        mesh=mesh,
        in_specs=placed,
        out_specs=P(("groups", "tensor"), "adapter"),
        check_vma=False,
    )
```

```python
import functools

import jax
import jax.numpy as jnp
from jax import lax
from jax.experimental import pallas as pl
from jax.experimental.pallas import tpu as pltpu
from jax.sharding import PartitionSpec as P

adapter_scale = 0.5
lane = 128
f32 = jnp.float32
bf16 = jnp.bfloat16


def general(
    tokens,
    base_up_weight,
    adapter_shrink_weight,
    adapter_expand_weight,
    row_adapter_index,
    adapter_slot_index,
):
    owner_count = lax.axis_size("adapter")
    owner_index = lax.axis_index("adapter")
    tensor_index = lax.axis_index("tensor")
    rank_block = adapter_expand_weight.shape[1]
    columns = base_up_weight.shape[1]
    slot = jnp.take(adapter_slot_index, row_adapter_index[:, 0], axis=0)
    rows = lax.all_gather(tokens, "adapter", axis=0, tiled=True)
    expand = adapter_expand_weight[0].reshape(rank_block, owner_count, columns)
    expand = lax.all_to_all(expand, "adapter", split_axis=1, concat_axis=1, tiled=True)
    shrunk = jnp.dot(rows, adapter_shrink_weight[0], preferred_element_type=f32)
    shrunk = jnp.where((slot == owner_index)[:, None], shrunk, 0.0)
    shrunk = lax.psum(shrunk, ("adapter", "tensor"))
    shrunk = (adapter_scale * shrunk).astype(bf16)
    shrunk = lax.dynamic_slice_in_dim(shrunk, tensor_index * rank_block, rank_block, 1)
    chosen = slot[:, None] == jnp.arange(owner_count, dtype=jnp.int32)[None, :]
    spread = jnp.where(chosen[:, None, :], shrunk[:, :, None], jnp.zeros((), bf16))
    total = jnp.dot(rows, base_up_weight, preferred_element_type=f32)
    total = total + jnp.dot(
        spread.reshape(-1, rank_block * owner_count),
        expand.reshape(rank_block * owner_count, columns),
        preferred_element_type=f32,
    )
    return lax.psum_scatter(total, "tensor", scatter_dimension=0, tiled=True).astype(bf16)


vmem = pl.BlockSpec(memory_space=pltpu.VMEM)
anywhere = pl.BlockSpec(memory_space=pl.ANY)


def kernel_call(kernel, name, flops, moved, mib, **specs):
    return pl.pallas_call(
        kernel,
        cost_estimate=pl.CostEstimate(flops=flops, bytes_accessed=moved, transcendentals=0),
        compiler_params=pltpu.CompilerParams(vmem_limit_bytes=mib << 20),
        name=name,
        **specs,
    )


def cut_kernel(block, numbers, small_count, expand, weight, *refs):
    small, refs = refs[:small_count], refs[small_count:]
    across, beside, own, *loaded, held, sem, held_sem = refs
    g, a = lax.axis_index("groups"), lax.axis_index("adapter")
    columns = own.shape[1]
    firsts = (
        lax.bitwise_xor(a, 2 + g) * columns,
        lax.bitwise_xor(a, 1) * columns,
        a * columns,
    )
    copies = []
    for n, (first, target) in enumerate(zip(firsts, (across, beside, own))):
        span = pl.ds(pl.multiple_of(first, lane), columns)
        copies.append(pltpu.make_async_copy(expand.at[0, :, span], target, sem.at[n]))
    for n, (source, target) in enumerate(zip(small, loaded)):
        copies.append(pltpu.make_async_copy(source, target, sem.at[len(firsts) + n]))
    copies += weight_copies(block, numbers, weight, held, held_sem)
    for copy in copies:
        copy.start()
    for copy in copies:
        copy.wait()


def weight_copies(block, numbers, weight, target, sem):
    band_count = sem.shape[1]
    band = weight.shape[0] // band_count
    copies = []
    for n, number in enumerate(numbers):
        span = pl.ds(number * block, block)
        for m in range(band_count):
            rows = pl.ds(m * band, band)
            copies.append(
                pltpu.make_async_copy(weight.at[rows, span], target.at[n, rows], sem.at[n, m])
            )
    return copies


def gather_kernel(offsets, slots, index, *refs):
    owner_count = len(offsets)
    blocks = refs[:owner_count]
    shrink, rows_out, keep, send, slot_out, rows, partial = refs[owner_count:]
    a, t = lax.axis_index("adapter"), lax.axis_index("tensor")
    height, depth = blocks[0].shape
    for j, part in zip(offsets, blocks):
        where = lax.bitwise_xor(a, j)
        rows[pl.ds(pl.multiple_of(where * height, height), height), :] = part[:, :depth]
    quarter = rows.shape[0] // 4
    for i, flip in enumerate((0, 2, 1, 3)):
        start = pl.multiple_of(lax.bitwise_xor(t, flip) * quarter, quarter)
        rows_out[i * quarter : (i + 1) * quarter, :] = rows[pl.ds(start, quarter), :]
    product = lax.dot_general(
        shrink[...], rows[...], (((1,), (1,)), ((), ())), preferred_element_type=f32
    )
    named, table = index[...], slots[...]
    slot = jnp.zeros_like(named)
    for k in range(table.shape[1]):
        slot = jnp.where(named == k, table[:, k : k + 1], slot)
    slot_out[...] = slot
    partial[...] = jnp.where(slot == a, product, 0.0)
    rank_block = partial.shape[0] // 4
    for i, flip in enumerate((0, 2, 1, 3)):
        start = pl.multiple_of(lax.bitwise_xor(t, flip) * rank_block, rank_block)
        target = keep if i < 2 else send
        at = i % 2 * rank_block
        target[at : at + rank_block, :] = partial[pl.ds(start, rank_block), :]


def base_kernel(block, places, numbers, streamed, rows, weight, *refs):
    total, ahead, sem = refs[-3:]
    copies = weight_copies(block, numbers, weight, ahead, sem)
    for copy in copies:
        copy.start()

    @pl.when(lax.axis_index("tensor") >= 0)
    def _():
        for n, (which, index) in enumerate(places):
            total[:, n * block : (n + 1) * block] = jnp.dot(
                rows[...], refs[which][index], preferred_element_type=f32
            )

    bands = sem.shape[1]
    for n in range(len(numbers)):
        for copy in copies[n * bands : (n + 1) * bands]:
            copy.wait()
        if streamed:
            at = (len(places) + n) * block
            total[:, at : at + block] = jnp.dot(
                rows[...], ahead[n], preferred_element_type=f32
            )


def delta_kernel(block, splits, slot, *refs):
    bases, refs = refs[: -len(splits) * 2 - 9], refs[-len(splits) * 2 - 9 :]
    own, shrunk, across, beside, swapped, own_keep, own_send = refs[:7]
    cross_keep, cross_send = refs[7 : 7 + len(splits)], refs[7 + len(splits) : 7 + 2 * len(splits)]
    flat, ordered = refs[-2:]
    g, a, t = (lax.axis_index(name) for name in ("groups", "adapter", "tensor"))
    row_count = bases[0].shape[0]
    quarter = row_count // 4
    merged = shrunk[...].astype(f32)
    spread = [
        jnp.where(slot[...] == lax.bitwise_xor(a, j), merged, 0.0)
        for j in (0, 2 + g, 1, 3 - g)
    ]
    flat[...] = jnp.concatenate(spread, axis=0).T
    for i, turn in enumerate((0, 2, 1, 3)):
        start = pl.multiple_of(lax.bitwise_xor(t, turn) * quarter, quarter)
        ordered[i * quarter : (i + 1) * quarter, :] = flat[pl.ds(start, quarter), :].astype(bf16)
    left = ordered[...]
    at, split = 0, 0
    for base in bases:
        for column in range(0, base.shape[1], block):
            span = slice(at, at + block)
            expand = jnp.concatenate(
                [own[:, span], across[:, span], beside[:, span], swapped[:, span]], axis=0
            )
            total = base[:, column : column + block] + jnp.dot(
                left, expand, preferred_element_type=f32
            )
            if at >= splits[split][1]:
                split += 1
            here = slice(at - splits[split][0], at - splits[split][0] + block)
            own_keep[:, span] = total[:quarter]
            cross_keep[split][:, here] = total[quarter : 2 * quarter]
            own_send[:, span] = total[2 * quarter : 3 * quarter]
            cross_send[split][:, here] = total[3 * quarter :]
            at += block


def column_block(width):
    for size in (512, 256, 128):
        if width % size == 0:
            return size


def paired(
    tokens,
    base_up_weight,
    adapter_shrink_weight,
    adapter_expand_weight,
    row_adapter_index,
    adapter_slot_index,
):
    owner_count = lax.axis_size("adapter")
    g = lax.axis_index("groups")
    height, depth = tokens.shape
    row_count = height * owner_count
    columns = base_up_weight.shape[1]
    rank_block = adapter_expand_weight.shape[1]
    rank = adapter_shrink_weight.shape[2]
    block = column_block(columns)
    block_count = columns // block

    def from_owner(x, first, second):
        pairs = []
        for group, m in ((0, first), (1, second)):
            for s in range(owner_count):
                pairs.append((group * owner_count + s, group * owner_count + (s ^ m)))
        return lax.ppermute(x, ("groups", "adapter"), pairs)

    def from_tensor(x, m):
        return lax.ppermute(x, "tensor", [(s, s ^ m) for s in range(4)])

    def from_group(x):
        return lax.ppermute(x, "groups", [(0, 1), (1, 0)])

    weight = pltpu.with_memory_space_constraint(base_up_weight, pltpu.HBM)
    expand = pltpu.with_memory_space_constraint(adapter_expand_weight, pltpu.HBM)
    offsets = (2, 3, 1)
    blocks = [from_owner(tokens, j, j) for j in offsets]

    cuts = [block_count * k // 14 for k in (0, 4, 8, 11, 14)]
    parts = list(zip(cuts[:-1], cuts[1:]))
    loads = [block_count * k // 14 for k in (0, 4, 8, 11, 12, 14)]
    bands = 4
    small = [
        pltpu.with_memory_space_constraint(x, pltpu.HBM)
        for x in (
            adapter_slot_index.reshape(1, owner_count),
            row_adapter_index.reshape(1, row_count),
            tokens,
            adapter_shrink_weight[0].T,
        )
    ]
    across, beside, own, slots, index, mine, shrink, held = kernel_call(
        functools.partial(cut_kernel, block, range(loads[1]), len(small)),
        "cut_expand",
        1,
        1,
        1,
        in_specs=[anywhere] * (2 + len(small)),
        out_specs=[vmem] * (4 + len(small)),
        out_shape=[pltpu.VMEM((rank_block, w), bf16) for w in (columns,) * 3]
        + [pltpu.VMEM(x.shape, x.dtype) for x in small]
        + [pltpu.VMEM((loads[1], depth, block), bf16)],
        scratch_shapes=[
            pltpu.SemaphoreType.DMA((3 + len(small),)),
            pltpu.SemaphoreType.DMA((loads[1], bands)),
        ],
    )(expand, weight, *small)
    loaded = [held]
    across, beside = from_owner(across, 2, 3), from_owner(beside, 1, 1)

    rows, keep, send, slot = kernel_call(
        functools.partial(gather_kernel, (0, *offsets)),
        "gather_rows",
        1,
        1,
        4,
        in_specs=[vmem] * (owner_count + 3),
        out_specs=[vmem] * 4,
        out_shape=[jax.ShapeDtypeStruct((row_count, depth), bf16)]
        + [jax.ShapeDtypeStruct((rank // 2, row_count), f32)] * 2
        + [jax.ShapeDtypeStruct((1, row_count), jnp.int32)],
        scratch_shapes=[pltpu.VMEM((row_count, depth), bf16), pltpu.VMEM((rank, row_count), f32)],
    )(
        slots,
        index,
        mine,
        *blocks,
        shrink,
    )

    def base_part(n, *after):
        first, last = parts[n]
        streamed = n + 1 == len(parts)
        numbers = range(loads[n + 1], loads[n + 2])
        places, used = [], []
        for number in range(first, numbers[0] if streamed else last):
            source = max(k for k in range(len(loads) - 1) if loads[k] <= number)
            if source not in used:
                used.append(source)
            places.append((used.index(source), number - loads[source]))
        ahead = pltpu.VMEM((len(numbers), depth, block), bf16)
        out = kernel_call(
            functools.partial(base_kernel, block, places, numbers, streamed),
            "base_part",
            (15 * 10**8, 15 * 10**8, 1, 1)[n],
            1,
            12,
            in_specs=[vmem, anywhere] + [vmem] * len(used) + [anywhere] * len(after),
            out_specs=[vmem] * (1 if streamed else 2),
            out_shape=[jax.ShapeDtypeStruct((row_count, (last - first) * block), f32)]
            + ([] if streamed else [ahead]),
            scratch_shapes=([ahead] if streamed else [])
            + [pltpu.SemaphoreType.DMA((len(numbers), bands))],
        )(rows, weight, *[loaded[k] for k in used], *after)
        loaded.append(out[-1])
        return out[0]

    arrived = from_tensor(send, 1)
    base_0 = base_part(0, send)
    arrived, base_0 = lax.optimization_barrier((arrived, base_0))
    pair = keep + arrived
    arrived = from_tensor(pair[rank_block:], 2)
    base_1 = base_part(1, pair)
    arrived, base_1 = lax.optimization_barrier((arrived, base_1))
    shrunk = (adapter_scale * (pair[:rank_block] + arrived)).astype(bf16)
    across, _ = lax.optimization_barrier((across, shrunk))
    swapped = from_group(across)
    bases = [base_0, base_1]
    for m, n in ((2, 2), (1, 3)):
        arrived = from_owner(shrunk, m, m)
        base = base_part(n, shrunk, across)
        arrived, base = lax.optimization_barrier((arrived, base))
        bases.append(base)
        shrunk = shrunk + arrived

    middle = block_count * 5 // 14 * block
    splits = [(0, middle), (middle, columns)]
    widths = [last - first for first, last in splits]
    quarter = row_count // 4
    out = kernel_call(
        functools.partial(delta_kernel, block, splits),
        "add_delta",
        1,
        1,
        8,
        in_specs=[vmem] * (len(bases) + 6),
        out_specs=[vmem] * (2 + 2 * len(splits)),
        out_shape=[
            jax.ShapeDtypeStruct((quarter, w), f32) for w in (columns, columns, *widths, *widths)
        ],
        scratch_shapes=[
            pltpu.VMEM((row_count, rank_block * owner_count), f32),
            pltpu.VMEM((row_count, rank_block * owner_count), bf16),
        ],
    )(slot, *bases, own, shrunk, across, beside, swapped)
    own_keep, own_send = out[:2]
    arrived = [from_tensor(x, 1) for x in out[4:6]]
    arrived[1], own_send = lax.optimization_barrier((arrived[1], own_send))
    crossed = [
        from_tensor((keep + other).astype(bf16), 2) for keep, other in zip(out[2:4], arrived)
    ]
    kept = own_keep + from_tensor(own_send, 1)
    return jnp.concatenate(
        [
            (kept[:, first:last] + part.astype(f32)).astype(bf16)
            for (first, last), part in zip(splits, crossed)
        ],
        axis=1,
    )


def on_device(tokens, base_up_weight, adapter_shrink_weight, adapter_expand_weight, *index):
    pairs = lax.axis_size("groups") == 2 and lax.axis_size("tensor") == 4
    few = lax.axis_size("adapter") == 4
    columns = base_up_weight.shape[1]
    even = columns % 512 == 0 and columns >= 4096 and tokens.shape[0] % 16 == 0
    arrange = paired if pairs and few and even else general
    return arrange(
        tokens, base_up_weight, adapter_shrink_weight, adapter_expand_weight, *index
    )


def solution(mesh):
    placed = (
        P(("groups", "adapter"), "tensor"),
        P("tensor", "adapter"),
        P("adapter", "tensor", None),
        P("adapter", "tensor", None),
        P("groups", None),
        P(),
    )
    return jax.shard_map(
        on_device,
        mesh=mesh,
        in_specs=placed,
        out_specs=P(("groups", "tensor"), "adapter"),
        check_vma=False,
    )
```

```python
import functools

import jax
import jax.numpy as jnp
from jax import lax
from jax.experimental import pallas as pl
from jax.experimental.pallas import tpu as pltpu
from jax.sharding import PartitionSpec as P

adapter_scale = 0.5
lane = 128
f32 = jnp.float32
bf16 = jnp.bfloat16


def general(
    tokens,
    base_up_weight,
    adapter_shrink_weight,
    adapter_expand_weight,
    row_adapter_index,
    adapter_slot_index,
):
    owner_count = lax.axis_size("adapter")
    owner_index = lax.axis_index("adapter")
    tensor_index = lax.axis_index("tensor")
    rank_block = adapter_expand_weight.shape[1]
    columns = base_up_weight.shape[1]
    slot = jnp.take(adapter_slot_index, row_adapter_index[:, 0], axis=0)
    rows = lax.all_gather(tokens, "adapter", axis=0, tiled=True)
    expand = adapter_expand_weight[0].reshape(rank_block, owner_count, columns)
    expand = lax.all_to_all(expand, "adapter", split_axis=1, concat_axis=1, tiled=True)
    shrunk = jnp.dot(rows, adapter_shrink_weight[0], preferred_element_type=f32)
    shrunk = jnp.where((slot == owner_index)[:, None], shrunk, 0.0)
    shrunk = lax.psum(shrunk, ("adapter", "tensor"))
    shrunk = (adapter_scale * shrunk).astype(bf16)
    shrunk = lax.dynamic_slice_in_dim(shrunk, tensor_index * rank_block, rank_block, 1)
    chosen = slot[:, None] == jnp.arange(owner_count, dtype=jnp.int32)[None, :]
    spread = jnp.where(chosen[:, None, :], shrunk[:, :, None], jnp.zeros((), bf16))
    total = jnp.dot(rows, base_up_weight, preferred_element_type=f32)
    total = total + jnp.dot(
        spread.reshape(-1, rank_block * owner_count),
        expand.reshape(rank_block * owner_count, columns),
        preferred_element_type=f32,
    )
    return lax.psum_scatter(total, "tensor", scatter_dimension=0, tiled=True).astype(bf16)


vmem = pl.BlockSpec(memory_space=pltpu.VMEM)
anywhere = pl.BlockSpec(memory_space=pl.ANY)


def kernel_call(kernel, name, flops, moved, mib, **specs):
    return pl.pallas_call(
        kernel,
        cost_estimate=pl.CostEstimate(flops=flops, bytes_accessed=moved, transcendentals=0),
        compiler_params=pltpu.CompilerParams(vmem_limit_bytes=mib << 20),
        name=name,
        **specs,
    )


def cut_kernel(block, numbers, small_count, expand, weight, *refs):
    small, refs = refs[:small_count], refs[small_count:]
    across, beside, own, *loaded, held, sem, held_sem = refs
    g, a = lax.axis_index("groups"), lax.axis_index("adapter")
    columns = own.shape[1]
    firsts = (
        lax.bitwise_xor(a, 2 + g) * columns,
        lax.bitwise_xor(a, 1) * columns,
        a * columns,
    )
    copies = []
    for n, (first, target) in enumerate(zip(firsts, (across, beside, own))):
        span = pl.ds(pl.multiple_of(first, lane), columns)
        copies.append(pltpu.make_async_copy(expand.at[0, :, span], target, sem.at[n]))
    for n, (source, target) in enumerate(zip(small, loaded)):
        copies.append(pltpu.make_async_copy(source, target, sem.at[len(firsts) + n]))
    copies += weight_copies(block, numbers, weight, held, held_sem)
    for copy in copies:
        copy.start()
    for copy in copies:
        copy.wait()


def weight_copies(block, numbers, weight, target, sem):
    band_count = sem.shape[1]
    band = weight.shape[0] // band_count
    copies = []
    for n, number in enumerate(numbers):
        span = pl.ds(number * block, block)
        for m in range(band_count):
            rows = pl.ds(m * band, band)
            copies.append(
                pltpu.make_async_copy(weight.at[rows, span], target.at[n, rows], sem.at[n, m])
            )
    return copies


def gather_kernel(offsets, slots, index, *refs):
    owner_count = len(offsets)
    blocks = refs[:owner_count]
    shrink, rows_out, keep, send, slot_out, rows, partial = refs[owner_count:]
    a, t = lax.axis_index("adapter"), lax.axis_index("tensor")
    height, depth = blocks[0].shape
    for j, part in zip(offsets, blocks):
        where = lax.bitwise_xor(a, j)
        rows[pl.ds(pl.multiple_of(where * height, height), height), :] = part[:, :depth]
    quarter = rows.shape[0] // 4
    for i, flip in enumerate((0, 2, 1, 3)):
        start = pl.multiple_of(lax.bitwise_xor(t, flip) * quarter, quarter)
        rows_out[i * quarter : (i + 1) * quarter, :] = rows[pl.ds(start, quarter), :]
    product = lax.dot_general(
        shrink[...], rows[...], (((1,), (1,)), ((), ())), preferred_element_type=f32
    )
    named, table = index[...], slots[...]
    slot = jnp.zeros_like(named)
    for k in range(table.shape[1]):
        slot = jnp.where(named == k, table[:, k : k + 1], slot)
    slot_out[...] = slot
    partial[...] = jnp.where(slot == a, product, 0.0)
    rank_block = partial.shape[0] // 4
    for i, flip in enumerate((0, 2, 1, 3)):
        start = pl.multiple_of(lax.bitwise_xor(t, flip) * rank_block, rank_block)
        target = keep if i < 2 else send
        at = i % 2 * rank_block
        target[at : at + rank_block, :] = partial[pl.ds(start, rank_block), :]


def base_kernel(block, places, numbers, streamed, rows, weight, *refs):
    total, ahead, sem = refs[-3:]
    copies = weight_copies(block, numbers, weight, ahead, sem)
    for copy in copies:
        copy.start()

    @pl.when(lax.axis_index("tensor") >= 0)
    def _():
        for n, (which, index) in enumerate(places):
            total[:, n * block : (n + 1) * block] = jnp.dot(
                rows[...], refs[which][index], preferred_element_type=f32
            )

    bands = sem.shape[1]
    for n in range(len(numbers)):
        for copy in copies[n * bands : (n + 1) * bands]:
            copy.wait()
        if streamed:
            at = (len(places) + n) * block
            total[:, at : at + block] = jnp.dot(
                rows[...], ahead[n], preferred_element_type=f32
            )


def delta_kernel(block, splits, slot, *refs):
    bases, refs = refs[: -len(splits) * 2 - 9], refs[-len(splits) * 2 - 9 :]
    own, shrunk, across, beside, swapped, own_keep, own_send = refs[:7]
    cross_keep, cross_send = refs[7 : 7 + len(splits)], refs[7 + len(splits) : 7 + 2 * len(splits)]
    flat, ordered = refs[-2:]
    g, a, t = (lax.axis_index(name) for name in ("groups", "adapter", "tensor"))
    row_count = bases[0].shape[0]
    quarter = row_count // 4
    merged = shrunk[...].astype(f32)
    spread = [
        jnp.where(slot[...] == lax.bitwise_xor(a, j), merged, 0.0)
        for j in (0, 2 + g, 1, 3 - g)
    ]
    flat[...] = jnp.concatenate(spread, axis=0).T
    for i, turn in enumerate((0, 2, 1, 3)):
        start = pl.multiple_of(lax.bitwise_xor(t, turn) * quarter, quarter)
        ordered[i * quarter : (i + 1) * quarter, :] = flat[pl.ds(start, quarter), :].astype(bf16)
    left = ordered[...]
    at, split = 0, 0
    for base in bases:
        for column in range(0, base.shape[1], block):
            span = slice(at, at + block)
            expand = jnp.concatenate(
                [own[:, span], across[:, span], beside[:, span], swapped[:, span]], axis=0
            )
            total = base[:, column : column + block] + jnp.dot(
                left, expand, preferred_element_type=f32
            )
            if at >= splits[split][1]:
                split += 1
            here = slice(at - splits[split][0], at - splits[split][0] + block)
            own_keep[:, span] = total[:quarter]
            cross_keep[split][:, here] = total[quarter : 2 * quarter]
            own_send[:, span] = total[2 * quarter : 3 * quarter]
            cross_send[split][:, here] = total[3 * quarter :]
            at += block


def column_block(width):
    for size in (512, 256, 128):
        if width % size == 0:
            return size


def paired(
    tokens,
    base_up_weight,
    adapter_shrink_weight,
    adapter_expand_weight,
    row_adapter_index,
    adapter_slot_index,
):
    owner_count = lax.axis_size("adapter")
    g = lax.axis_index("groups")
    height, depth = tokens.shape
    row_count = height * owner_count
    columns = base_up_weight.shape[1]
    rank_block = adapter_expand_weight.shape[1]
    rank = adapter_shrink_weight.shape[2]
    block = column_block(columns)
    block_count = columns // block

    def from_owner(x, first, second):
        pairs = []
        for group, m in ((0, first), (1, second)):
            for s in range(owner_count):
                pairs.append((group * owner_count + s, group * owner_count + (s ^ m)))
        return lax.ppermute(x, ("groups", "adapter"), pairs)

    def from_tensor(x, m):
        return lax.ppermute(x, "tensor", [(s, s ^ m) for s in range(4)])

    def from_group(x):
        return lax.ppermute(x, "groups", [(0, 1), (1, 0)])

    weight = pltpu.with_memory_space_constraint(base_up_weight, pltpu.HBM)
    expand = pltpu.with_memory_space_constraint(adapter_expand_weight, pltpu.HBM)
    offsets = (2, 3, 1)
    blocks = [from_owner(tokens, j, j) for j in offsets]

    cuts = [block_count * k // 14 for k in (0, 4, 8, 11, 14)]
    parts = list(zip(cuts[:-1], cuts[1:]))
    loads = [block_count * k // 14 for k in (0, 4, 8, 11, 13, 14)]
    bands = 4
    small = [
        pltpu.with_memory_space_constraint(x, pltpu.HBM)
        for x in (
            adapter_slot_index.reshape(1, owner_count),
            row_adapter_index.reshape(1, row_count),
            tokens,
            adapter_shrink_weight[0].T,
        )
    ]
    across, beside, own, slots, index, mine, shrink, held = kernel_call(
        functools.partial(cut_kernel, block, range(loads[1]), len(small)),
        "cut_expand",
        1,
        1,
        1,
        in_specs=[anywhere] * (2 + len(small)),
        out_specs=[vmem] * (4 + len(small)),
        out_shape=[pltpu.VMEM((rank_block, w), bf16) for w in (columns,) * 3]
        + [pltpu.VMEM(x.shape, x.dtype) for x in small]
        + [pltpu.VMEM((loads[1], depth, block), bf16)],
        scratch_shapes=[
            pltpu.SemaphoreType.DMA((3 + len(small),)),
            pltpu.SemaphoreType.DMA((loads[1], bands)),
        ],
    )(expand, weight, *small)
    loaded = [held]
    across, blocks[0] = lax.optimization_barrier((across, blocks[0]))
    beside = from_owner(beside, 1, 1)
    across = from_owner(across, 2, 3)

    rows, keep, send, slot = kernel_call(
        functools.partial(gather_kernel, (0, *offsets)),
        "gather_rows",
        1,
        1,
        4,
        in_specs=[vmem] * (owner_count + 3),
        out_specs=[vmem] * 4,
        out_shape=[jax.ShapeDtypeStruct((row_count, depth), bf16)]
        + [jax.ShapeDtypeStruct((rank // 2, row_count), f32)] * 2
        + [jax.ShapeDtypeStruct((1, row_count), jnp.int32)],
        scratch_shapes=[pltpu.VMEM((row_count, depth), bf16), pltpu.VMEM((rank, row_count), f32)],
    )(
        slots,
        index,
        mine,
        *blocks,
        shrink,
    )

    def base_part(n, *after):
        first, last = parts[n]
        streamed = n + 1 == len(parts)
        numbers = range(loads[n + 1], loads[n + 2])
        places, used = [], []
        for number in range(first, numbers[0] if streamed else last):
            source = max(k for k in range(len(loads) - 1) if loads[k] <= number)
            if source not in used:
                used.append(source)
            places.append((used.index(source), number - loads[source]))
        ahead = pltpu.VMEM((len(numbers), depth, block), bf16)
        out = kernel_call(
            functools.partial(base_kernel, block, places, numbers, streamed),
            "base_part",
            (10**9, 1, 10**10, 1)[n],
            1,
            12,
            in_specs=[vmem, anywhere] + [vmem] * len(used) + [anywhere] * len(after),
            out_specs=[vmem] * (1 if streamed else 2),
            out_shape=[jax.ShapeDtypeStruct((row_count, (last - first) * block), f32)]
            + ([] if streamed else [ahead]),
            scratch_shapes=([ahead] if streamed else [])
            + [pltpu.SemaphoreType.DMA((len(numbers), bands))],
        )(rows, weight, *[loaded[k] for k in used], *after)
        loaded.append(out[-1])
        return out[0]

    arrived = from_tensor(send, 1)
    base_0 = base_part(0, send)
    arrived, base_0 = lax.optimization_barrier((arrived, base_0))
    pair = keep + arrived
    arrived = from_tensor(pair[rank_block:], 2)
    base_1 = base_part(1, pair)
    arrived, base_1 = lax.optimization_barrier((arrived, base_1))
    shrunk = (adapter_scale * (pair[:rank_block] + arrived)).astype(bf16)
    across, _ = lax.optimization_barrier((across, shrunk))
    swapped = from_group(across)
    bases = [base_0, base_1]
    for m, n in ((2, 2), (1, 3)):
        arrived = from_owner(shrunk, m, m)
        base = base_part(n, shrunk, across)
        arrived, base = lax.optimization_barrier((arrived, base))
        bases.append(base)
        shrunk = shrunk + arrived

    middle = block_count * 5 // 14 * block
    splits = [(0, middle), (middle, columns)]
    widths = [last - first for first, last in splits]
    quarter = row_count // 4
    out = kernel_call(
        functools.partial(delta_kernel, block, splits),
        "add_delta",
        1,
        1,
        8,
        in_specs=[vmem] * (len(bases) + 6),
        out_specs=[vmem] * (2 + 2 * len(splits)),
        out_shape=[
            jax.ShapeDtypeStruct((quarter, w), f32) for w in (columns, columns, *widths, *widths)
        ],
        scratch_shapes=[
            pltpu.VMEM((row_count, rank_block * owner_count), f32),
            pltpu.VMEM((row_count, rank_block * owner_count), bf16),
        ],
    )(slot, *bases, own, shrunk, across, beside, swapped)
    own_keep, own_send = out[:2]
    arrived = [from_tensor(x, 1) for x in out[4:6]]
    arrived[1], own_send = lax.optimization_barrier((arrived[1], own_send))
    crossed = [
        from_tensor((keep + other).astype(bf16), 2) for keep, other in zip(out[2:4], arrived)
    ]
    kept = own_keep + from_tensor(own_send, 1)
    return jnp.concatenate(
        [
            (kept[:, first:last] + part.astype(f32)).astype(bf16)
            for (first, last), part in zip(splits, crossed)
        ],
        axis=1,
    )


def on_device(tokens, base_up_weight, adapter_shrink_weight, adapter_expand_weight, *index):
    pairs = lax.axis_size("groups") == 2 and lax.axis_size("tensor") == 4
    few = lax.axis_size("adapter") == 4
    columns = base_up_weight.shape[1]
    even = columns % 512 == 0 and columns >= 4096 and tokens.shape[0] % 16 == 0
    arrange = paired if pairs and few and even else general
    return arrange(
        tokens, base_up_weight, adapter_shrink_weight, adapter_expand_weight, *index
    )


def solution(mesh):
    placed = (
        P(("groups", "adapter"), "tensor"),
        P("tensor", "adapter"),
        P("adapter", "tensor", None),
        P("adapter", "tensor", None),
        P("groups", None),
        P(),
    )
    return jax.shard_map(
        on_device,
        mesh=mesh,
        in_specs=placed,
        out_specs=P(("groups", "tensor"), "adapter"),
        check_vma=False,
    )
```

```python
import functools

import jax
import jax.numpy as jnp
from jax import lax
from jax.experimental import pallas as pl
from jax.experimental.pallas import tpu as pltpu
from jax.sharding import PartitionSpec as P

adapter_scale = 0.5
lane = 128
f32 = jnp.float32
bf16 = jnp.bfloat16


def general(
    tokens,
    base_up_weight,
    adapter_shrink_weight,
    adapter_expand_weight,
    row_adapter_index,
    adapter_slot_index,
):
    owner_count = lax.axis_size("adapter")
    owner_index = lax.axis_index("adapter")
    tensor_index = lax.axis_index("tensor")
    rank_block = adapter_expand_weight.shape[1]
    columns = base_up_weight.shape[1]
    slot = jnp.take(adapter_slot_index, row_adapter_index[:, 0], axis=0)
    rows = lax.all_gather(tokens, "adapter", axis=0, tiled=True)
    expand = adapter_expand_weight[0].reshape(rank_block, owner_count, columns)
    expand = lax.all_to_all(expand, "adapter", split_axis=1, concat_axis=1, tiled=True)
    shrunk = jnp.dot(rows, adapter_shrink_weight[0], preferred_element_type=f32)
    shrunk = jnp.where((slot == owner_index)[:, None], shrunk, 0.0)
    shrunk = lax.psum(shrunk, ("adapter", "tensor"))
    shrunk = (adapter_scale * shrunk).astype(bf16)
    shrunk = lax.dynamic_slice_in_dim(shrunk, tensor_index * rank_block, rank_block, 1)
    chosen = slot[:, None] == jnp.arange(owner_count, dtype=jnp.int32)[None, :]
    spread = jnp.where(chosen[:, None, :], shrunk[:, :, None], jnp.zeros((), bf16))
    total = jnp.dot(rows, base_up_weight, preferred_element_type=f32)
    total = total + jnp.dot(
        spread.reshape(-1, rank_block * owner_count),
        expand.reshape(rank_block * owner_count, columns),
        preferred_element_type=f32,
    )
    return lax.psum_scatter(total, "tensor", scatter_dimension=0, tiled=True).astype(bf16)


vmem = pl.BlockSpec(memory_space=pltpu.VMEM)
anywhere = pl.BlockSpec(memory_space=pl.ANY)


def kernel_call(kernel, name, flops, moved, mib, **specs):
    return pl.pallas_call(
        kernel,
        cost_estimate=pl.CostEstimate(flops=flops, bytes_accessed=moved, transcendentals=0),
        compiler_params=pltpu.CompilerParams(vmem_limit_bytes=mib << 20),
        name=name,
        **specs,
    )


def cut_kernel(block, numbers, small_count, expand, weight, *refs):
    small, refs = refs[:small_count], refs[small_count:]
    across, beside, own, *loaded, held, sem, held_sem = refs
    g, a = lax.axis_index("groups"), lax.axis_index("adapter")
    columns = own.shape[1]
    firsts = (
        lax.bitwise_xor(a, 2 + g) * columns,
        lax.bitwise_xor(a, 1) * columns,
        a * columns,
    )
    copies = []
    for n, (first, target) in enumerate(zip(firsts, (across, beside, own))):
        span = pl.ds(pl.multiple_of(first, lane), columns)
        copies.append(pltpu.make_async_copy(expand.at[0, :, span], target, sem.at[n]))
    for n, (source, target) in enumerate(zip(small, loaded)):
        copies.append(pltpu.make_async_copy(source, target, sem.at[len(firsts) + n]))
    copies += weight_copies(block, numbers, weight, held, held_sem)
    for copy in copies:
        copy.start()
    for copy in copies:
        copy.wait()


def weight_copies(block, numbers, weight, target, sem):
    band_count = sem.shape[1]
    band = weight.shape[0] // band_count
    copies = []
    for n, number in enumerate(numbers):
        span = pl.ds(number * block, block)
        for m in range(band_count):
            rows = pl.ds(m * band, band)
            copies.append(
                pltpu.make_async_copy(weight.at[rows, span], target.at[n, rows], sem.at[n, m])
            )
    return copies


def gather_kernel(offsets, slots, index, *refs):
    owner_count = len(offsets)
    blocks = refs[:owner_count]
    shrink, rows_out, keep, send, slot_out, rows, partial = refs[owner_count:]
    a, t = lax.axis_index("adapter"), lax.axis_index("tensor")
    height, depth = blocks[0].shape
    for j, part in zip(offsets, blocks):
        where = lax.bitwise_xor(a, j)
        rows[pl.ds(pl.multiple_of(where * height, height), height), :] = part[:, :depth]
    quarter = rows.shape[0] // 4
    for i, flip in enumerate((0, 2, 1, 3)):
        start = pl.multiple_of(lax.bitwise_xor(t, flip) * quarter, quarter)
        rows_out[i * quarter : (i + 1) * quarter, :] = rows[pl.ds(start, quarter), :]
    product = lax.dot_general(
        shrink[...], rows[...], (((1,), (1,)), ((), ())), preferred_element_type=f32
    )
    named, table = index[...], slots[...]
    slot = jnp.zeros_like(named)
    for k in range(table.shape[1]):
        slot = jnp.where(named == k, table[:, k : k + 1], slot)
    slot_out[...] = slot
    partial[...] = jnp.where(slot == a, product, 0.0)
    rank_block = partial.shape[0] // 4
    for i, flip in enumerate((0, 2, 1, 3)):
        start = pl.multiple_of(lax.bitwise_xor(t, flip) * rank_block, rank_block)
        target = keep if i < 2 else send
        at = i % 2 * rank_block
        target[at : at + rank_block, :] = partial[pl.ds(start, rank_block), :]


def base_kernel(block, places, numbers, streamed, rows, weight, *refs):
    total, ahead, sem = refs[-3:]
    copies = weight_copies(block, numbers, weight, ahead, sem)
    for copy in copies:
        copy.start()

    @pl.when(lax.axis_index("tensor") >= 0)
    def _():
        for n, (which, index) in enumerate(places):
            total[:, n * block : (n + 1) * block] = jnp.dot(
                rows[...], refs[which][index], preferred_element_type=f32
            )

    bands = sem.shape[1]
    for n in range(len(numbers)):
        for copy in copies[n * bands : (n + 1) * bands]:
            copy.wait()
        if streamed:
            at = (len(places) + n) * block
            total[:, at : at + block] = jnp.dot(
                rows[...], ahead[n], preferred_element_type=f32
            )


def delta_kernel(block, begin, end, slot, *refs):
    bases, refs = refs[:-11], refs[-11:]
    own, shrunk, across, beside, swapped = refs[:5]
    outs, (flat, ordered) = refs[5:9], refs[9:]
    g, a, t = (lax.axis_index(name) for name in ("groups", "adapter", "tensor"))
    row_count = bases[0].shape[0]
    quarter = row_count // 4
    merged = shrunk[...].astype(f32)
    spread = [
        jnp.where(slot[...] == lax.bitwise_xor(a, j), merged, 0.0)
        for j in (0, 2 + g, 1, 3 - g)
    ]
    flat[...] = jnp.concatenate(spread, axis=0).T
    for i, turn in enumerate((0, 2, 1, 3)):
        start = pl.multiple_of(lax.bitwise_xor(t, turn) * quarter, quarter)
        ordered[i * quarter : (i + 1) * quarter, :] = flat[pl.ds(start, quarter), :].astype(bf16)
    left = ordered[...]
    at = 0
    for base in bases:
        for column in range(0, base.shape[1], block):
            span, here = slice(at, at + block), slice(at - begin, at - begin + block)
            at += block
            if not begin < at <= end:
                continue
            expand = jnp.concatenate(
                [own[:, span], across[:, span], beside[:, span], swapped[:, span]], axis=0
            )
            total = base[:, column : column + block] + jnp.dot(
                left, expand, preferred_element_type=f32
            )
            for n, out in enumerate(outs):
                out[:, here] = total[n * quarter : (n + 1) * quarter]


def column_block(width):
    for size in (512, 256, 128):
        if width % size == 0:
            return size


def paired(
    tokens,
    base_up_weight,
    adapter_shrink_weight,
    adapter_expand_weight,
    row_adapter_index,
    adapter_slot_index,
):
    owner_count = lax.axis_size("adapter")
    g = lax.axis_index("groups")
    height, depth = tokens.shape
    row_count = height * owner_count
    columns = base_up_weight.shape[1]
    rank_block = adapter_expand_weight.shape[1]
    rank = adapter_shrink_weight.shape[2]
    block = column_block(columns)
    block_count = columns // block

    def from_owner(x, first, second):
        pairs = []
        for group, m in ((0, first), (1, second)):
            for s in range(owner_count):
                pairs.append((group * owner_count + s, group * owner_count + (s ^ m)))
        return lax.ppermute(x, ("groups", "adapter"), pairs)

    def from_tensor(x, m):
        return lax.ppermute(x, "tensor", [(s, s ^ m) for s in range(4)])

    def from_group(x):
        return lax.ppermute(x, "groups", [(0, 1), (1, 0)])

    weight = pltpu.with_memory_space_constraint(base_up_weight, pltpu.HBM)
    expand = pltpu.with_memory_space_constraint(adapter_expand_weight, pltpu.HBM)
    offsets = (2, 3, 1)
    blocks = [from_owner(tokens, j, j) for j in offsets]

    cuts = [block_count * k // 14 for k in (0, 4, 8, 11, 14)]
    parts = list(zip(cuts[:-1], cuts[1:]))
    loads = [block_count * k // 14 for k in (0, 4, 8, 11, 13, 14)]
    bands = 4
    small = [
        pltpu.with_memory_space_constraint(x, pltpu.HBM)
        for x in (
            adapter_slot_index.reshape(1, owner_count),
            row_adapter_index.reshape(1, row_count),
            tokens,
            adapter_shrink_weight[0].T,
        )
    ]
    across, beside, own, slots, index, mine, shrink, held = kernel_call(
        functools.partial(cut_kernel, block, range(loads[1]), len(small)),
        "cut_expand",
        1,
        1,
        1,
        in_specs=[anywhere] * (2 + len(small)),
        out_specs=[vmem] * (4 + len(small)),
        out_shape=[pltpu.VMEM((rank_block, w), bf16) for w in (columns,) * 3]
        + [pltpu.VMEM(x.shape, x.dtype) for x in small]
        + [pltpu.VMEM((loads[1], depth, block), bf16)],
        scratch_shapes=[
            pltpu.SemaphoreType.DMA((3 + len(small),)),
            pltpu.SemaphoreType.DMA((loads[1], bands)),
        ],
    )(expand, weight, *small)
    loaded = [held]
    across, beside = from_owner(across, 2, 3), from_owner(beside, 1, 1)

    rows, keep, send, slot = kernel_call(
        functools.partial(gather_kernel, (0, *offsets)),
        "gather_rows",
        1,
        1,
        4,
        in_specs=[vmem] * (owner_count + 3),
        out_specs=[vmem] * 4,
        out_shape=[jax.ShapeDtypeStruct((row_count, depth), bf16)]
        + [jax.ShapeDtypeStruct((rank // 2, row_count), f32)] * 2
        + [jax.ShapeDtypeStruct((1, row_count), jnp.int32)],
        scratch_shapes=[pltpu.VMEM((row_count, depth), bf16), pltpu.VMEM((rank, row_count), f32)],
    )(
        slots,
        index,
        mine,
        *blocks,
        shrink,
    )

    def base_part(n, *after):
        first, last = parts[n]
        streamed = n + 1 == len(parts)
        numbers = range(loads[n + 1], loads[n + 2])
        places, used = [], []
        for number in range(first, numbers[0] if streamed else last):
            source = max(k for k in range(len(loads) - 1) if loads[k] <= number)
            if source not in used:
                used.append(source)
            places.append((used.index(source), number - loads[source]))
        ahead = pltpu.VMEM((len(numbers), depth, block), bf16)
        out = kernel_call(
            functools.partial(base_kernel, block, places, numbers, streamed),
            "base_part",
            (15 * 10**8, 15 * 10**8, 10**10, 1)[n],
            1,
            12,
            in_specs=[vmem, anywhere] + [vmem] * len(used) + [anywhere] * len(after),
            out_specs=[vmem] * (1 if streamed else 2),
            out_shape=[jax.ShapeDtypeStruct((row_count, (last - first) * block), f32)]
            + ([] if streamed else [ahead]),
            scratch_shapes=([ahead] if streamed else [])
            + [pltpu.SemaphoreType.DMA((len(numbers), bands))],
        )(rows, weight, *[loaded[k] for k in used], *after)
        loaded.append(out[-1])
        return out[0]

    arrived = from_tensor(send, 1)
    base_0 = base_part(0, send)
    arrived, base_0 = lax.optimization_barrier((arrived, base_0))
    pair = keep + arrived
    arrived = from_tensor(pair[rank_block:], 2)
    base_1 = base_part(1, pair)
    arrived, base_1 = lax.optimization_barrier((arrived, base_1))
    shrunk = (adapter_scale * (pair[:rank_block] + arrived)).astype(bf16)
    across, _ = lax.optimization_barrier((across, shrunk))
    swapped = from_group(across)
    bases = [base_0, base_1]
    for m, n in ((2, 2), (1, 3)):
        arrived = from_owner(shrunk, m, m)
        base = base_part(n, shrunk, across)
        arrived, base = lax.optimization_barrier((arrived, base))
        bases.append(base)
        shrunk = shrunk + arrived

    middle = block_count * 5 // 14 * block
    splits = [(0, middle), (middle, columns)]
    quarter = row_count // 4

    def delta_part(begin, end):
        return kernel_call(
            functools.partial(delta_kernel, block, begin, end),
            "add_delta",
            1,
            1,
            8,
            in_specs=[vmem] * (len(bases) + 6),
            out_specs=[vmem] * 4,
            out_shape=[jax.ShapeDtypeStruct((quarter, end - begin), f32)] * 4,
            scratch_shapes=[
                pltpu.VMEM((row_count, rank_block * owner_count), f32),
                pltpu.VMEM((row_count, rank_block * owner_count), bf16),
            ],
        )(slot, *bases, own, shrunk, across, beside, swapped)

    first, second = delta_part(*splits[0]), delta_part(*splits[1])
    arrived = [from_tensor(first[3], 1), from_tensor(second[3], 1)]
    arrived[0], *rest = lax.optimization_barrier((arrived[0], *second[:3]))
    second = [*rest, second[3]]
    arrived[1], sent_a, sent_b = lax.optimization_barrier((arrived[1], first[2], second[2]))
    halves = []
    for part, other, sent in ((first, arrived[0], sent_a), (second, arrived[1], sent_b)):
        crossed = from_tensor((part[1] + other).astype(bf16), 2)
        kept = part[0] + from_tensor(sent, 1)
        halves.append((kept + crossed.astype(f32)).astype(bf16))
    return jnp.concatenate(halves, axis=1)


def on_device(tokens, base_up_weight, adapter_shrink_weight, adapter_expand_weight, *index):
    pairs = lax.axis_size("groups") == 2 and lax.axis_size("tensor") == 4
    few = lax.axis_size("adapter") == 4
    columns = base_up_weight.shape[1]
    even = columns % 512 == 0 and columns >= 4096 and tokens.shape[0] % 16 == 0
    arrange = paired if pairs and few and even else general
    return arrange(
        tokens, base_up_weight, adapter_shrink_weight, adapter_expand_weight, *index
    )


def solution(mesh):
    placed = (
        P(("groups", "adapter"), "tensor"),
        P("tensor", "adapter"),
        P("adapter", "tensor", None),
        P("adapter", "tensor", None),
        P("groups", None),
        P(),
    )
    return jax.shard_map(
        on_device,
        mesh=mesh,
        in_specs=placed,
        out_specs=P(("groups", "tensor"), "adapter"),
        check_vma=False,
    )
```

```python
import functools

import jax
import jax.numpy as jnp
from jax import lax
from jax.experimental import pallas as pl
from jax.experimental.pallas import tpu as pltpu
from jax.sharding import PartitionSpec as P

adapter_scale = 0.5
lane = 128
f32 = jnp.float32
bf16 = jnp.bfloat16


def general(
    tokens,
    base_up_weight,
    adapter_shrink_weight,
    adapter_expand_weight,
    row_adapter_index,
    adapter_slot_index,
):
    owner_count = lax.axis_size("adapter")
    owner_index = lax.axis_index("adapter")
    tensor_index = lax.axis_index("tensor")
    rank_block = adapter_expand_weight.shape[1]
    columns = base_up_weight.shape[1]
    slot = jnp.take(adapter_slot_index, row_adapter_index[:, 0], axis=0)
    rows = lax.all_gather(tokens, "adapter", axis=0, tiled=True)
    expand = adapter_expand_weight[0].reshape(rank_block, owner_count, columns)
    expand = lax.all_to_all(expand, "adapter", split_axis=1, concat_axis=1, tiled=True)
    shrunk = jnp.dot(rows, adapter_shrink_weight[0], preferred_element_type=f32)
    shrunk = jnp.where((slot == owner_index)[:, None], shrunk, 0.0)
    shrunk = lax.psum(shrunk, ("adapter", "tensor"))
    shrunk = (adapter_scale * shrunk).astype(bf16)
    shrunk = lax.dynamic_slice_in_dim(shrunk, tensor_index * rank_block, rank_block, 1)
    chosen = slot[:, None] == jnp.arange(owner_count, dtype=jnp.int32)[None, :]
    spread = jnp.where(chosen[:, None, :], shrunk[:, :, None], jnp.zeros((), bf16))
    total = jnp.dot(rows, base_up_weight, preferred_element_type=f32)
    total = total + jnp.dot(
        spread.reshape(-1, rank_block * owner_count),
        expand.reshape(rank_block * owner_count, columns),
        preferred_element_type=f32,
    )
    return lax.psum_scatter(total, "tensor", scatter_dimension=0, tiled=True).astype(bf16)


vmem = pl.BlockSpec(memory_space=pltpu.VMEM)
anywhere = pl.BlockSpec(memory_space=pl.ANY)


def kernel_call(kernel, name, flops, moved, mib, **specs):
    return pl.pallas_call(
        kernel,
        cost_estimate=pl.CostEstimate(flops=flops, bytes_accessed=moved, transcendentals=0),
        compiler_params=pltpu.CompilerParams(vmem_limit_bytes=mib << 20),
        name=name,
        **specs,
    )


def cut_kernel(block, numbers, small_count, expand, weight, *refs):
    small, refs = refs[:small_count], refs[small_count:]
    across, beside, own, *loaded, held, sem, held_sem = refs
    g, a = lax.axis_index("groups"), lax.axis_index("adapter")
    columns = own.shape[1]
    firsts = (
        lax.bitwise_xor(a, 2 + g) * columns,
        lax.bitwise_xor(a, 1) * columns,
        a * columns,
    )
    copies = []
    for n, (first, target) in enumerate(zip(firsts, (across, beside, own))):
        span = pl.ds(pl.multiple_of(first, lane), columns)
        copies.append(pltpu.make_async_copy(expand.at[0, :, span], target, sem.at[n]))
    for n, (source, target) in enumerate(zip(small, loaded)):
        copies.append(pltpu.make_async_copy(source, target, sem.at[len(firsts) + n]))
    copies += weight_copies(block, numbers, weight, held, held_sem)
    for copy in copies:
        copy.start()
    for copy in copies:
        copy.wait()


def weight_copies(block, numbers, weight, target, sem):
    band_count = sem.shape[1]
    band = weight.shape[0] // band_count
    copies = []
    for n, number in enumerate(numbers):
        span = pl.ds(number * block, block)
        for m in range(band_count):
            rows = pl.ds(m * band, band)
            copies.append(
                pltpu.make_async_copy(weight.at[rows, span], target.at[n, rows], sem.at[n, m])
            )
    return copies


def gather_kernel(offsets, slots, index, *refs):
    owner_count = len(offsets)
    blocks = refs[:owner_count]
    shrink, rows_out, keep, send, slot_out, rows, partial = refs[owner_count:]
    a, t = lax.axis_index("adapter"), lax.axis_index("tensor")
    height, depth = blocks[0].shape
    for j, part in zip(offsets, blocks):
        where = lax.bitwise_xor(a, j)
        rows[pl.ds(pl.multiple_of(where * height, height), height), :] = part[:, :depth]
    quarter = rows.shape[0] // 4
    for i, flip in enumerate((0, 2, 1, 3)):
        start = pl.multiple_of(lax.bitwise_xor(t, flip) * quarter, quarter)
        rows_out[i * quarter : (i + 1) * quarter, :] = rows[pl.ds(start, quarter), :]
    product = lax.dot_general(
        shrink[...], rows[...], (((1,), (1,)), ((), ())), preferred_element_type=f32
    )
    named, table = index[...], slots[...]
    slot = jnp.zeros_like(named)
    for k in range(table.shape[1]):
        slot = jnp.where(named == k, table[:, k : k + 1], slot)
    slot_out[...] = slot
    partial[...] = jnp.where(slot == a, product, 0.0)
    rank_block = partial.shape[0] // 4
    for i, flip in enumerate((0, 2, 1, 3)):
        start = pl.multiple_of(lax.bitwise_xor(t, flip) * rank_block, rank_block)
        target = keep if i < 2 else send
        at = i % 2 * rank_block
        target[at : at + rank_block, :] = partial[pl.ds(start, rank_block), :]


def base_kernel(block, places, numbers, streamed, rows, weight, *refs):
    total, ahead, sem = refs[-3:]
    copies = weight_copies(block, numbers, weight, ahead, sem)
    for copy in copies:
        copy.start()

    @pl.when(lax.axis_index("tensor") >= 0)
    def _():
        for n, (which, index) in enumerate(places):
            total[:, n * block : (n + 1) * block] = jnp.dot(
                rows[...], refs[which][index], preferred_element_type=f32
            )

    bands = sem.shape[1]
    for n in range(len(numbers)):
        for copy in copies[n * bands : (n + 1) * bands]:
            copy.wait()
        if streamed:
            at = (len(places) + n) * block
            total[:, at : at + block] = jnp.dot(
                rows[...], ahead[n], preferred_element_type=f32
            )


def delta_kernel(block, begin, end, slot, *refs):
    bases, refs = refs[:-11], refs[-11:]
    own, shrunk, across, beside, swapped = refs[:5]
    outs, (flat, ordered) = refs[5:9], refs[9:]
    g, a, t = (lax.axis_index(name) for name in ("groups", "adapter", "tensor"))
    row_count = bases[0].shape[0]
    quarter = row_count // 4
    merged = shrunk[...].astype(f32)
    spread = [
        jnp.where(slot[...] == lax.bitwise_xor(a, j), merged, 0.0)
        for j in (0, 2 + g, 1, 3 - g)
    ]
    flat[...] = jnp.concatenate(spread, axis=0).T
    for i, turn in enumerate((0, 2, 1, 3)):
        start = pl.multiple_of(lax.bitwise_xor(t, turn) * quarter, quarter)
        ordered[i * quarter : (i + 1) * quarter, :] = flat[pl.ds(start, quarter), :].astype(bf16)
    left = ordered[...]
    at = 0
    for base in bases:
        for column in range(0, base.shape[1], block):
            span, here = slice(at, at + block), slice(at - begin, at - begin + block)
            at += block
            if not begin < at <= end:
                continue
            expand = jnp.concatenate(
                [own[:, span], across[:, span], beside[:, span], swapped[:, span]], axis=0
            )
            total = base[:, column : column + block] + jnp.dot(
                left, expand, preferred_element_type=f32
            )
            for n, out in enumerate(outs):
                out[:, here] = total[n * quarter : (n + 1) * quarter]


def column_block(width):
    for size in (512, 256, 128):
        if width % size == 0:
            return size


def paired(
    tokens,
    base_up_weight,
    adapter_shrink_weight,
    adapter_expand_weight,
    row_adapter_index,
    adapter_slot_index,
):
    owner_count = lax.axis_size("adapter")
    g = lax.axis_index("groups")
    height, depth = tokens.shape
    row_count = height * owner_count
    columns = base_up_weight.shape[1]
    rank_block = adapter_expand_weight.shape[1]
    rank = adapter_shrink_weight.shape[2]
    block = column_block(columns)
    block_count = columns // block

    def from_owner(x, first, second):
        pairs = []
        for group, m in ((0, first), (1, second)):
            for s in range(owner_count):
                pairs.append((group * owner_count + s, group * owner_count + (s ^ m)))
        return lax.ppermute(x, ("groups", "adapter"), pairs)

    def from_tensor(x, m):
        return lax.ppermute(x, "tensor", [(s, s ^ m) for s in range(4)])

    def from_group(x):
        return lax.ppermute(x, "groups", [(0, 1), (1, 0)])

    weight = pltpu.with_memory_space_constraint(base_up_weight, pltpu.HBM)
    expand = pltpu.with_memory_space_constraint(adapter_expand_weight, pltpu.HBM)
    offsets = (2, 3, 1)
    blocks = [from_owner(tokens, j, j) for j in offsets]

    cuts = [block_count * k // 14 for k in (0, 4, 8, 11, 14)]
    parts = list(zip(cuts[:-1], cuts[1:]))
    loads = [block_count * k // 14 for k in (0, 4, 8, 11, 13, 14)]
    bands = 4
    small = [
        pltpu.with_memory_space_constraint(x, pltpu.HBM)
        for x in (
            adapter_slot_index.reshape(1, owner_count),
            row_adapter_index.reshape(1, row_count),
            tokens,
            adapter_shrink_weight[0].T,
        )
    ]
    across, beside, own, slots, index, mine, shrink, held = kernel_call(
        functools.partial(cut_kernel, block, range(loads[1]), len(small)),
        "cut_expand",
        1,
        1,
        1,
        in_specs=[anywhere] * (2 + len(small)),
        out_specs=[vmem] * (4 + len(small)),
        out_shape=[pltpu.VMEM((rank_block, w), bf16) for w in (columns,) * 3]
        + [pltpu.VMEM(x.shape, x.dtype) for x in small]
        + [pltpu.VMEM((loads[1], depth, block), bf16)],
        scratch_shapes=[
            pltpu.SemaphoreType.DMA((3 + len(small),)),
            pltpu.SemaphoreType.DMA((loads[1], bands)),
        ],
    )(expand, weight, *small)
    loaded = [held]
    across, beside = from_owner(across, 2, 3), from_owner(beside, 1, 1)

    rows, keep, send, slot = kernel_call(
        functools.partial(gather_kernel, (0, *offsets)),
        "gather_rows",
        1,
        1,
        4,
        in_specs=[vmem] * (owner_count + 3),
        out_specs=[vmem] * 4,
        out_shape=[jax.ShapeDtypeStruct((row_count, depth), bf16)]
        + [jax.ShapeDtypeStruct((rank // 2, row_count), f32)] * 2
        + [jax.ShapeDtypeStruct((1, row_count), jnp.int32)],
        scratch_shapes=[pltpu.VMEM((row_count, depth), bf16), pltpu.VMEM((rank, row_count), f32)],
    )(
        slots,
        index,
        mine,
        *blocks,
        shrink,
    )

    def base_part(n, *after):
        first, last = parts[n]
        streamed = n + 1 == len(parts)
        numbers = range(loads[n + 1], loads[n + 2])
        places, used = [], []
        for number in range(first, numbers[0] if streamed else last):
            source = max(k for k in range(len(loads) - 1) if loads[k] <= number)
            if source not in used:
                used.append(source)
            places.append((used.index(source), number - loads[source]))
        ahead = pltpu.VMEM((len(numbers), depth, block), bf16)
        out = kernel_call(
            functools.partial(base_kernel, block, places, numbers, streamed),
            "base_part",
            (15 * 10**8, 15 * 10**8, 10**10, 1)[n],
            1,
            12,
            in_specs=[vmem, anywhere] + [vmem] * len(used) + [anywhere] * len(after),
            out_specs=[vmem] * (1 if streamed else 2),
            out_shape=[jax.ShapeDtypeStruct((row_count, (last - first) * block), f32)]
            + ([] if streamed else [ahead]),
            scratch_shapes=([ahead] if streamed else [])
            + [pltpu.SemaphoreType.DMA((len(numbers), bands))],
        )(rows, weight, *[loaded[k] for k in used], *after)
        loaded.append(out[-1])
        return out[0]

    arrived = from_tensor(send, 1)
    base_0 = base_part(0, send)
    arrived, base_0 = lax.optimization_barrier((arrived, base_0))
    pair = keep + arrived
    arrived = from_tensor(pair[rank_block:], 2)
    base_1 = base_part(1, pair)
    arrived, base_1 = lax.optimization_barrier((arrived, base_1))
    shrunk = (adapter_scale * (pair[:rank_block] + arrived)).astype(bf16)
    across, _ = lax.optimization_barrier((across, shrunk))
    swapped = from_group(across)
    bases = [base_0, base_1]
    for m, n in ((2, 2), (1, 3)):
        arrived = from_owner(shrunk, m, m)
        base = base_part(n, shrunk, across)
        arrived, base = lax.optimization_barrier((arrived, base))
        bases.append(base)
        shrunk = shrunk + arrived

    middle = block_count * 5 // 14 * block
    splits = [(0, middle), (middle, columns)]
    quarter = row_count // 4

    def delta_part(begin, end):
        return kernel_call(
            functools.partial(delta_kernel, block, begin, end),
            "add_delta",
            1,
            1,
            8,
            in_specs=[vmem] * (len(bases) + 6),
            out_specs=[vmem] * 4,
            out_shape=[jax.ShapeDtypeStruct((quarter, end - begin), f32)] * 4,
            scratch_shapes=[
                pltpu.VMEM((row_count, rank_block * owner_count), f32),
                pltpu.VMEM((row_count, rank_block * owner_count), bf16),
            ],
        )(slot, *bases, own, shrunk, across, beside, swapped)

    first, second = delta_part(*splits[0]), delta_part(*splits[1])
    arrived = [from_tensor(first[3], 1), from_tensor(second[3], 1)]
    arrived[0], *rest = lax.optimization_barrier((arrived[0], *second[:3]))
    second = [*rest, second[3]]
    summed = [(part[1] + other).astype(bf16) for part, other in zip((first, second), arrived)]
    crossed = [from_tensor(x, 2) for x in summed]
    _, *sent = lax.optimization_barrier((summed[1], first[2], second[2]))
    halves = []
    for part, across_x, own_rows in zip((first, second), crossed, sent):
        kept = part[0] + from_tensor(own_rows, 1)
        halves.append((kept + across_x.astype(f32)).astype(bf16))
    return jnp.concatenate(halves, axis=1)


def on_device(tokens, base_up_weight, adapter_shrink_weight, adapter_expand_weight, *index):
    pairs = lax.axis_size("groups") == 2 and lax.axis_size("tensor") == 4
    few = lax.axis_size("adapter") == 4
    columns = base_up_weight.shape[1]
    even = columns % 512 == 0 and columns >= 4096 and tokens.shape[0] % 16 == 0
    arrange = paired if pairs and few and even else general
    return arrange(
        tokens, base_up_weight, adapter_shrink_weight, adapter_expand_weight, *index
    )


def solution(mesh):
    placed = (
        P(("groups", "adapter"), "tensor"),
        P("tensor", "adapter"),
        P("adapter", "tensor", None),
        P("adapter", "tensor", None),
        P("groups", None),
        P(),
    )
    return jax.shard_map(
        on_device,
        mesh=mesh,
        in_specs=placed,
        out_specs=P(("groups", "tensor"), "adapter"),
        check_vma=False,
    )
```
